32 devices in a mesh: dp: 8 (over z, y), tensor: 4 (over x, core).
Axes of the slice: x: 2, y: 2, z: 4, core: 2. Of those that a mesh axis runs over, the one named last changes fastest.
Arguments:
- tokens: bfloat16 [20480, 768], P(('dp', 'tensor')), may hold values from -6 to 6
- w_query: bfloat16 [768, 768], P(None, 'tensor'), may hold values from -0.3125 to 0.3125
- w_key: bfloat16 [768, 768], P(None, 'tensor'), may hold values from -0.3125 to 0.3125
- w_value: bfloat16 [768, 768], P(None, 'tensor'), may hold values from -0.21875 to 0.21875
- conv_weight: float32 [12, 33], P('tensor'), may hold values from -1.25 to 1.25
- w_out: bfloat16 [768, 768], replicated, may hold values from -0.4375 to 0.4375
- gain_one: float32 [768], replicated, may hold values from 0.5 to 1.5
- shift_one: float32 [768], replicated, may hold values from -3 to 3
- w_up: bfloat16 [768, 3072], P(None, 'tensor'), may hold values from -0.21875 to 0.21875
- w_down: bfloat16 [3072, 768], P('tensor'), may hold values from -0.15625 to 0.15625
- gain_two: float32 [768], replicated, may hold values from 0.5 to 1.5
- shift_two: float32 [768], replicated, may hold values from -3 to 3
- lengths: int32 [8, 3], P('dp'), may hold values from 64 to 2432, as said below
- grad_output: bfloat16 [20480, 768], P(('dp', 'tensor')), may hold values from -6 to 6
Outputs:
- output: float32 [20480, 768], P(('dp', 'tensor'))
- grad_tokens: float32 [20480, 768], P(('dp', 'tensor'))
- grad_w_query: float32 [768, 768], P(None, 'tensor')
- grad_w_key: float32 [768, 768], P(None, 'tensor')
- grad_w_value: float32 [768, 768], P(None, 'tensor')
- grad_conv: float32 [12, 33], P('tensor')
- grad_w_out: float32 [768, 768], replicated
- grad_gain_one: float32 [768], replicated
- grad_shift_one: float32 [768], replicated
- grad_w_up: float32 [768, 3072], P(None, 'tensor')
- grad_w_down: float32 [3072, 768], P('tensor')
- grad_gain_two: float32 [768], replicated
- grad_shift_two: float32 [768], replicated
The draws below stay inside these ranges and needn't reach their ends.
Inputs may be any that keep to these rules, and one draw needn't show every extreme that they name: Row g lists the lengths of the 3 sequences of group g, laid end to end over its 2560 tokens; they sum to 2560.
All inputs are finite; a program needn't handle non-finite values.
Results may differ from the reference program's by a relative error of at most 0.02.
The reference program's roundings to bfloat16 on the way count: a program that leaves them out, or rounds other values in their place, can miss the bound.
Values may be sent and summed in bfloat16 or wider, within the bound.
No kernel may reach another device: no remote copies, remote signals or barrier semaphores. Data moves between devices by JAX's collectives and lax.ppermute only.
A program may use at most 256 MiB of HBM per device.

```python
import jax
import jax.numpy as jnp
from jax import lax

D = 768
HEADS = 12
HEAD = 64
FF = 3072
LANDMARKS = 64
NS_ITERS = 6
KERNEL = 33
SEQS = 3
TOK_DEV = 640
GROUP = 2560
GROUPS = 8
TOKENS = 20480
MARKS = 192


def draw_lengths(key, part):
    short_key = jax.random.fold_in(key, 11)
    place_key = jax.random.fold_in(key, 12)
    brief_sequence_list = jax.random.randint(short_key, (GROUPS, SEQS - 1), LANDMARKS, TOK_DEV // 2, dtype=jnp.int32)
    first_row = (jnp.arange(GROUPS, dtype=jnp.int32) == 0)[:, None]
    brief_sequence_list = jnp.where(first_row, LANDMARKS, brief_sequence_list).astype(jnp.int32)
    longest = (GROUP - jnp.sum(brief_sequence_list, axis=1, keepdims=True)).astype(jnp.int32)
    long_place = jax.random.randint(place_key, (GROUPS, 1), 0, SEQS, dtype=jnp.int32)
    slot_index = jnp.arange(SEQS, dtype=jnp.int32)[None, :]
    short_index = jnp.clip(slot_index - (slot_index > long_place).astype(jnp.int32), 0, SEQS - 2)
    picked = jnp.take_along_axis(brief_sequence_list, short_index, axis=1)
    return jnp.where(slot_index == long_place, longest, picked).astype(jnp.int32)


def block_scale(stream_key, shape, pieces, low, largest):
    loudness = 1.0
    for axis_at, blocks in pieces:
        draws = jax.random.uniform(jax.random.fold_in(jax.random.fold_in(stream_key, 6), axis_at), (blocks,), jnp.float32, low / len(pieces), largest / len(pieces))
        loudness = loudness * jnp.repeat(jnp.exp(draws), shape[axis_at] // blocks).reshape((-1,) + (1,) * (len(shape) - 1 - axis_at))
    return loudness


def noise(own_key, extent, scale, most, split=(), kind=jnp.bfloat16):
    entries = scale * jax.random.normal(own_key, extent, jnp.float32)
    if split:
        entries = entries * block_scale(own_key, extent, split, -0.22, 0.18)
    return jnp.clip(entries, -most, most).astype(kind)


def setup_inputs(seed: int = 0) -> dict:
    keys = jax.random.split(jax.random.key(seed), 15)
    return {
        "tokens": noise(keys[0], (TOKENS, D), 1.0, 6.0, ((0, 32),)),
        "w_query": noise(keys[1], (D, D), (D // 2) ** -0.5, 0.3125, ((1, 4),)),
        "w_key": noise(keys[2], (D, D), (D // 2) ** -0.5, 0.3125, ((1, 4),)),
        "w_value": noise(keys[3], (D, D), D ** -0.5, 0.21875, ((1, 4),)),
        "conv_weight": noise(keys[4], (HEADS, KERNEL), 0.08, 1.25, ((0, 4),), jnp.float32),
        "w_out": noise(keys[5], (D, D), (D // 4) ** -0.5, 0.4375),
        "gain_one": jnp.clip(1.0 + 0.1 * jax.random.normal(keys[6], (D,), jnp.float32), 0.5, 1.5),
        "shift_one": noise(keys[7], (D,), 0.5, 3.0, (), jnp.float32),
        "w_up": noise(keys[8], (D, FF), D ** -0.5, 0.21875, ((1, 4),)),
        "w_down": noise(keys[9], (FF, D), (FF // 2) ** -0.5, 0.15625, ((0, 4),)),
        "gain_two": jnp.clip(1.0 + 0.1 * jax.random.normal(keys[10], (D,), jnp.float32), 0.5, 1.5),
        "shift_two": noise(keys[11], (D,), 0.5, 3.0, (), jnp.float32),
        "lengths": draw_lengths(jax.random.fold_in(keys[14], 71), 0),
        "grad_output": noise(keys[13], (TOKENS, D), 1.0, 6.0, ((0, 32),)),
    }


@jax.custom_vjp
def lowrank_output(v):
    return lax.optimization_barrier(v.astype(jnp.bfloat16)).astype(jnp.float32)

@jax.custom_vjp
def lowrank_backward(v):
    return v

def low_keep(v):
    return (lowrank_output(v), None)

def low_pass(kept, grad):
    return (grad,)

def back_keep(v):
    return (v, None)

def back_low(kept, grad):
    return (lowrank_output(grad),)
lowrank_output.defvjp(low_keep, low_pass)
lowrank_backward.defvjp(back_keep, back_low)
TOP_PRECISION = lax.Precision.HIGHEST

def matmul(left_side, right_side):
    return jnp.dot(left_side, right_side, precision=TOP_PRECISION)

def layer_norm(values, norm_gain, norm_shift):
    row_mean = lax.optimization_barrier(jnp.mean(values, axis=-1, keepdims=True))
    centered = values - row_mean
    spread = lax.optimization_barrier(jnp.mean(centered * centered, axis=-1, keepdims=True))
    return centered * lax.rsqrt(spread + 1e-05) * norm_gain + norm_shift

def group_layout(length_row, group_size):
    seq_ends = jnp.cumsum(length_row).astype(jnp.int32)
    seq_starts = (seq_ends - length_row).astype(jnp.int32)
    places = jnp.arange(group_size, dtype=jnp.int32)
    sequence = lax.optimization_barrier(jnp.sum((places[:, None] >= seq_ends[None, :]).astype(jnp.int32), axis=1)).astype(jnp.int32)
    member = (sequence[:, None] == jnp.arange(SEQS, dtype=jnp.int32)[None, :]).astype(jnp.int32)
    own_start = lax.optimization_barrier(jnp.sum(member * seq_starts[None, :], axis=1)).astype(jnp.int32)
    own_length = lax.optimization_barrier(jnp.sum(member * length_row[None, :], axis=1)).astype(jnp.int32)
    within = places - own_start
    segment = ((within + 1) * LANDMARKS + own_length - 1) // own_length - 1
    return (sequence, (sequence * LANDMARKS + segment).astype(jnp.int32))

def softmax_with_mask(scores, allowed):
    masked = jnp.where(allowed, scores, -1e+30)
    row_top = lax.optimization_barrier(jnp.max(masked, axis=-1, keepdims=True))
    raised = jnp.where(allowed, jnp.exp(masked - row_top), 0.0)
    return raised / lax.optimization_barrier(jnp.sum(raised, axis=-1, keepdims=True))

def iterative_pseudoinverse(kernel):
    identity = jnp.eye(kernel.shape[-1], dtype=kernel.dtype)
    column_top = lax.optimization_barrier(jnp.max(lax.optimization_barrier(jnp.sum(kernel, axis=1)), axis=-1))[:, None, None]
    approx = jnp.swapaxes(kernel, 1, 2) / column_top
    for sweep_step in range(NS_ITERS):
        product = jnp.einsum('hij,hjk->hik', kernel, approx, precision=TOP_PRECISION)
        bracket = 7.0 * identity - product
        bracket = 15.0 * identity - jnp.einsum('hij,hjk->hik', product, bracket, precision=TOP_PRECISION)
        bracket = 13.0 * identity - jnp.einsum('hij,hjk->hik', product, bracket, precision=TOP_PRECISION)
        approx = 0.25 * jnp.einsum('hij,hjk->hik', approx, bracket, precision=TOP_PRECISION)
    return approx

def convolve(values, conv_weight, sequence):
    reach = KERNEL // 2
    size_rows = values.shape[0]
    padded = jnp.pad(values, ((reach, reach), (0, 0), (0, 0)))
    seq_padded = jnp.pad(sequence, (reach, reach), constant_values=-1)
    summed = jnp.zeros_like(values)
    for offset in range(KERNEL):
        same_seq = (seq_padded[offset:offset + size_rows] == sequence)[:, None, None]
        shifted = jnp.where(same_seq, padded[offset:offset + size_rows], 0.0)
        summed = summed + shifted * conv_weight[:, offset][None, :, None]
    return summed

def attend(query_grouped, key_grouped, value_grouped, length_row, conv_weight):
    group_size = query_grouped.shape[0]
    sequence, landmark = group_layout(length_row, group_size)
    marks = jnp.arange(MARKS, dtype=jnp.int32)
    mark_seq = marks // LANDMARKS
    landmark_pooling = (landmark[None, :] == marks[:, None]).astype(jnp.float32)
    token_counts = lax.optimization_barrier(jnp.sum(landmark_pooling, axis=1))[:, None, None]
    query_landmarks = lowrank_output(lowrank_backward(jnp.einsum('br,rwi->bwi', landmark_pooling, query_grouped, precision=TOP_PRECISION) / token_counts))
    key_landmarks = lowrank_output(lowrank_backward(jnp.einsum('br,rwi->bwi', landmark_pooling, key_grouped, precision=TOP_PRECISION) / token_counts))
    local_neighbour_response = sequence[:, None] == mark_seq[None, :]
    block_layer = mark_seq[:, None] == mark_seq[None, :]
    target_landmark_scores = lowrank_output(softmax_with_mask(lowrank_backward(jnp.einsum('tfu,kfu->ftk', query_grouped, key_landmarks, precision=TOP_PRECISION)), local_neighbour_response[None]))
    landmark_mixing = softmax_with_mask(jnp.einsum('jos,eos->oje', query_landmarks, key_landmarks, precision=TOP_PRECISION), block_layer[None])
    source_landmark_scores = lowrank_output(softmax_with_mask(lowrank_backward(jnp.einsum('oeu,peu->eop', query_landmarks, key_grouped, precision=TOP_PRECISION)), local_neighbour_response.T[None]))
    landmark_digest = lowrank_backward(jnp.einsum('uca,aue->uce', source_landmark_scores, value_grouped, precision=TOP_PRECISION))
    anchor_values_pooled = lowrank_output(jnp.einsum('kej,kjq->keq', iterative_pseudoinverse(landmark_mixing), landmark_digest, precision=TOP_PRECISION))
    blended_output = jnp.einsum('lvk,lko->vlo', target_landmark_scores, anchor_values_pooled, precision=TOP_PRECISION)
    return blended_output + convolve(value_grouped, conv_weight, sequence)

def forward(tokens, w_query, w_key, w_value, conv_weight, w_out, gain_one, shift_one, w_up, w_down, gain_two, shift_two, lengths):
    qk_scale = HEAD ** (-0.25)
    query_all = lowrank_output(lowrank_backward(matmul(tokens, w_query) * qk_scale)).reshape(GROUPS, GROUP, HEADS, HEAD)
    key_all = lowrank_output(lowrank_backward(matmul(tokens, w_key) * qk_scale)).reshape(GROUPS, GROUP, HEADS, HEAD)
    value_all = lowrank_output(lowrank_backward(matmul(tokens, w_value))).reshape(GROUPS, GROUP, HEADS, HEAD)

    def one_group(operands):
        query_grouped, key_grouped, value_grouped, length_row = operands
        return attend(query_grouped, key_grouped, value_grouped, length_row, conv_weight)
    context = lax.map(jax.checkpoint(one_group), (query_all, key_all, value_all, lengths))
    context = lowrank_output(lowrank_backward(context.reshape(TOKENS, D)))
    attended = lowrank_backward(matmul(context, w_out))
    normed = layer_norm(tokens + attended, gain_one, shift_one)
    preactivation_feedforward = lowrank_backward(matmul(lowrank_output(normed), w_up))
    hidden = lowrank_output(jax.nn.gelu(preactivation_feedforward, approximate=False))
    branch = lowrank_backward(matmul(hidden, w_down))
    return layer_norm(normed + branch, gain_two, shift_two)

def reference(tokens, w_query, w_key, w_value, conv_weight, w_out, gain_one, shift_one, w_up, w_down, gain_two, shift_two, lengths, grad_output):
    floats = tuple((entry.astype(jnp.float32) for entry in (tokens, w_query, w_key, w_value, conv_weight, w_out, gain_one, shift_one, w_up, w_down, gain_two, shift_two)))

    def bound(*params):
        return forward(*params, lengths)
    final_answer, pull_back = jax.vjp(bound, *floats)
    grads = pull_back(grad_output.astype(jnp.float32))
    return (final_answer, grads[0], grads[1], grads[2], grads[3], grads[4], grads[5], grads[6], grads[7], grads[8], grads[9], grads[10], grads[11])
```

```python
import jax
import jax.numpy as jnp
from jax import lax
from jax.experimental import pallas as pl
from jax.experimental.pallas import tpu as pltpu
from jax.sharding import PartitionSpec as P

HEAD = 64
LANDMARKS = 64
NS_ITERS = 6
KERNEL = 33
SEQS = 3
MARKS = 192
REACH = KERNEL // 2
PAD = 128
BAND_IN = 512
BAND_OUT = 256
TILE = 512
VMEM_LIMIT = 60 * 1024 * 1024
F32 = jnp.float32
BF16 = jnp.bfloat16


def dot_nn(a, b):
    return lax.dot_general(a, b, (((1,), (0,)), ((), ())), preferred_element_type=F32)


def dot_nt(a, b):
    return lax.dot_general(a, b, (((1,), (1,)), ((), ())), preferred_element_type=F32)


def dot_tn(a, b):
    return lax.dot_general(a, b, (((0,), (0,)), ((), ())), preferred_element_type=F32)


def split_low(a):
    high = a.astype(BF16)
    return (high, (a - high.astype(F32)).astype(BF16))


def dot_three(a, b, dot=dot_nn):
    a_high, a_low = a
    b_high, b_low = b
    return dot(a_high, b_high) + (dot(a_high, b_low) + dot(a_low, b_high))


def block_mask(dtype):
    rows = lax.broadcasted_iota(jnp.int32, (MARKS, MARKS), 0) // LANDMARKS
    columns = lax.broadcasted_iota(jnp.int32, (MARKS, MARKS), 1) // LANDMARKS
    return jnp.where(rows == columns, 1.0, 0.0).astype(dtype)


def spread(packed, mask):
    return jnp.concatenate([packed] * SEQS, axis=0) * mask


def spread_split(packed, mask):
    high, low = split_low(packed)
    return (spread(high, mask), spread(low, mask))


def fold(blocks):
    return (
        blocks[:LANDMARKS] + blocks[LANDMARKS : 2 * LANDMARKS] + blocks[2 * LANDMARKS :]
    )


def packed_identity():
    rows = lax.broadcasted_iota(jnp.int32, (LANDMARKS, MARKS), 0)
    columns = lax.broadcasted_iota(jnp.int32, (LANDMARKS, MARKS), 1) % LANDMARKS
    return jnp.where(rows == columns, 1.0, 0.0).astype(F32)


def sequence_of(places, first_end, second_end):
    return (places >= first_end).astype(jnp.int32) + (places >= second_end).astype(jnp.int32)


def pooling_tile(start, width, ends):
    first_end, second_end, group_size = ends
    places = start + lax.broadcasted_iota(jnp.int32, (1, width), 1)
    sequence = sequence_of(places, first_end, second_end)
    own_start = jnp.where(sequence == 0, 0, jnp.where(sequence == 1, first_end, second_end))
    own_end = jnp.where(
        sequence == 0, first_end, jnp.where(sequence == 1, second_end, group_size)
    )
    own_length = (own_end - own_start).astype(F32)
    within = places - own_start
    numerator = ((within + 1) * LANDMARKS - 1).astype(F32) + own_length + 0.5
    segment = jnp.floor(numerator / own_length).astype(jnp.int32) - 1
    landmark = sequence * LANDMARKS + segment
    marks = lax.broadcasted_iota(jnp.int32, (MARKS, width), 0)
    return jnp.where(marks == landmark, 1.0, 0.0).astype(BF16)


def own_tokens_tile(start, width, ends):
    places = start + lax.broadcasted_iota(jnp.int32, (1, width), 1)
    sequence = sequence_of(places, ends[0], ends[1])
    marks = lax.broadcasted_iota(jnp.int32, (MARKS, width), 0) // LANDMARKS
    return marks == sequence


def landmark_counts(ends, axis):
    first_end, second_end, group_size = ends
    shape = (1, MARKS) if axis == 1 else (MARKS, 1)
    marks = lax.broadcasted_iota(jnp.int32, shape, axis)
    sequence = marks // LANDMARKS
    k = marks % LANDMARKS
    own_length = jnp.where(
        sequence == 0,
        first_end,
        jnp.where(sequence == 1, second_end - first_end, group_size - second_end),
    )
    upper = lax.shift_right_logical((k + 1) * own_length, 6)
    return (upper - lax.shift_right_logical(k * own_length, 6)).astype(F32)


def band_mask(start, ends):
    into = start - PAD + lax.broadcasted_iota(jnp.int32, (BAND_IN, 1), 0)
    out = start + lax.broadcasted_iota(jnp.int32, (1, BAND_OUT), 1)
    return sequence_of(into, ends[0], ends[1]) == sequence_of(out, ends[0], ends[1])


def ends_of(scalars, group_size):
    first_end = scalars[0]
    return (first_end, first_end + scalars[1], group_size)


def lane_slice(start, width):
    return pl.ds(pl.multiple_of(start, 128), width)


def attend_kernel(
    heads,
    scalars,
    x0,
    x1,
    x2,
    x3,
    w_t,
    bands,
    qkv_t,
    c0,
    c1,
    c2,
    c3,
    land_t,
    mark_values_out,
    summary_out,
    steps_out,
    among_out,
    inverse_out,
    lse_to,
    lse_from,
    context_t,
    scores,
    pooled,
    mvt_scratch,
):
    width = heads * HEAD
    block = x0.shape[0]
    group_size = 4 * block
    ends = ends_of(scalars, group_size)
    me = scalars[3]
    qk_scale = HEAD ** (-0.25)
    tiles = group_size // TILE

    qkv_t[:, :PAD] = jnp.zeros((3 * width, PAD), BF16)
    qkv_t[:, PAD + group_size :] = jnp.zeros((3 * width, PAD), BF16)
    for at, x in enumerate((x0, x1, x2, x3)):
        offset = PAD + (me ^ at) * block

        @pl.loop(0, 3)
        def _(part):
            rows = pl.ds(pl.multiple_of(part * width, width), width)
            product = dot_nt(w_t[rows, :], x[...])
            scale = jnp.where(part < 2, qk_scale, 1.0).astype(F32)
            qkv_t[rows, lane_slice(offset, block)] = (product * scale).astype(BF16)

    pooled[...] = jnp.zeros_like(pooled)

    @pl.loop(0, tiles)
    def _(i):
        pool = pooling_tile(i * TILE, TILE, ends)
        pooled[...] += dot_nt(qkv_t[: 2 * width, lane_slice(PAD + i * TILE, TILE)], pool)

    pooled[...] = pooled[...] / landmark_counts(ends, 1)
    land_t[...] = pooled[...].astype(BF16)

    mask_f = block_mask(F32)
    mask_b = block_mask(BF16)
    eye = packed_identity()
    summaries = []
    amongs = []
    packs = []
    approxes = []
    key_lands = []
    for h in range(heads):
        head_rows = slice(h * HEAD, (h + 1) * HEAD)
        key_rows = slice(width + h * HEAD, width + (h + 1) * HEAD)
        value_rows = slice(2 * width + h * HEAD, 2 * width + (h + 1) * HEAD)
        q_land = land_t[head_rows, :].astype(F32).T.astype(BF16)
        k_land = land_t[key_rows, :].astype(F32).T.astype(BF16)
        key_lands.append(k_land)

        def score_pass(i, top):
            raw = dot_nn(q_land, qkv_t[key_rows, lane_slice(PAD + i * TILE, TILE)])
            masked = jnp.where(own_tokens_tile(i * TILE, TILE, ends), raw, -1e30)
            scores[:, lane_slice(i * TILE, TILE)] = masked
            return jnp.maximum(top, jnp.max(masked, axis=1, keepdims=True))

        top = lax.fori_loop(0, tiles, score_pass, jnp.full((MARKS, 1), -1e30, F32))

        def raise_pass(i, total):
            at = lane_slice(i * TILE, TILE)
            raised = jnp.exp(scores[:, at] - top)
            scores[:, at] = raised
            return total + jnp.sum(raised, axis=1, keepdims=True)

        total = lax.fori_loop(0, tiles, raise_pass, jnp.zeros((MARKS, 1), F32))
        recip = 1.0 / total
        lse_from[h] = jnp.broadcast_to(top + jnp.log(total), (MARKS, 128))

        def summary_pass(i, summed):
            low = (scores[:, lane_slice(i * TILE, TILE)] * recip).astype(BF16)
            return summed + dot_nt(low, qkv_t[value_rows, lane_slice(PAD + i * TILE, TILE)])

        summary = lax.fori_loop(0, tiles, summary_pass, jnp.zeros((MARKS, HEAD), F32))
        summary_out[h] = summary
        summaries.append(summary)

        raw = dot_nn(q_land, land_t[key_rows, :])
        masked = jnp.where(mask_f > 0.0, raw, -1e30)
        row_top = jnp.max(masked, axis=1, keepdims=True)
        raised = jnp.exp(masked - row_top)
        among = raised / jnp.sum(raised, axis=1, keepdims=True)
        column_top = jnp.max(jnp.sum(among, axis=0, keepdims=True), axis=1, keepdims=True)
        packed = fold(among)
        among_out[h] = packed
        amongs.append(split_low(packed))
        approxes.append(fold(among.T) / column_top)

    for step in range(NS_ITERS):
        product = [
            dot_three(amongs[h], spread_split(approxes[h], mask_b)) for h in range(heads)
        ]
        split = [split_low(product[h]) for h in range(heads)]
        bracket = [7.0 * eye - product[h] for h in range(heads)]
        second = [
            15.0 * eye - dot_three(split[h], spread_split(bracket[h], mask_b))
            for h in range(heads)
        ]
        third = [
            13.0 * eye - dot_three(split[h], spread_split(second[h], mask_b))
            for h in range(heads)
        ]
        for h in range(heads):
            steps_out[h, 4 * step] = approxes[h]
            steps_out[h, 4 * step + 1] = product[h]
            steps_out[h, 4 * step + 2] = second[h]
            steps_out[h, 4 * step + 3] = third[h]
        approxes = [
            0.25 * dot_three(split_low(approxes[h]), spread_split(third[h], mask_b))
            for h in range(heads)
        ]

    for h in range(heads):
        inverse_out[h] = approxes[h]
        mark_values = dot_three(
            spread_split(approxes[h], mask_b), split_low(summaries[h])
        )
        mark_values_out[h] = mark_values.astype(BF16)
        mvt_scratch[h] = mark_values.astype(BF16).astype(F32).T.astype(BF16)

    @pl.loop(0, group_size // BAND_OUT)
    def _(i):
        start = i * BAND_OUT
        near = own_tokens_tile(start, BAND_OUT, ends)
        same = jnp.where(band_mask(start, ends), 1.0, 0.0).astype(BF16)
        for h in range(heads):
            head_rows = slice(h * HEAD, (h + 1) * HEAD)
            value_rows = slice(2 * width + h * HEAD, 2 * width + (h + 1) * HEAD)
            raw = dot_nn(key_lands[h], qkv_t[head_rows, lane_slice(PAD + start, BAND_OUT)])
            masked = jnp.where(near, raw, -1e30)
            top = jnp.max(masked, axis=0, keepdims=True)
            raised = jnp.exp(masked - top)
            total = jnp.sum(raised, axis=0, keepdims=True)
            lse_to[h : h + 1, lane_slice(start, BAND_OUT)] = top + jnp.log(total)
            low = (raised * (1.0 / total)).astype(BF16)
            window = qkv_t[value_rows, lane_slice(start, BAND_IN)]
            blended = dot_nn(mvt_scratch[h], low)
            smooth = dot_nn(window, bands[h, 0] * same) + dot_nn(window, bands[h, 1] * same)
            context_t[head_rows, lane_slice(start, BAND_OUT)] = (blended + smooth).astype(BF16)

    for at, out in enumerate((c0, c1, c2, c3)):
        out[...] = context_t[:, lane_slice((me ^ at) * block, block)]


def attend(scalars, blocks, w_t, bands):
    block = blocks[0].shape[0]
    group_size = 4 * block
    width = w_t.shape[0] // 3
    heads = width // HEAD
    out_shape = (
        jax.ShapeDtypeStruct((3 * width, group_size + 2 * PAD), BF16),
        *[jax.ShapeDtypeStruct((width, block), BF16) for _ in range(4)],
        jax.ShapeDtypeStruct((2 * width, MARKS), BF16),
        jax.ShapeDtypeStruct((heads, MARKS, HEAD), BF16),
        jax.ShapeDtypeStruct((heads, MARKS, HEAD), F32),
        jax.ShapeDtypeStruct((heads, 4 * NS_ITERS, LANDMARKS, MARKS), F32),
        jax.ShapeDtypeStruct((heads, LANDMARKS, MARKS), F32),
        jax.ShapeDtypeStruct((heads, LANDMARKS, MARKS), F32),
        jax.ShapeDtypeStruct((heads, group_size), F32),
        jax.ShapeDtypeStruct((heads, MARKS, 128), F32),
    )
    vmem = pl.BlockSpec(memory_space=pltpu.VMEM)

    def kernel(*refs):
        attend_kernel(heads, *refs)

    return pl.pallas_call(
        kernel,
        name="attend",
        out_shape=out_shape,
        in_specs=[pl.BlockSpec(memory_space=pltpu.SMEM)] + [vmem] * 6,
        out_specs=[vmem] * len(out_shape),
        scratch_shapes=[
            pltpu.VMEM((width, group_size), BF16),
            pltpu.VMEM((MARKS, group_size), F32),
            pltpu.VMEM((2 * width, MARKS), F32),
            pltpu.VMEM((heads, HEAD, MARKS), BF16),
        ],
        compiler_params=pltpu.CompilerParams(vmem_limit_bytes=VMEM_LIMIT),
        cost_estimate=pl.CostEstimate(
            flops=15_000_000_000, bytes_accessed=20_000_000, transcendentals=4_000_000
        ),
    )(scalars, *blocks, w_t, bands)


def attend_back_kernel(
    heads,
    scalars,
    qkv_t,
    land_t,
    mark_values_in,
    summary_in,
    steps_in,
    among_in,
    inverse_in,
    lse_to,
    lse_from,
    bands,
    g0,
    g1,
    g2,
    g3,
    x0,
    x1,
    x2,
    x3,
    w_t,
    grad_w_t,
    grad_conv,
    d0,
    d1,
    d2,
    d3,
    context_grad,
    grad_qkv,
    partial_query,
    partial_key,
    partial_value,
    grad_q_land,
    grad_k_land,
    grad_mark,
    correlation,
):
    width = heads * HEAD
    block = x0.shape[0]
    group_size = 4 * block
    ends = ends_of(scalars, group_size)
    me = scalars[3]
    qk_scale = HEAD ** (-0.25)
    tiles = group_size // TILE

    context_grad[:, :PAD] = jnp.zeros((width, PAD), BF16)
    context_grad[:, PAD + group_size :] = jnp.zeros((width, PAD), BF16)
    for at, g in enumerate((g0, g1, g2, g3)):
        context_grad[:, lane_slice(PAD + (me ^ at) * block, block)] = g[...]

    mask_f = block_mask(F32)
    mask_b = block_mask(BF16)
    lands = []
    for h in range(heads):
        q_land_t = land_t[h * HEAD : (h + 1) * HEAD, :]
        k_land_t = land_t[width + h * HEAD : width + (h + 1) * HEAD, :]
        lands.append(
            (
                q_land_t,
                k_land_t,
                q_land_t.astype(F32).T.astype(BF16),
                k_land_t.astype(F32).T.astype(BF16),
            )
        )

    grad_k_land[...] = jnp.zeros_like(grad_k_land)
    grad_mark[...] = jnp.zeros_like(grad_mark)
    grad_q_land[...] = jnp.zeros_like(grad_q_land)

    @pl.loop(0, tiles)
    def _(i):
        at = lane_slice(i * TILE, TILE)
        padded = lane_slice(PAD + i * TILE, TILE)
        near = own_tokens_tile(i * TILE, TILE, ends)
        for h in range(heads):
            head_rows = slice(h * HEAD, (h + 1) * HEAD)
            q_land_t, k_land_t, q_land, k_land = lands[h]
            query = qkv_t[head_rows, padded]
            out_grad = context_grad[head_rows, padded]
            raw = dot_nn(k_land, query)
            probs = jnp.exp(jnp.where(near, raw, -1e30) - lse_to[h : h + 1, at])
            grad_to = dot_nn(mark_values_in[h], out_grad)
            inner = jnp.sum(grad_to * probs, axis=0, keepdims=True)
            grad_scores = (probs * (grad_to - inner)).astype(BF16)
            grad_mark[h] += dot_nt(probs.astype(BF16), out_grad)
            grad_k_land[h] += dot_nt(grad_scores, query)
            partial_query[head_rows, at] = dot_nn(k_land_t, grad_scores)

    grad_summaries = []
    offsets = []
    carried = []
    among_grads = []
    for h in range(heads):
        mark = grad_mark[h]
        mark_split = split_low(mark)
        summary = summary_in[h]
        carried.append(fold(dot_three(split_low(summary), mark_split, dot_nt) * mask_f))
        inverse_blocks = spread(inverse_in[h], mask_f).T
        grad_summary = dot_three(split_low(inverse_blocks), mark_split)
        grad_low = grad_summary.astype(BF16)
        grad_summaries.append((grad_low, grad_low.astype(F32).T.astype(BF16)))
        offsets.append(jnp.sum(grad_low.astype(F32) * summary, axis=1, keepdims=True))

    @pl.loop(0, tiles)
    def _(i):
        at = lane_slice(i * TILE, TILE)
        padded = lane_slice(PAD + i * TILE, TILE)
        near = own_tokens_tile(i * TILE, TILE, ends)
        for h in range(heads):
            head_rows = slice(h * HEAD, (h + 1) * HEAD)
            key_rows = slice(width + h * HEAD, width + (h + 1) * HEAD)
            value_rows = slice(2 * width + h * HEAD, 2 * width + (h + 1) * HEAD)
            q_land_t, k_land_t, q_land, k_land = lands[h]
            key = qkv_t[key_rows, padded]
            value = qkv_t[value_rows, padded]
            raw = dot_nn(q_land, key)
            lse = jnp.concatenate([lse_from[h]] * (TILE // 128), axis=1)
            probs = jnp.exp(jnp.where(near, raw, -1e30) - lse)
            grad_low, grad_low_t = grad_summaries[h]
            grad_from = dot_nn(grad_low, value)
            grad_scores = (probs * (grad_from - offsets[h])).astype(BF16)
            partial_value[head_rows, at] = dot_nn(grad_low_t, probs.astype(BF16))
            grad_q_land[h] += dot_nt(grad_scores, key)
            partial_key[head_rows, at] = dot_nn(q_land_t, grad_scores)

    eye = packed_identity()
    among_split = [split_low(among_in[h]) for h in range(heads)]
    for step in reversed(range(NS_ITERS)):
        for h in range(heads):
            approx = steps_in[h, 4 * step]
            product = steps_in[h, 4 * step + 1]
            second = steps_in[h, 4 * step + 2]
            third = steps_in[h, 4 * step + 3]
            first = 7.0 * eye - product
            approx_split = split_low(approx)
            approx_wide = tuple(spread(a, mask_b) for a in approx_split)
            product_wide = spread_split(product, mask_b)
            grad = carried[h]
            grad_third = 0.25 * dot_three(split_low(grad), approx_wide)
            third_split = split_low(grad_third)
            grad_second = -dot_three(third_split, product_wide)
            second_split = split_low(grad_second)
            grad_first = -dot_three(second_split, product_wide)
            grad_product = -(
                grad_first
                + dot_three(
                    split_low(second), tuple(spread(a, mask_b) for a in third_split)
                )
                + dot_three(
                    split_low(first), tuple(spread(a, mask_b) for a in second_split)
                )
            )
            product_split = split_low(grad_product)
            among_part = dot_three(
                approx_split, tuple(spread(a, mask_b) for a in product_split)
            )
            if step == NS_ITERS - 1:
                among_grads.append(among_part)
            else:
                among_grads[h] = among_grads[h] + among_part
            carried[h] = 0.25 * dot_three(
                split_low(third), spread_split(grad, mask_b)
            ) + dot_three(
                product_split, tuple(spread(a, mask_b) for a in among_split[h])
            )

    land_grads = []
    for h in range(heads):
        q_land_t, k_land_t, q_land, k_land = lands[h]
        among = spread(among_in[h], mask_f)
        column_sums = jnp.sum(among, axis=0, keepdims=True)
        column_top = jnp.max(column_sums, axis=1, keepdims=True)
        start = steps_in[h, 0]
        start_grad = carried[h]
        start_blocks = spread(start, mask_f).T
        top_grad = -jnp.sum(
            jnp.sum(start_grad * fold(start_blocks), axis=1, keepdims=True),
            axis=0,
            keepdims=True,
        ) / column_top
        at_top = jnp.where(column_sums == column_top, 1.0, 0.0)
        shared = top_grad * at_top / jnp.sum(at_top, axis=1, keepdims=True)
        among_grad = spread(among_grads[h], mask_f).T + (
            spread(start_grad, mask_f) / column_top + shared * mask_f
        )
        inner = jnp.sum(among_grad * among, axis=1, keepdims=True)
        grad_scores = among * (among_grad - inner)
        high, low = split_low(grad_scores)
        back_high, back_low = split_low(grad_scores.T)
        q_total = grad_q_land[h] + (dot_nn(high, k_land) + dot_nn(low, k_land))
        k_total = grad_k_land[h] + (dot_nn(back_high, q_land) + dot_nn(back_low, q_land))
        counts = landmark_counts(ends, 0)
        q_share = q_total.astype(BF16).astype(F32) / counts
        k_share = k_total.astype(BF16).astype(F32) / counts
        land_grads.append((split_low(q_share.T), split_low(k_share.T)))

    correlation[...] = jnp.zeros_like(correlation)

    @pl.loop(0, group_size // BAND_OUT)
    def _(i):
        start = i * BAND_OUT
        at = lane_slice(start, BAND_OUT)
        padded = lane_slice(PAD + start, BAND_OUT)
        around = lane_slice(start, BAND_IN)
        pool = pooling_tile(start, BAND_OUT, ends)
        same = band_mask(start, ends)
        same_f = jnp.where(same, 1.0, 0.0)
        same_b = same_f.astype(BF16)
        for h in range(heads):
            head_rows = slice(h * HEAD, (h + 1) * HEAD)
            key_rows = slice(width + h * HEAD, width + (h + 1) * HEAD)
            value_rows = slice(2 * width + h * HEAD, 2 * width + (h + 1) * HEAD)
            (q_high, q_low), (k_high, k_low) = land_grads[h]
            query = partial_query[head_rows, at] + (dot_nn(q_high, pool) + dot_nn(q_low, pool))
            key = partial_key[head_rows, at] + (dot_nn(k_high, pool) + dot_nn(k_low, pool))
            window = context_grad[head_rows, around]
            value = partial_value[head_rows, at] + (
                dot_nn(window, bands[h, 0] * same_b) + dot_nn(window, bands[h, 1] * same_b)
            )
            grad_qkv[head_rows, at] = query.astype(BF16)
            grad_qkv[key_rows, at] = key.astype(BF16)
            grad_qkv[value_rows, at] = value.astype(BF16)
            across = dot_tn(qkv_t[value_rows, around], context_grad[head_rows, padded])
            across = across * same_f
            correlation[h, 0] += across[:128, :128] + across[128:256, 128:]
            correlation[h, 1] += across[128:256, :128] + across[256:384, 128:]
            correlation[h, 2] += across[256:384, :128] + across[384:, 128:]

    apart = lax.broadcasted_iota(jnp.int32, (128, 128), 0) - lax.broadcasted_iota(
        jnp.int32, (128, 128), 1
    )
    lanes = lax.broadcasted_iota(jnp.int32, (8, 128), 1)
    rows = lax.broadcasted_iota(jnp.int32, (8, 128), 0)
    taps = jnp.zeros((8, 128), F32)
    for h in range(heads):
        for tap in range(KERNEL):
            away = tap - REACH
            picked = jnp.where(apart == away, correlation[h, 1], 0.0)
            if away < 0:
                picked += jnp.where(apart == away + 128, correlation[h, 0], 0.0)
            if away > 0:
                picked += jnp.where(apart == away - 128, correlation[h, 2], 0.0)
            total = jnp.sum(
                jnp.sum(picked, axis=0, keepdims=True), axis=1, keepdims=True
            )
            taps = taps + jnp.where((lanes == tap) & (rows == h), total, 0.0)
    grad_conv[...] = taps

    grad_w_t[...] = jnp.zeros_like(grad_w_t)
    for at, (x, d) in enumerate(((x0, d0), (x1, d1), (x2, d2), (x3, d3))):
        offset = (me ^ at) * block

        @pl.loop(0, 3)
        def _(part):
            rows = pl.ds(pl.multiple_of(part * width, width), width)
            grad_w_t[rows, :] += dot_nn(grad_qkv[rows, lane_slice(offset, block)], x[...])

        @pl.loop(0, block // 128)
        def _(piece):
            lanes = lane_slice(offset + piece * 128, 128)
            scaled = dot_tn(grad_qkv[: 2 * width, lanes], w_t[: 2 * width, :])
            plain = dot_tn(grad_qkv[2 * width :, lanes], w_t[2 * width :, :])
            d[pl.ds(pl.multiple_of(piece * 128, 128), 128), :] = (
                scaled * qk_scale + plain
            ).astype(BF16)

    grad_w_t[: 2 * width, :] = grad_w_t[: 2 * width, :] * qk_scale


def attend_back(scalars, saved, bands, grads, blocks, w_t):
    block, features = blocks[0].shape
    group_size = 4 * block
    width = w_t.shape[0] // 3
    heads = width // HEAD
    out_shape = (
        jax.ShapeDtypeStruct((3 * width, features), F32),
        jax.ShapeDtypeStruct((8, 128), F32),
        *[jax.ShapeDtypeStruct((block, features), BF16) for _ in range(4)],
    )
    vmem = pl.BlockSpec(memory_space=pltpu.VMEM)

    def kernel(*refs):
        attend_back_kernel(heads, *refs)

    operands = (scalars, *saved, bands, *grads, *blocks, w_t)
    return pl.pallas_call(
        kernel,
        name="attend_back",
        out_shape=out_shape,
        in_specs=[pl.BlockSpec(memory_space=pltpu.SMEM)] + [vmem] * (len(operands) - 1),
        out_specs=[vmem] * len(out_shape),
        scratch_shapes=[
            pltpu.VMEM((width, group_size + 2 * PAD), BF16),
            pltpu.VMEM((3 * width, group_size), BF16),
            pltpu.VMEM((width, group_size), F32),
            pltpu.VMEM((width, group_size), F32),
            pltpu.VMEM((width, group_size), F32),
            pltpu.VMEM((heads, MARKS, HEAD), F32),
            pltpu.VMEM((heads, MARKS, HEAD), F32),
            pltpu.VMEM((heads, MARKS, HEAD), F32),
            pltpu.VMEM((heads, 3, 128, 128), F32),
        ],
        compiler_params=pltpu.CompilerParams(vmem_limit_bytes=VMEM_LIMIT),
        cost_estimate=pl.CostEstimate(
            flops=30_000_000_000, bytes_accessed=40_000_000, transcendentals=4_000_000
        ),
    )(*operands)


def gelu_and_slope(values):
    z = jnp.abs(values) * 0.7071067811865476
    t = pl.reciprocal(1.0 + 0.5 * z)
    poly = t * 0.17087277 - 0.82215223
    for coefficient in (
        1.48851587,
        -1.13520398,
        0.27886807,
        -0.18628806,
        0.09678418,
        0.37409196,
        1.00002368,
        -1.26551223,
    ):
        poly = poly * t + coefficient
    bell = jnp.exp(-z * z)
    half_tail = (0.5 * t) * jnp.exp(poly) * bell
    below = jnp.where(values >= 0.0, 1.0 - half_tail, half_tail)
    return values * below, below + values * (bell * 0.3989422804014327)


def unit_norm(values):
    row_mean = jnp.mean(values, axis=-1, keepdims=True)
    centered = values - row_mean
    spread_out = jnp.mean(centered * centered, axis=-1, keepdims=True)
    recip = lax.rsqrt(spread_out + 1e-05)
    return (centered * recip, recip)


def unit_back(grad, unit, recip):
    mean_grad = jnp.mean(grad, axis=-1, keepdims=True)
    mean_cross = jnp.mean(grad * unit, axis=-1, keepdims=True)
    return recip * (grad - mean_grad - unit * mean_cross)


ROWS = 128
UNITS = 256


def feed_kernel(
    scalars,
    c0,
    c1,
    c2,
    c3,
    tokens,
    grad_output,
    w_out,
    norms,
    up0,
    up1,
    up2,
    up3,
    down0,
    down1,
    down2,
    down3,
    output,
    normed_out,
    branch_grad_out,
    resid_grad_out,
    grad_w_out,
    norm_grads,
    g0,
    g1,
    g2,
    g3,
    normed,
    unit_one,
    recip_one,
    hidden,
    slope,
    summed_grad,
    attended_grad,
):
    me = scalars[3]
    width, block = c0.shape
    features = tokens.shape[1]
    units = up0.shape[1]
    ups = (up0, up1, up2, up3)
    downs = (down0, down1, down2, down3)
    gain_one, shift_one = norms[0:1, :], norms[1:2, :]
    gain_two, shift_two = norms[2:3, :], norms[3:4, :]
    pieces = block // ROWS
    norm_grads[...] = jnp.zeros_like(norm_grads)

    def rows_of(i):
        return pl.ds(pl.multiple_of(i * ROWS, ROWS), ROWS)

    def weight_rows(at):
        return pl.ds(pl.multiple_of((me ^ at) * width, width), width)

    @pl.loop(0, pieces)
    def _(i):
        rows = rows_of(i)
        resid = tokens[rows, :].astype(F32)
        for at, c in enumerate((c0, c1, c2, c3)):
            resid += dot_tn(c[:, rows], w_out[weight_rows(at), :])
        unit, recip = unit_norm(resid)
        unit_one[rows, :] = unit
        recip_one[rows, :] = jnp.broadcast_to(recip, (ROWS, 128))
        value = unit * gain_one + shift_one
        normed[rows, :] = value
        normed_out[rows, :] = value.astype(BF16)

    for s, up in enumerate(ups):

        @pl.loop(0, units // UNITS)
        def _(j):
            columns = lane_slice(j * UNITS, UNITS)
            target = lane_slice(s * units + j * UNITS, UNITS)
            value, derivative = gelu_and_slope(dot_nn(normed_out[...], up[:, columns]))
            hidden[:, target] = value.astype(BF16)
            slope[:, target] = derivative

    @pl.loop(0, pieces)
    def _(i):
        rows = rows_of(i)
        total = normed[rows, :]
        for s, down in enumerate(downs):
            total += dot_nn(hidden[rows, s * units : (s + 1) * units], down[...])
        unit, recip = unit_norm(total)
        output[rows, :] = unit * gain_two + shift_two
        top = grad_output[rows, :].astype(F32)
        norm_grads[2:3, :] += jnp.sum(top * unit, axis=0, keepdims=True)
        norm_grads[3:4, :] += jnp.sum(top, axis=0, keepdims=True)
        grad = unit_back(top * gain_two, unit, recip)
        summed_grad[rows, :] = grad
        branch_grad_out[rows, :] = grad.astype(BF16)

    for s, down in enumerate(downs):

        @pl.loop(0, units // UNITS)
        def _(j):
            target = lane_slice(s * units + j * UNITS, UNITS)
            grad = dot_nt(
                branch_grad_out[...], down[pl.ds(pl.multiple_of(j * UNITS, UNITS), UNITS), :]
            )
            hidden[:, target] = (slope[:, target] * grad).astype(BF16)

    @pl.loop(0, pieces)
    def _(i):
        rows = rows_of(i)
        total = summed_grad[rows, :]
        for s, up in enumerate(ups):
            total += dot_nt(hidden[rows, s * units : (s + 1) * units], up[...])
        unit = unit_one[rows, :]
        norm_grads[0:1, :] += jnp.sum(total * unit, axis=0, keepdims=True)
        norm_grads[1:2, :] += jnp.sum(total, axis=0, keepdims=True)
        grad = unit_back(total * gain_one, unit, recip_one[rows, :1])
        resid_grad_out[rows, :] = grad
        attended_grad[rows, :] = grad.astype(BF16)

    for at, (c, g) in enumerate(((c0, g0), (c1, g1), (c2, g2), (c3, g3))):
        rows = weight_rows(at)
        g[...] = dot_nt(w_out[rows, :], attended_grad[...]).astype(BF16)
        grad_w_out[rows, :] = dot_nn(c[...], attended_grad[...])


def feed(scalars, contexts, tokens, grad_output, w_out, norms, ups, downs):
    width, block = contexts[0].shape
    features = tokens.shape[1]
    units = ups[0].shape[1]
    out_shape = (
        jax.ShapeDtypeStruct((block, features), F32),
        jax.ShapeDtypeStruct((block, features), BF16),
        jax.ShapeDtypeStruct((block, features), BF16),
        jax.ShapeDtypeStruct((block, features), F32),
        jax.ShapeDtypeStruct((features, features), F32),
        jax.ShapeDtypeStruct((8, features), F32),
        *[jax.ShapeDtypeStruct((width, block), BF16) for _ in range(4)],
    )
    vmem = pl.BlockSpec(memory_space=pltpu.VMEM)
    operands = (scalars, *contexts, tokens, grad_output, w_out, norms, *ups, *downs)
    return pl.pallas_call(
        feed_kernel,
        name="feed",
        out_shape=out_shape,
        in_specs=[pl.BlockSpec(memory_space=pltpu.SMEM)] + [vmem] * (len(operands) - 1),
        out_specs=[vmem] * len(out_shape),
        scratch_shapes=[
            pltpu.VMEM((block, features), F32),
            pltpu.VMEM((block, features), F32),
            pltpu.VMEM((block, 128), F32),
            pltpu.VMEM((block, 4 * units), BF16),
            pltpu.VMEM((block, 4 * units), F32),
            pltpu.VMEM((block, features), F32),
            pltpu.VMEM((block, features), BF16),
        ],
        compiler_params=pltpu.CompilerParams(vmem_limit_bytes=VMEM_LIMIT),
        cost_estimate=pl.CostEstimate(
            flops=25_000_000_000, bytes_accessed=30_000_000, transcendentals=6_000_000
        ),
    )(*operands)


def feed_weights_kernel(
    n0, n1, n2, n3, b0, b1, b2, b3, up, down, grad_up, grad_down, up_total, down_total
):
    units = up.shape[1]
    for at, (n, b) in enumerate(((n0, b0), (n1, b1), (n2, b2), (n3, b3))):

        @pl.loop(0, units // UNITS)
        def _(j):
            columns = lane_slice(j * UNITS, UNITS)
            rows = pl.ds(pl.multiple_of(j * UNITS, UNITS), UNITS)
            value, derivative = gelu_and_slope(dot_nn(n[...], up[:, columns]))
            grad_hidden = dot_nt(b[...], down[rows, :])
            grad_pre = (derivative * grad_hidden).astype(BF16)
            down_part = dot_tn(value.astype(BF16), b[...])
            up_part = dot_tn(n[...], grad_pre)
            if at == 0:
                down_total[rows, :] = down_part
                up_total[:, columns] = up_part
            elif at < 3:
                down_total[rows, :] += down_part
                up_total[:, columns] += up_part
            else:
                grad_down[rows, :] = (down_total[rows, :] + down_part).astype(BF16)
                grad_up[:, columns] = (up_total[:, columns] + up_part).astype(BF16)


def feed_weights(normeds, branch_grads, up, down):
    features, units = up.shape
    vmem = pl.BlockSpec(memory_space=pltpu.VMEM)
    return pl.pallas_call(
        feed_weights_kernel,
        name="feed_weights",
        out_shape=(
            jax.ShapeDtypeStruct((features, units), BF16),
            jax.ShapeDtypeStruct((units, features), BF16),
        ),
        in_specs=[vmem] * 10,
        out_specs=[vmem] * 2,
        scratch_shapes=[
            pltpu.VMEM((features, units), F32),
            pltpu.VMEM((units, features), F32),
        ],
        compiler_params=pltpu.CompilerParams(vmem_limit_bytes=VMEM_LIMIT),
        cost_estimate=pl.CostEstimate(
            flops=18_000_000_000, bytes_accessed=12_000_000, transcendentals=6_000_000
        ),
    )(*normeds, *branch_grads, up, down)


def to_partner(array, axis, size, bit):
    return lax.ppermute(array, axis, [(i, i ^ bit) for i in range(size)])


def gather_tensor(array):
    one = to_partner(array, "tensor", 4, 1)
    two = to_partner(array, "tensor", 4, 2)
    three = to_partner(two, "tensor", 4, 1)
    return (array, one, two, three)


def exchange_tensor(blocks):
    return (
        blocks[0],
        to_partner(blocks[1], "tensor", 4, 1),
        to_partner(blocks[2], "tensor", 4, 2),
        to_partner(blocks[3], "tensor", 4, 3),
    )


def make_bands(conv_weight):
    apart = (
        lax.broadcasted_iota(jnp.int32, (BAND_IN, BAND_OUT), 0)
        - PAD
        - lax.broadcasted_iota(jnp.int32, (BAND_IN, BAND_OUT), 1)
        + REACH
    )
    band = jnp.zeros((conv_weight.shape[0], BAND_IN, BAND_OUT), F32)
    for tap in range(KERNEL):
        band = jnp.where(apart[None] == tap, conv_weight[:, tap][:, None, None], band)
    return jnp.stack(split_low(band), axis=1)


def sum_dp(array, size):
    me = lax.axis_index("dp")
    bits = [1 << b for b in range(size.bit_length() - 1)]
    for bit in bits:
        half = array.shape[0] // 2
        low, high = array[:half], array[half:]
        mine = (me & bit) != 0
        got = to_partner(jnp.where(mine, low, high), "dp", size, bit)
        array = (jnp.where(mine, high, low).astype(F32) + got.astype(F32)).astype(array.dtype)
    for bit in reversed(bits):
        mine = (me & bit) != 0
        got = to_partner(array, "dp", size, bit)
        array = jnp.concatenate(
            [jnp.where(mine, got, array), jnp.where(mine, array, got)], axis=0
        )
    return array


def solution(mesh):
    dp_size = mesh.shape["dp"]

    def shards(
        tokens,
        w_query,
        w_key,
        w_value,
        conv_weight,
        w_out,
        gain_one,
        shift_one,
        w_up,
        w_down,
        gain_two,
        shift_two,
        lengths,
        grad_output,
    ):
        width = w_query.shape[1]
        heads = width // HEAD
        features = tokens.shape[1]
        me = lax.axis_index("tensor").astype(jnp.int32)
        scalars = jnp.concatenate([lengths[0], me[None]])
        blocks = gather_tensor(tokens)
        w_t = jnp.concatenate([w_query.T, w_key.T, w_value.T], axis=0)
        bands = make_bands(conv_weight)
        bands_back = make_bands(conv_weight[:, ::-1])
        norms = jnp.stack([gain_one, shift_one, gain_two, shift_two])
        ups = gather_tensor(w_up)
        downs = gather_tensor(w_down)

        attended = attend(scalars, blocks, w_t, bands)
        saved = (attended[0], *attended[5:])
        contexts = exchange_tensor(attended[1:5])
        (
            output,
            normed_low,
            branch_grad,
            resid_grad,
            grad_w_out,
            norm_grads,
            *context_grads,
        ) = feed(scalars, contexts, tokens, grad_output, w_out, norms, ups, downs)
        context_grads = exchange_tensor(context_grads)
        normeds = gather_tensor(normed_low)
        branch_grads = gather_tensor(branch_grad)
        grad_up, grad_down = feed_weights(normeds, branch_grads, w_up, w_down)
        ffn_grads = sum_dp(jnp.concatenate([grad_up, grad_down], axis=0), dp_size)

        grad_w_t, taps, *token_grads = attend_back(
            scalars, saved, bands_back, context_grads, blocks, w_t
        )
        got = (
            to_partner(token_grads[1], "tensor", 4, 1),
            to_partner(token_grads[3], "tensor", 4, 1),
        )
        away = (token_grads[2].astype(F32) + got[1].astype(F32)).astype(BF16)
        here = token_grads[0].astype(F32) + got[0].astype(F32)
        arrived = to_partner(away, "tensor", 4, 2)
        grad_tokens = resid_grad + here + arrived.astype(F32)

        qkv_grads = sum_dp(grad_w_t.astype(BF16), dp_size)
        taps = lax.psum(taps, "dp")
        small = lax.psum(
            jnp.concatenate([grad_w_out, norm_grads], axis=0).astype(BF16), ("dp", "tensor")
        ).astype(F32)
        qkv_wide = qkv_grads.astype(F32)
        return (
            output,
            grad_tokens,
            qkv_wide[:width].T,
            qkv_wide[width : 2 * width].T,
            qkv_wide[2 * width :].T,
            taps[:heads, :KERNEL],
            small[:features],
            small[features],
            small[features + 1],
            ffn_grads[:features].astype(F32),
            ffn_grads[features:].astype(F32),
            small[features + 2],
            small[features + 3],
        )

    rows = P(("dp", "tensor"), None)
    columns = P(None, "tensor")
    in_specs = (
        rows,
        columns,
        columns,
        columns,
        P("tensor", None),
        P(),
        P(),
        P(),
        columns,
        P("tensor", None),
        P(),
        P(),
        P("dp", None),
        rows,
    )
    out_specs = (
        rows,
        rows,
        columns,
        columns,
        columns,
        P("tensor", None),
        P(),
        P(),
        P(),
        columns,
        P("tensor", None),
        P(),
        P(),
    )
    return jax.shard_map(shards, mesh=mesh, in_specs=in_specs, out_specs=out_specs, check_vma=False)
```

```python
import jax
import jax.numpy as jnp
from jax import lax
from jax.experimental import pallas as pl
from jax.experimental.pallas import tpu as pltpu
from jax.sharding import PartitionSpec as P

HEAD = 64
LANDMARKS = 64
NS_ITERS = 6
KERNEL = 33
SEQS = 3
MARKS = 192
REACH = KERNEL // 2
PAD = 128
BAND_IN = 512
BAND_OUT = 256
TILE = 512
AHEAD = 20
VMEM_LIMIT = 60 * 1024 * 1024
F32 = jnp.float32
BF16 = jnp.bfloat16


def dot_nn(a, b):
    return lax.dot_general(a, b, (((1,), (0,)), ((), ())), preferred_element_type=F32)


def dot_nt(a, b):
    return lax.dot_general(a, b, (((1,), (1,)), ((), ())), preferred_element_type=F32)


def dot_tn(a, b):
    return lax.dot_general(a, b, (((0,), (0,)), ((), ())), preferred_element_type=F32)


def split_low(a):
    high = a.astype(BF16)
    return (high, (a - high.astype(F32)).astype(BF16))


def dot_three(a, b, dot=dot_nn):
    a_high, a_low = a
    b_high, b_low = b
    return dot(a_high, b_high) + (dot(a_high, b_low) + dot(a_low, b_high))


def block_mask(dtype):
    rows = lax.broadcasted_iota(jnp.int32, (MARKS, MARKS), 0) // LANDMARKS
    columns = lax.broadcasted_iota(jnp.int32, (MARKS, MARKS), 1) // LANDMARKS
    return jnp.where(rows == columns, 1.0, 0.0).astype(dtype)


def spread(packed, mask):
    return jnp.concatenate([packed] * SEQS, axis=0) * mask


def spread_split(packed, mask):
    high, low = split_low(packed)
    return (spread(high, mask), spread(low, mask))


def fold(blocks):
    return (
        blocks[:LANDMARKS] + blocks[LANDMARKS : 2 * LANDMARKS] + blocks[2 * LANDMARKS :]
    )


def packed_identity():
    rows = lax.broadcasted_iota(jnp.int32, (LANDMARKS, MARKS), 0)
    columns = lax.broadcasted_iota(jnp.int32, (LANDMARKS, MARKS), 1) % LANDMARKS
    return jnp.where(rows == columns, 1.0, 0.0).astype(F32)


def sequence_of(places, first_end, second_end):
    return (places >= first_end).astype(jnp.int32) + (places >= second_end).astype(jnp.int32)


def lane_slice(start, width):
    return pl.ds(pl.multiple_of(start, 128), width)


def row_block(i, size):
    return pl.ds(pl.multiple_of(i * size, size), size)


class Layout:
    def __init__(self, scalars, group_size):
        self.first_end = scalars[0]
        self.second_end = scalars[0] + scalars[1]
        self.group_size = group_size
        self.tiles = group_size // TILE
        last = [
            (self.first_end - 1) // TILE,
            (self.second_end - 1) // TILE,
            self.tiles - 1,
        ]
        self.first_tile = [0, self.first_end // TILE, self.second_end // TILE]
        counts = [b - a + 1 for a, b in zip(self.first_tile, last, strict=True)]
        self.before = [0, counts[0], counts[0] + counts[1]]
        self.pairs = counts[0] + counts[1] + counts[2]

    def pick(self, sequence, values):
        return jnp.where(
            sequence == 0, values[0], jnp.where(sequence == 1, values[1], values[2])
        )

    def pair(self, p):
        sequence = (p >= self.before[1]).astype(jnp.int32) + (p >= self.before[2]).astype(
            jnp.int32
        )
        tile = p - self.pick(sequence, self.before) + self.pick(sequence, self.first_tile)
        start = self.pick(sequence, [0, self.first_end, self.second_end])
        end = self.pick(sequence, [self.first_end, self.second_end, self.group_size])
        return sequence, tile, start, end

    def own(self, tile, start, end):
        places = tile * TILE + lax.broadcasted_iota(jnp.int32, (LANDMARKS, TILE), 1)
        return (places >= start) & (places < end)

    def pool(self, tile, start, end):
        places = tile * TILE + lax.broadcasted_iota(jnp.int32, (1, TILE), 1)
        length = jnp.full((1, TILE), end - start, jnp.int32).astype(F32)
        numerator = ((places - start + 1) * LANDMARKS - 1).astype(F32) + length + 0.5
        segment = jnp.floor(numerator / length).astype(jnp.int32) - 1
        segment = jnp.where((places >= start) & (places < end), segment, -1)
        marks = lax.broadcasted_iota(jnp.int32, (LANDMARKS, TILE), 0)
        return jnp.where(marks == segment, 1.0, 0.0).astype(BF16)

    def counts(self):
        marks = lax.broadcasted_iota(jnp.int32, (MARKS, 1), 0)
        sequence = marks // LANDMARKS
        k = marks % LANDMARKS
        length = self.pick(
            sequence,
            [
                self.first_end,
                self.second_end - self.first_end,
                self.group_size - self.second_end,
            ],
        )
        upper = lax.shift_right_logical((k + 1) * length, 6)
        return (upper - lax.shift_right_logical(k * length, 6)).astype(F32)

    def same(self, start):
        into = start - PAD + lax.broadcasted_iota(jnp.int32, (BAND_IN, 1), 0)
        out = start + lax.broadcasted_iota(jnp.int32, (1, BAND_OUT), 1)
        return sequence_of(into, self.first_end, self.second_end) == sequence_of(
            out, self.first_end, self.second_end
        )


class Joined:
    def __init__(self, *pieces):
        self.pieces = pieces
        first = pieces[0][0]
        self.shape = (sum(rows for _, _, rows in pieces), first.shape[1])
        self.dtype = first.dtype

    def copies(self, sources, local):
        pairs, at = [], 0
        for source, (_, start, rows) in zip(sources, self.pieces, strict=True):
            pairs.append((source.at[start : start + rows, :], local.at[at : at + rows, :]))
            at += rows
        return pairs


class Io:
    def __init__(self, copies, inputs, outputs, targets, in_sems, out_sems):
        self.inputs, self.outputs = inputs, outputs
        self.arriving = [
            [
                pltpu.make_async_copy(source, local, in_sems.at[at])
                for source, local, at in group
            ]
            for group in copies
        ]
        self.leaving = [
            pltpu.make_async_copy(local, target, out_sems.at[i])
            for i, (local, target) in enumerate(zip(outputs, targets, strict=True))
        ]
        self.sent = set()
        self.started = 0
        self.waited = set()
        self.start_to(AHEAD)

    def start_to(self, end):
        for group in self.arriving[self.started : end]:
            for copy in group:
                copy.start()
        self.started = max(self.started, min(end, len(self.arriving)))

    def need(self, *which):
        self.start_to(max(which) + 1 + AHEAD)
        for i in which:
            if i not in self.waited:
                self.waited.add(i)
                for copy in self.arriving[i]:
                    copy.wait()
        return [self.inputs[i] for i in which]

    def send(self, *which):
        for i in which:
            self.sent.add(i)
            self.leaving[i].start()

    def close(self):
        self.need(*range(len(self.arriving)))
        self.send(*[i for i in range(len(self.leaving)) if i not in self.sent])
        for copy in self.leaving:
            copy.wait()


def local_call(kernel, name, scalars, operands, out_shape, scratch, gigaflops):
    anywhere = pl.BlockSpec(memory_space=pl.ANY)
    flat = [
        a
        for o in operands
        for a in ([piece[0] for piece in o.pieces] if isinstance(o, Joined) else [o])
    ]
    moved = sum(x.size * x.dtype.itemsize for x in (*flat, *out_shape))
    n_in, n_out, n_flat = len(operands), len(out_shape), len(flat)

    def body(scalar_ref, *refs):
        sources, refs = refs[:n_flat], refs[n_flat:]
        targets, refs = refs[:n_out], refs[n_out:]
        inputs, refs = refs[:n_in], refs[n_in:]
        outputs, refs = refs[:n_out], refs[n_out:]
        copies, at = [], 0
        for o, local in zip(operands, inputs, strict=True):
            count = len(o.pieces) if isinstance(o, Joined) else 1
            mine = sources[at : at + count]
            pairs = o.copies(mine, local) if isinstance(o, Joined) else [(mine[0], local)]
            copies.append([(a, b, at + i) for i, (a, b) in enumerate(pairs)])
            at += count
        io = Io(copies, inputs, outputs, targets, refs[0], refs[1])
        kernel(io, scalar_ref, *refs[2:])
        io.close()

    return pl.pallas_call(
        body,
        name=name,
        out_shape=out_shape,
        in_specs=[pl.BlockSpec(memory_space=pltpu.SMEM)] + [anywhere] * n_flat,
        out_specs=[anywhere] * n_out,
        scratch_shapes=[
            *[pltpu.VMEM(x.shape, x.dtype) for x in operands],
            *[pltpu.VMEM(x.shape, x.dtype) for x in out_shape],
            pltpu.SemaphoreType.DMA((n_flat,)),
            pltpu.SemaphoreType.DMA((n_out,)),
            *scratch,
        ],
        compiler_params=pltpu.CompilerParams(vmem_limit_bytes=VMEM_LIMIT),
        cost_estimate=pl.CostEstimate(
            flops=gigaflops * 1_000_000_000, bytes_accessed=moved, transcendentals=0
        ),
    )(scalars, *flat)


def shape_of(dtype, *shape):
    return jax.ShapeDtypeStruct(shape, dtype)


def wide(narrow):
    return jnp.concatenate([narrow] * (TILE // 128), axis=1)


def attend_kernel(
    io,
    scalars,
    context,
    scores,
    pooled,
    tops,
    totals,
    q_lands,
    k_lands,
    mvts,
):
    w_t, bands = io.inputs[0], io.inputs[5]
    qkv_t, c0, c1, c2, c3, land_out, mark_values_out, summary_out = io.outputs[:8]
    steps_out, among_out, inverse_out, lse_to, lse_from = io.outputs[8:]
    width = w_t.shape[0] // 3
    heads = width // HEAD
    block = io.inputs[1].shape[0]
    group_size = 4 * block
    layout = Layout(scalars, group_size)
    me = scalars[3]
    qk_scale = HEAD ** (-0.25)

    qkv_t[:, :PAD] = jnp.zeros((3 * width, PAD), BF16)
    qkv_t[:, PAD + group_size :] = jnp.zeros((3 * width, PAD), BF16)
    io.need(0)
    for at in range(4):
        x = io.need(1 + at)[0]
        lanes = lane_slice(PAD + (me ^ at) * block, block)
        qkv_t[: 2 * width, lanes] = (dot_nt(w_t[: 2 * width, :], x[...]) * qk_scale).astype(BF16)
        qkv_t[2 * width :, lanes] = dot_nt(w_t[2 * width :, :], x[...]).astype(BF16)
    io.send(0)

    pooled[...] = jnp.zeros_like(pooled)

    @pl.loop(0, layout.pairs)
    def _(p):
        sequence, tile, start, end = layout.pair(p)
        rows = row_block(sequence, LANDMARKS)
        pool = layout.pool(tile, start, end)
        pooled[rows, :] += dot_nt(pool, qkv_t[: 2 * width, lane_slice(PAD + tile * TILE, TILE)])

    pooled[...] = pooled[...] / layout.counts()
    land_t = pooled[...].T.astype(BF16)
    land_out[...] = land_t
    for h in range(heads):
        q_lands[h] = pooled[:, h * HEAD : (h + 1) * HEAD].astype(BF16)
        k_lands[h] = pooled[:, width + h * HEAD : width + (h + 1) * HEAD].astype(BF16)
    io.send(5)

    tops[...] = jnp.full(tops.shape, -1e30, F32)
    totals[...] = jnp.zeros_like(totals)
    summary_out[...] = jnp.zeros_like(summary_out)

    each = range(heads)

    def part_rows(part, h):
        return slice(part * width + h * HEAD, part * width + (h + 1) * HEAD)

    @pl.loop(0, layout.pairs)
    def _(p):
        sequence, tile, start, end = layout.pair(p)
        rows = row_block(sequence, LANDMARKS)
        own = layout.own(tile, start, end)
        padded = lane_slice(PAD + tile * TILE, TILE)
        raw = [dot_nn(q_lands[h, rows, :], qkv_t[part_rows(1, h), padded]) for h in each]
        masked = [jnp.where(own, raw[h], -1e30) for h in each]
        top = [tops[h, rows, :] for h in each]
        for lane in range(0, TILE, 128):
            top = [jnp.maximum(top[h], masked[h][:, lane : lane + 128]) for h in each]
        for h in each:
            scores[h, :, lane_slice(p * TILE, TILE)] = masked[h]
            tops[h, rows, :] = top[h]

    for h in range(heads):
        tops[h] = jnp.broadcast_to(jnp.max(tops[h], axis=1, keepdims=True), (MARKS, 128))

    @pl.loop(0, layout.pairs)
    def _(p):
        sequence, _, _, _ = layout.pair(p)
        rows = row_block(sequence, LANDMARKS)
        at = lane_slice(p * TILE, TILE)
        raised = [jnp.exp(scores[h, :, at] - wide(tops[h, rows, :])) for h in each]
        total = [totals[h, rows, :] for h in each]
        for lane in range(0, TILE, 128):
            total = [total[h] + raised[h][:, lane : lane + 128] for h in each]
        for h in each:
            scores[h, :, at] = raised[h]
            totals[h, rows, :] = total[h]

    for h in range(heads):
        total = jnp.broadcast_to(jnp.sum(totals[h], axis=1, keepdims=True), (MARKS, 128))
        lse_from[h] = tops[h] + jnp.log(total)
        totals[h] = 1.0 / total

    @pl.loop(0, layout.pairs)
    def _(p):
        sequence, tile, _, _ = layout.pair(p)
        rows = row_block(sequence, LANDMARKS)
        at = lane_slice(p * TILE, TILE)
        padded = lane_slice(PAD + tile * TILE, TILE)
        low = [(scores[h, :, at] * wide(totals[h, rows, :])).astype(BF16) for h in each]
        part = [dot_nt(low[h], qkv_t[part_rows(2, h), padded]) for h in each]
        part = [summary_out[h, rows, :] + part[h] for h in each]
        for h in each:
            summary_out[h, rows, :] = part[h]

    io.send(7, 12)
    mask_f = block_mask(F32)
    mask_b = block_mask(BF16)
    eye = packed_identity()
    amongs = []
    approxes = []
    for h in range(heads):
        raw = dot_nt(q_lands[h], k_lands[h])
        masked = jnp.where(mask_f > 0.0, raw, -1e30)
        row_top = jnp.max(masked, axis=1, keepdims=True)
        raised = jnp.exp(masked - row_top)
        among = raised / jnp.sum(raised, axis=1, keepdims=True)
        column_top = jnp.max(jnp.sum(among, axis=0, keepdims=True), axis=1, keepdims=True)
        packed = fold(among)
        among_out[h] = packed
        amongs.append(split_low(packed))
        approxes.append(fold(among.T) / column_top)

    for step in range(NS_ITERS):
        product = [
            dot_three(amongs[h], spread_split(approxes[h], mask_b)) for h in range(heads)
        ]
        split = [split_low(product[h]) for h in range(heads)]
        bracket = [7.0 * eye - product[h] for h in range(heads)]
        second = [
            15.0 * eye - dot_three(split[h], spread_split(bracket[h], mask_b))
            for h in range(heads)
        ]
        third = [
            13.0 * eye - dot_three(split[h], spread_split(second[h], mask_b))
            for h in range(heads)
        ]
        for h in range(heads):
            steps_out[h, 4 * step] = approxes[h]
            steps_out[h, 4 * step + 1] = product[h]
            steps_out[h, 4 * step + 2] = second[h]
            steps_out[h, 4 * step + 3] = third[h]
        approxes = [
            0.25 * dot_three(split_low(approxes[h]), spread_split(third[h], mask_b))
            for h in range(heads)
        ]

    for h in range(heads):
        inverse_out[h] = approxes[h]
        mark_values = dot_three(
            spread_split(approxes[h], mask_b), split_low(summary_out[h])
        )
        mark_values_out[h] = mark_values.astype(BF16)
        for s in range(SEQS):
            part = mark_values[s * LANDMARKS : (s + 1) * LANDMARKS, :]
            mvts[SEQS * h + s] = part.T.astype(BF16)
    io.send(6, 8, 9, 10)
    io.need(5)

    @pl.loop(0, group_size // BAND_OUT)
    def _(i):
        start = i * BAND_OUT
        same = jnp.where(layout.same(start), 1.0, 0.0).astype(BF16)
        smooth = [
            dot_nn(qkv_t[part_rows(2, h), lane_slice(start, BAND_IN)], bands[h] * same)
            for h in each
        ]
        for h in each:
            context[part_rows(0, h), lane_slice(start, BAND_OUT)] = smooth[h]

    @pl.loop(0, layout.pairs)
    def _(p):
        sequence, tile, start, end = layout.pair(p)
        rows = row_block(sequence, LANDMARKS)
        own = layout.own(tile, start, end)
        at = lane_slice(tile * TILE, TILE)
        padded = lane_slice(PAD + tile * TILE, TILE)
        raw = [dot_nn(k_lands[h, rows, :], qkv_t[part_rows(0, h), padded]) for h in each]
        top = [jnp.max(raw[h], axis=0, keepdims=True) for h in each]
        raised = [jnp.exp(raw[h] - top[h]) for h in each]
        total = [jnp.sum(raised[h], axis=0, keepdims=True) for h in each]
        low = [
            jnp.where(own, raised[h] * (1.0 / total[h]), 0.0).astype(BF16) for h in each
        ]
        blended = [dot_nn(mvts[SEQS * h + sequence], low[h]) for h in each]
        blended = [context[part_rows(0, h), at] + blended[h] for h in each]
        lse = [
            jnp.where(own[:1], top[h] + jnp.log(total[h]), lse_to[h : h + 1, at]) for h in each
        ]
        for h in each:
            lse_to[h : h + 1, at] = lse[h]
            context[part_rows(0, h), at] = blended[h]

    for at, out in enumerate((c0, c1, c2, c3)):
        out[...] = context[:, lane_slice((me ^ at) * block, block)].astype(BF16)


def attend(scalars, blocks, w_t, bands):
    block = blocks[0].shape[0]
    group_size = 4 * block
    width = w_t.shape[0] // 3
    heads = width // HEAD
    most_pairs = group_size // TILE + SEQS - 1
    return local_call(
        attend_kernel,
        "attend",
        scalars,
        (w_t, *blocks, bands),
        (
            shape_of(BF16, 3 * width, group_size + 2 * PAD),
            *[shape_of(BF16, width, block) for _ in range(4)],
            shape_of(BF16, 2 * width, MARKS),
            shape_of(BF16, heads, MARKS, HEAD),
            shape_of(F32, heads, MARKS, HEAD),
            shape_of(F32, heads, 4 * NS_ITERS, LANDMARKS, MARKS),
            shape_of(F32, heads, LANDMARKS, MARKS),
            shape_of(F32, heads, LANDMARKS, MARKS),
            shape_of(F32, heads, group_size),
            shape_of(F32, heads, MARKS, 128),
        ),
        [
            pltpu.VMEM((width, group_size), F32),
            pltpu.VMEM((heads, LANDMARKS, most_pairs * TILE), F32),
            pltpu.VMEM((MARKS, 2 * width), F32),
            pltpu.VMEM((heads, MARKS, 128), F32),
            pltpu.VMEM((heads, MARKS, 128), F32),
            pltpu.VMEM((heads, MARKS, HEAD), BF16),
            pltpu.VMEM((heads, MARKS, HEAD), BF16),
            pltpu.VMEM((SEQS * heads, HEAD, LANDMARKS), BF16),
        ],
        30,
    )


def attend_back_kernel(
    io,
    scalars,
    context_grad,
    partial_value,
    correlation,
    q_lands,
    k_lands,
    q_lands_t,
    k_lands_t,
    grad_summaries,
    grad_summaries_t,
    offsets,
):
    g_refs = io.inputs[:4]
    qkv_t, land_t, mark_values_in, summary_in = io.inputs[4:8]
    inverse_in, lse_to, lse_from = io.inputs[8:11]
    bands = io.inputs[11]
    grad_value, taps_out, partial_query, partial_key = io.outputs[:4]
    grad_q_land, grad_k_land, grad_mark = io.outputs[4:]
    width, block = g_refs[0].shape
    heads = width // HEAD
    group_size = 4 * block
    layout = Layout(scalars, group_size)
    me = scalars[3]
    each = range(heads)

    def part_rows(part, h):
        return slice(part * width + h * HEAD, part * width + (h + 1) * HEAD)

    io.need(*range(11))
    context_grad[:, :PAD] = jnp.zeros((width, PAD), BF16)
    context_grad[:, PAD + group_size :] = jnp.zeros((width, PAD), BF16)
    for at, g in enumerate(g_refs):
        context_grad[:, lane_slice(PAD + (me ^ at) * block, block)] = g[...]

    for h in range(heads):
        q_t = land_t[h * HEAD : (h + 1) * HEAD, :].astype(F32)
        k_t = land_t[width + h * HEAD : width + (h + 1) * HEAD, :].astype(F32)
        q_lands[h] = q_t.T.astype(BF16)
        k_lands[h] = k_t.T.astype(BF16)
        for s in range(SEQS):
            columns = slice(s * LANDMARKS, (s + 1) * LANDMARKS)
            q_lands_t[SEQS * h + s] = q_t[:, columns].astype(BF16)
            k_lands_t[SEQS * h + s] = k_t[:, columns].astype(BF16)

    for ref in (grad_k_land, grad_mark, grad_q_land, partial_query, partial_key, partial_value):
        ref[...] = jnp.zeros_like(ref)

    @pl.loop(0, layout.pairs)
    def _(p):
        sequence, tile, start, end = layout.pair(p)
        rows = row_block(sequence, LANDMARKS)
        own = layout.own(tile, start, end)
        at = lane_slice(tile * TILE, TILE)
        padded = lane_slice(PAD + tile * TILE, TILE)
        query = [qkv_t[part_rows(0, h), padded] for h in each]
        out_grad = [context_grad[part_rows(0, h), padded] for h in each]
        raw = [dot_nn(k_lands[h, rows, :], query[h]) for h in each]
        grad_to = [dot_nn(mark_values_in[h, rows, :], out_grad[h]) for h in each]
        probs = [
            jnp.exp(jnp.where(own, raw[h] - lse_to[h : h + 1, at], -1e30)) for h in each
        ]
        inner = [jnp.sum(grad_to[h] * probs[h], axis=0, keepdims=True) for h in each]
        grad_scores = [(probs[h] * (grad_to[h] - inner[h])).astype(BF16) for h in each]
        mark_part = [
            grad_mark[h, rows, :] + dot_nt(probs[h].astype(BF16), out_grad[h]) for h in each
        ]
        land_part = [
            grad_k_land[h, rows, :] + dot_nt(grad_scores[h], query[h]) for h in each
        ]
        query_part = [
            partial_query[part_rows(0, h), at]
            + dot_nn(k_lands_t[SEQS * h + sequence], grad_scores[h])
            for h in each
        ]
        for h in each:
            grad_mark[h, rows, :] = mark_part[h]
            grad_k_land[h, rows, :] = land_part[h]
            partial_query[part_rows(0, h), at] = query_part[h]

    io.send(2, 5, 6)
    mask_f = block_mask(F32)
    for h in range(heads):
        mark_split = split_low(grad_mark[h])
        summary = summary_in[h]
        inverse_blocks = spread(inverse_in[h], mask_f).T
        grad_summary = dot_three(split_low(inverse_blocks), mark_split)
        grad_low = grad_summary.astype(BF16)
        grad_summaries[h] = grad_low
        exact = grad_low.astype(F32)
        for s in range(SEQS):
            part = exact[s * LANDMARKS : (s + 1) * LANDMARKS, :]
            grad_summaries_t[SEQS * h + s] = part.T.astype(BF16)
        inner = jnp.sum(exact * summary, axis=1, keepdims=True)
        offsets[h] = jnp.broadcast_to(inner, (MARKS, 128))

    @pl.loop(0, layout.pairs)
    def _(p):
        sequence, tile, start, end = layout.pair(p)
        rows = row_block(sequence, LANDMARKS)
        own = layout.own(tile, start, end)
        at = lane_slice(tile * TILE, TILE)
        padded = lane_slice(PAD + tile * TILE, TILE)
        key = [qkv_t[part_rows(1, h), padded] for h in each]
        value = [qkv_t[part_rows(2, h), padded] for h in each]
        raw = [dot_nn(q_lands[h, rows, :], key[h]) for h in each]
        grad_from = [dot_nn(grad_summaries[h, rows, :], value[h]) for h in each]
        probs = [
            jnp.exp(jnp.where(own, raw[h] - wide(lse_from[h, rows, :]), -1e30)) for h in each
        ]
        grad_scores = [
            (probs[h] * (grad_from[h] - wide(offsets[h, rows, :]))).astype(BF16) for h in each
        ]
        value_part = [
            partial_value[part_rows(0, h), padded]
            + dot_nn(grad_summaries_t[SEQS * h + sequence], probs[h].astype(BF16))
            for h in each
        ]
        land_part = [grad_q_land[h, rows, :] + dot_nt(grad_scores[h], key[h]) for h in each]
        key_part = [
            partial_key[part_rows(0, h), at]
            + dot_nn(q_lands_t[SEQS * h + sequence], grad_scores[h])
            for h in each
        ]
        for h in each:
            partial_value[part_rows(0, h), padded] = value_part[h]
            grad_q_land[h, rows, :] = land_part[h]
            partial_key[part_rows(0, h), at] = key_part[h]

    io.send(3, 4)

    correlation[...] = jnp.zeros_like(correlation)
    io.need(11)

    @pl.loop(0, group_size // BAND_OUT)
    def _(i):
        start = i * BAND_OUT
        padded = lane_slice(PAD + start, BAND_OUT)
        around = lane_slice(start, BAND_IN)
        same = jnp.where(layout.same(start), 1.0, 0.0)
        same_b = same.astype(BF16)
        out_grad = [context_grad[part_rows(0, h), padded] for h in each]
        value_part = [
            partial_value[part_rows(0, h), around] + dot_nt(out_grad[h], bands[h] * same_b)
            for h in each
        ]
        across = [
            dot_tn(qkv_t[part_rows(2, h), around], out_grad[h]) * same for h in each
        ]
        parts = [
            (
                a[:128, :128] + a[128:256, 128:],
                a[128:256, :128] + a[256:384, 128:],
                a[256:384, :128] + a[384:, 128:],
            )
            for a in across
        ]
        for h in each:
            partial_value[part_rows(0, h), around] = value_part[h]
            for at in range(3):
                correlation[h, at] += parts[h][at]

    grad_value[...] = partial_value[:, PAD : PAD + group_size].astype(BF16)
    io.send(0)
    apart = lax.broadcasted_iota(jnp.int32, (128, 128), 0) - lax.broadcasted_iota(
        jnp.int32, (128, 128), 1
    )
    lanes = lax.broadcasted_iota(jnp.int32, (8, 128), 1)
    rows = lax.broadcasted_iota(jnp.int32, (8, 128), 0)
    taps = jnp.zeros((8, 128), F32)
    for h in range(heads):
        for tap in range(KERNEL):
            away = tap - REACH
            picked = jnp.where(apart == away, correlation[h, 1], 0.0)
            if away < 0:
                picked += jnp.where(apart == away + 128, correlation[h, 0], 0.0)
            if away > 0:
                picked += jnp.where(apart == away - 128, correlation[h, 2], 0.0)
            total = jnp.sum(
                jnp.sum(picked, axis=0, keepdims=True), axis=1, keepdims=True
            )
            taps = taps + jnp.where((lanes == tap) & (rows == h), total, 0.0)
    taps_out[...] = taps


def attend_steps_kernel(group_size, io, scalars):
    grad_mark_in, summary_in, among_in, steps_in = io.inputs[:4]
    land_t, grad_q_land, grad_k_land = io.inputs[4:]
    shares = io.outputs[0]
    heads = summary_in.shape[0]
    width = heads * HEAD
    layout = Layout(scalars, group_size)
    each = range(heads)
    mask_f = block_mask(F32)
    mask_b = block_mask(BF16)
    io.need(0, 1, 2)
    carried = [
        fold(dot_three(split_low(summary_in[h]), split_low(grad_mark_in[h]), dot_nt) * mask_f)
        for h in each
    ]
    io.need(*range(3, 7))
    eye = packed_identity()

    def spread_both(pair):
        return tuple(spread(a, mask_b) for a in pair)

    among_wide = [spread_split(among_in[h], mask_b) for h in each]
    among_grads = [jnp.zeros((LANDMARKS, MARKS), F32) for _ in each]
    for step in reversed(range(NS_ITERS)):
        approx = [split_low(steps_in[h, 4 * step]) for h in each]
        product = [steps_in[h, 4 * step + 1] for h in each]
        product_wide = [spread_split(product[h], mask_b) for h in each]
        grad = [split_low(carried[h]) for h in each]
        third = [
            split_low(0.25 * dot_three(grad[h], spread_both(approx[h]))) for h in each
        ]
        through = [
            dot_three(split_low(steps_in[h, 4 * step + 3]), spread_both(grad[h])) for h in each
        ]
        second = [split_low(-dot_three(third[h], product_wide[h])) for h in each]
        from_third = [
            dot_three(split_low(steps_in[h, 4 * step + 2]), spread_both(third[h]))
            for h in each
        ]
        first = [dot_three(second[h], product_wide[h]) for h in each]
        from_second = [
            dot_three(split_low(7.0 * eye - product[h]), spread_both(second[h])) for h in each
        ]
        grad_product = [
            split_low(first[h] - from_third[h] - from_second[h]) for h in each
        ]
        carried = [
            0.25 * through[h] + dot_three(grad_product[h], among_wide[h]) for h in each
        ]
        among_grads = [
            among_grads[h] + dot_three(approx[h], spread_both(grad_product[h])) for h in each
        ]

    for h in each:
        among = spread(among_in[h], mask_f)
        column_sums = jnp.sum(among, axis=0, keepdims=True)
        column_top = jnp.max(column_sums, axis=1, keepdims=True)
        start_grad = carried[h]
        start_blocks = spread(steps_in[h, 0], mask_f).T
        top_grad = -jnp.sum(
            jnp.sum(start_grad * fold(start_blocks), axis=1, keepdims=True),
            axis=0,
            keepdims=True,
        ) / column_top
        at_top = jnp.where(column_sums == column_top, 1.0, 0.0)
        shared = top_grad * at_top / jnp.sum(at_top, axis=1, keepdims=True)
        among_grad = spread(among_grads[h], mask_f).T + (
            spread(start_grad, mask_f) / column_top + shared * mask_f
        )
        inner = jnp.sum(among_grad * among, axis=1, keepdims=True)
        grad_scores = among * (among_grad - inner)
        high, low = split_low(grad_scores)
        back_high, back_low = split_low(grad_scores.T)
        q_land = land_t[h * HEAD : (h + 1) * HEAD, :].astype(F32).T.astype(BF16)
        k_land = land_t[width + h * HEAD : width + (h + 1) * HEAD, :].astype(F32).T.astype(BF16)
        q_total = grad_q_land[h] + (dot_nn(high, k_land) + dot_nn(low, k_land))
        k_total = grad_k_land[h] + (dot_nn(back_high, q_land) + dot_nn(back_low, q_land))
        counts = layout.counts()
        for which, total in enumerate((q_total, k_total)):
            share = total.astype(BF16).astype(F32) / counts
            for s in range(SEQS):
                part = share[s * LANDMARKS : (s + 1) * LANDMARKS, :].T
                shares[which, SEQS * h + s] = part.astype(BF16)


def attend_grads_kernel(io, scalars, grad_qkv, grad_w_t):
    grad_value, taps, partial_query, partial_key, shares, w_t = io.inputs[:6]
    x_refs = io.inputs[6:]
    low_out, high_out, d_refs = io.outputs[0], io.outputs[1], io.outputs[2:]
    width, group_size = partial_query.shape
    heads = width // HEAD
    block, features = x_refs[0].shape
    half = low_out.shape[0]
    me = scalars[3]
    qk_scale = HEAD ** (-0.25)
    layout = Layout(scalars, group_size)
    each = range(heads)

    def part_rows(part, h):
        return slice(part * width + h * HEAD, part * width + (h + 1) * HEAD)

    io.need(0, 2, 3, 4)

    @pl.loop(0, layout.pairs)
    def _(p):
        sequence, tile, start, end = layout.pair(p)
        at = lane_slice(tile * TILE, TILE)
        pool = layout.pool(tile, start, end)
        query = [
            partial_query[part_rows(0, h), at] + dot_nn(shares[0, SEQS * h + sequence], pool)
            for h in each
        ]
        key = [
            partial_key[part_rows(0, h), at] + dot_nn(shares[1, SEQS * h + sequence], pool)
            for h in each
        ]
        for h in each:
            partial_query[part_rows(0, h), at] = query[h]
            partial_key[part_rows(0, h), at] = key[h]

    grad_qkv[:width, :] = partial_query[...].astype(BF16)
    grad_qkv[width : 2 * width, :] = partial_key[...].astype(BF16)
    grad_qkv[2 * width :, :] = grad_value[...]

    io.need(1, 5)
    for at in (3, 1, 2, 0):
        x = io.need(6 + at)[0]
        lanes = lane_slice((me ^ at) * block, block)
        part = dot_nn(grad_qkv[:, lanes], x[...])
        if at == 3:
            grad_w_t[...] = part
        else:
            grad_w_t[...] += part

    def put(start, value):
        end = start + value.shape[0]
        if start < half:
            low_out[start : min(end, half), :] = value[: min(end, half) - start]
        if end > half:
            high_out[max(start, half) - half : end - half, :] = value[max(start, half) - start :]

    put(0, (grad_w_t[: 2 * width] * qk_scale).astype(BF16))
    put(2 * width, grad_w_t[2 * width :].astype(BF16))
    put(3 * width, jnp.zeros((2 * half - 3 * width, features), BF16))
    start = 3 * width - half
    high_out[start : start + 16, :128] = jnp.concatenate(
        [taps[...], jnp.zeros((8, 128), F32)], axis=0
    ).astype(BF16)
    io.send(0, 1)

    for at in (3, 1, 2, 0):
        d = d_refs[at]
        lanes = lane_slice((me ^ at) * block, block)
        scaled = dot_tn(grad_qkv[: 2 * width, lanes], w_t[: 2 * width, :])
        plain = dot_tn(grad_qkv[2 * width :, lanes], w_t[2 * width :, :])
        d[...] = (scaled * qk_scale + plain).astype(BF16)
        io.send(2 + at)


def attend_back(scalars, saved, grads, bands):
    qkv_t, land_t, mark_values, summary, steps, among, inverse, lse_to, lse_from = saved
    width, block = grads[0].shape
    group_size = 4 * block
    heads = width // HEAD
    lands = pltpu.VMEM((heads, MARKS, HEAD), BF16)
    lands_t = pltpu.VMEM((SEQS * heads, HEAD, LANDMARKS), BF16)
    return local_call(
        attend_back_kernel,
        "attend_back",
        scalars,
        (*grads, qkv_t, land_t, mark_values, summary, inverse, lse_to, lse_from, bands),
        (
            shape_of(BF16, width, group_size),
            shape_of(F32, 8, 128),
            shape_of(F32, width, group_size),
            shape_of(F32, width, group_size),
            *[shape_of(F32, heads, MARKS, HEAD) for _ in range(3)],
        ),
        [
            pltpu.VMEM((width, group_size + 2 * PAD), BF16),
            pltpu.VMEM((width, group_size + 2 * PAD), F32),
            pltpu.VMEM((heads, 3, 128, 128), F32),
            lands,
            lands,
            lands_t,
            lands_t,
            lands,
            lands_t,
            pltpu.VMEM((heads, MARKS, 128), F32),
        ],
        8,
    )


def attend_steps(scalars, saved, passed):
    qkv_t, land_t, mark_values, summary, steps, among, inverse, lse_to, lse_from = saved
    grad_q_land, grad_k_land, grad_mark = passed[4:]
    heads = summary.shape[0]

    def kernel(*refs):
        attend_steps_kernel(qkv_t.shape[1] - 2 * PAD, *refs)

    return local_call(
        kernel,
        "attend_steps",
        scalars,
        (grad_mark, summary, among, steps, land_t, grad_q_land, grad_k_land),
        (shape_of(BF16, 2, SEQS * heads, HEAD, LANDMARKS),),
        [],
        5,
    )[0]


def attend_grads(scalars, passed, shares, blocks, w_t, multiple):
    grad_value, taps, partial_query, partial_key = passed[:4]
    block, features = blocks[0].shape
    width, group_size = partial_query.shape
    heads = width // HEAD
    half = -(-(w_t.shape[0] + 16) // (2 * multiple)) * multiple
    return local_call(
        attend_grads_kernel,
        "attend_grads",
        scalars,
        (
            grad_value,
            taps,
            partial_query,
            partial_key,
            shares,
            w_t,
            *blocks,
        ),
        (
            shape_of(BF16, half, features),
            shape_of(BF16, half, features),
            *[shape_of(BF16, block, features) for _ in range(4)],
        ),
        [
            pltpu.VMEM((3 * width, group_size), BF16),
            pltpu.VMEM(w_t.shape, F32),
        ],
        8,
    )


def gelu_and_slope(values):
    z = jnp.abs(values) * 0.7071067811865476
    t = pl.reciprocal(1.0 + 0.3275911 * z)
    poly = t * 1.061405429 - 1.453152027
    for coefficient in (1.421413741, -0.284496736, 0.254829592):
        poly = poly * t + coefficient
    bell = jnp.exp(-z * z)
    half_tail = (0.5 * t) * poly * bell
    below = jnp.where(values >= 0.0, 1.0 - half_tail, half_tail)
    return values * below, below + values * (bell * 0.3989422804014327)


def unit_norm(values):
    row_mean = jnp.mean(values, axis=-1, keepdims=True)
    centered = values - row_mean
    spread_out = jnp.mean(centered * centered, axis=-1, keepdims=True)
    recip = lax.rsqrt(spread_out + 1e-05)
    return (centered * recip, recip)


def unit_back(grad, unit, recip):
    mean_grad = jnp.mean(grad, axis=-1, keepdims=True)
    mean_cross = jnp.mean(grad * unit, axis=-1, keepdims=True)
    return recip * (grad - mean_grad - unit * mean_cross)


ROWS = 320
UNITS = 768


def norm_in_kernel(io, scalars):
    contexts, (tokens, w_out, norms) = io.inputs[:4], io.inputs[4:]
    normed_out, unit_one, recip_one = io.outputs
    me = scalars[3]
    width, block = contexts[0].shape
    io.need(*range(7))

    @pl.loop(0, block // 128)
    def _(i):
        rows = row_block(i, 128)
        resid = tokens[rows, :].astype(F32)
        for at, c in enumerate(contexts):
            resid += dot_tn(c[:, rows], w_out[row_block(me ^ at, width), :])
        unit, recip = unit_norm(resid)
        unit_one[rows, :] = unit
        recip_one[rows, :] = jnp.broadcast_to(recip, (128, 128))
        normed_out[rows, :] = (unit * norms[0:1, :] + norms[1:2, :]).astype(BF16)


def feed_kernel(io, scalars, hidden):
    normed_low, norms = io.inputs[:2]
    ups, downs = io.inputs[2:6], io.inputs[6:10]
    unit_one, grad_output = io.inputs[10:]
    output, slope, summed_grad, branch_grad, norm_grads = io.outputs
    block, features = normed_low.shape
    units = ups[0].shape[0]
    norm_grads[...] = jnp.zeros_like(norm_grads)
    io.need(0, 1)

    for s, up in enumerate(ups):
        io.need(2 + s)

        @pl.loop(0, units // UNITS)
        def _(j):
            target = lane_slice(s * units + j * UNITS, UNITS)
            value, derivative = gelu_and_slope(
                dot_nt(normed_low[...], up[row_block(j, UNITS), :])
            )
            hidden[:, target] = value.astype(BF16)
            slope[:, target] = derivative.astype(BF16)

    io.send(1)
    io.need(*range(6, 12))

    @pl.loop(0, block // ROWS)
    def _(i):
        rows = row_block(i, ROWS)
        total = unit_one[rows, :] * norms[0:1, :] + norms[1:2, :]
        for s, down in enumerate(downs):
            total += dot_nn(hidden[rows, s * units : (s + 1) * units], down[...])
        unit, recip = unit_norm(total)
        output[rows, :] = unit * norms[2:3, :] + norms[3:4, :]
        top = grad_output[rows, :].astype(F32)
        norm_grads[0:1, :] += jnp.sum(top * unit, axis=0, keepdims=True)
        norm_grads[1:2, :] += jnp.sum(top, axis=0, keepdims=True)
        grad = unit_back(top * norms[2:3, :], unit, recip)
        summed_grad[rows, :] = grad
        branch_grad[rows, :] = grad.astype(BF16)


def feed_back_kernel(io, scalars, grad_pre, attended_grad):
    branch_grad, norms = io.inputs[:2]
    downs, slope = io.inputs[2:6], io.inputs[6]
    ups = io.inputs[7:11]
    summed_grad, unit_one, recip_one, w_out = io.inputs[11:15]
    contexts = io.inputs[15:19]
    resid_grad, grad_w_out, norm_grads = io.outputs[:3]
    targets = io.outputs[3:]
    me = scalars[3]
    width, block = contexts[0].shape
    units = ups[0].shape[0]
    norm_grads[...] = jnp.zeros_like(norm_grads)
    io.need(0, 1, 2, 6)

    for s, down in enumerate(downs):
        io.need(2 + s)

        @pl.loop(0, units // UNITS)
        def _(j):
            target = lane_slice(s * units + j * UNITS, UNITS)
            grad = dot_nt(branch_grad[...], down[row_block(j, UNITS), :])
            grad_pre[:, target] = (slope[:, target] * grad).astype(BF16)

    io.need(*range(7, 19))

    @pl.loop(0, block // ROWS)
    def _(i):
        rows = row_block(i, ROWS)
        total = summed_grad[rows, :]
        for s, up in enumerate(ups):
            total += dot_nn(grad_pre[rows, s * units : (s + 1) * units], up[...])
        unit = unit_one[rows, :]
        norm_grads[0:1, :] += jnp.sum(total * unit, axis=0, keepdims=True)
        norm_grads[1:2, :] += jnp.sum(total, axis=0, keepdims=True)
        grad = unit_back(total * norms[0:1, :], unit, recip_one[rows, :1])
        resid_grad[rows, :] = grad
        attended_grad[rows, :] = grad.astype(BF16)

    for at in (3, 2, 1, 0):
        rows = row_block(me ^ at, width)
        targets[at][...] = dot_nt(w_out[rows, :], attended_grad[...]).astype(BF16)
        io.send(3 + at)
    for at, c in enumerate(contexts):
        rows = row_block(me ^ at, width)
        grad_w_out[rows, :] = dot_nn(c[...], attended_grad[...]).astype(BF16)


def norm_in(scalars, contexts, tokens, w_out, norms):
    block, features = tokens.shape
    return local_call(
        norm_in_kernel,
        "norm_in",
        scalars,
        (*contexts, tokens, w_out, norms),
        (
            shape_of(BF16, block, features),
            shape_of(F32, block, features),
            shape_of(F32, block, 128),
        ),
        [],
        6,
    )


def feed(scalars, normed_low, unit_one, grad_output, norms, ups, downs):
    block, features = normed_low.shape
    units = ups[0].shape[0]
    return local_call(
        feed_kernel,
        "feed",
        scalars,
        (normed_low, norms, *ups, *downs, unit_one, grad_output),
        (
            shape_of(F32, block, features),
            shape_of(BF16, block, 4 * units),
            shape_of(F32, block, features),
            shape_of(BF16, block, features),
            shape_of(F32, 8, features),
        ),
        [pltpu.VMEM((block, 4 * units), BF16)],
        22,
    )


def feed_back(scalars, fed, unit_one, recip_one, contexts, w_out, norms, ups, downs):
    slope, summed_grad, branch_grad = fed
    width, block = contexts[0].shape
    features = w_out.shape[0]
    units = ups[0].shape[0]
    return local_call(
        feed_back_kernel,
        "feed_back",
        scalars,
        (
            branch_grad,
            norms,
            *downs,
            slope,
            *ups,
            summed_grad,
            unit_one,
            recip_one,
            w_out,
            *contexts,
        ),
        (
            shape_of(F32, block, features),
            shape_of(BF16, features, features),
            shape_of(F32, 8, features),
            *[shape_of(BF16, width, block) for _ in range(4)],
        ),
        [
            pltpu.VMEM((block, 4 * units), BF16),
            pltpu.VMEM((block, features), BF16),
        ],
        20,
    )


def feed_weights_kernel(io, scalars, pre, grad_hidden, up_total, down_total):
    up, down = io.inputs[0], io.inputs[1]
    grad_up, grad_down = io.outputs
    units = up.shape[1]

    def into(at, j):
        n, b = io.inputs[2 + 2 * at], io.inputs[3 + 2 * at]
        columns = lane_slice(j * UNITS, UNITS)
        pre[at % 2, :, columns] = dot_nn(n[...], up[:, columns])
        grad_hidden[at % 2, :, columns] = dot_nt(b[...], down[row_block(j, UNITS), :])

    def out_of(at, j):
        n, b = io.inputs[2 + 2 * at], io.inputs[3 + 2 * at]
        columns = lane_slice(j * UNITS, UNITS)
        rows = row_block(j, UNITS)
        value, derivative = gelu_and_slope(pre[at % 2, :, columns])
        grad_pre = (derivative * grad_hidden[at % 2, :, columns]).astype(BF16)
        down_part = dot_tn(value.astype(BF16), b[...])
        up_part = dot_tn(grad_pre, n[...])
        if at == 0:
            down_total[rows, :] = down_part
            up_total[rows, :] = up_part
        elif at < 3:
            down_total[rows, :] += down_part
            up_total[rows, :] += up_part
        else:
            grad_down[rows, :] = (down_total[rows, :] + down_part).astype(BF16)
            grad_up[:, columns] = (up_total[rows, :] + up_part).T.astype(BF16)

    io.need(0, 1)
    for at in range(5):
        if at < 4:
            io.need(2 + 2 * at, 3 + 2 * at)

        @pl.loop(0, units // UNITS)
        def _(j):
            if at < 4:
                into(at, j)
            if at > 0:
                out_of(at - 1, j)


def feed_weights(scalars, normeds, branch_grads, up, down):
    features, units = up.shape
    block = normeds[0].shape[0]
    between = [a for pair in zip(normeds, branch_grads, strict=True) for a in pair]
    return local_call(
        feed_weights_kernel,
        "feed_weights",
        scalars,
        (up, down, *between),
        (shape_of(BF16, features, units), shape_of(BF16, units, features)),
        [
            pltpu.VMEM((2, block, units), F32),
            pltpu.VMEM((2, block, units), F32),
            pltpu.VMEM((units, features), F32),
            pltpu.VMEM((units, features), F32),
        ],
        25,
    )


def to_partner(array, axis, size, bit):
    return lax.ppermute(array, axis, [(i, i ^ bit) for i in range(size)])


def exchange_tensor(blocks):
    return (
        blocks[0],
        to_partner(blocks[1], "tensor", 4, 1),
        to_partner(blocks[2], "tensor", 4, 2),
        to_partner(blocks[3], "tensor", 4, 3),
    )


def make_bands(conv_weight):
    apart = (
        lax.broadcasted_iota(jnp.int32, (BAND_IN, BAND_OUT), 0)
        - PAD
        - lax.broadcasted_iota(jnp.int32, (BAND_IN, BAND_OUT), 1)
        + REACH
    )
    band = jnp.zeros((conv_weight.shape[0], BAND_IN, BAND_OUT), F32)
    for tap in range(KERNEL):
        band = jnp.where(apart[None] == tap, conv_weight[:, tap][:, None, None], band)
    return band.astype(BF16)


def after(array, *others):
    return lax.optimization_barrier((array, *others))[0]


def hop(arrays, axis, size, bit):
    columns = arrays[0].shape[-1]
    flat = [a.reshape(-1, columns) for a in arrays]
    got = to_partner(jnp.concatenate(flat, axis=0) if len(flat) > 1 else flat[0], axis, size, bit)
    parts, start = [], 0
    for array, rows in zip(arrays, flat, strict=True):
        parts.append(got[start : start + rows.shape[0]].reshape(array.shape))
        start += rows.shape[0]
    return parts


def is_upper(axis, bit):
    return (lax.axis_index(axis) & bit) != 0


def halve(array, axis, bit):
    rows = array.shape[-2] // 2
    low, high = array[..., :rows, :], array[..., rows:, :]
    upper = is_upper(axis, bit)
    return jnp.where(upper, high, low), jnp.where(upper, low, high)


def add(kept, got):
    return (kept.astype(F32) + got.astype(F32)).astype(kept.dtype)


def rejoin(array, got, axis, bit):
    upper = is_upper(axis, bit)
    return jnp.concatenate(
        [jnp.where(upper, got, array), jnp.where(upper, array, got)], axis=-2
    )


def solution(mesh):
    dp_size = mesh.shape["dp"]
    first, second, *others = [1 << b for b in range(dp_size.bit_length() - 1)]

    def dp_hop(arrays, bit):
        return hop(arrays, "dp", dp_size, bit)

    def shards(
        tokens,
        w_query,
        w_key,
        w_value,
        conv_weight,
        w_out,
        gain_one,
        shift_one,
        w_up,
        w_down,
        gain_two,
        shift_two,
        lengths,
        grad_output,
    ):
        width = w_query.shape[1]
        heads = width // HEAD
        features, units = w_up.shape
        me = lax.axis_index("tensor").astype(jnp.int32)
        scalars = jnp.concatenate([lengths[0], me[None]])
        w_t = jnp.concatenate([w_query.T, w_key.T, w_value.T], axis=0)
        bands = make_bands(conv_weight)
        norms = jnp.stack([gain_one, shift_one, gain_two, shift_two])
        tokens_two = to_partner(tokens, "tensor", 4, 2)
        tokens_one = to_partner(tokens, "tensor", 4, 1)
        weights = jnp.concatenate([w_up.T, w_down], axis=0)
        weights_one = to_partner(weights, "tensor", 4, 1)
        turn = lax.axis_index("dp") & 1
        half_units = units // 2
        weights_half = jnp.concatenate(
            [
                lax.dynamic_slice_in_dim(weights, start + turn * half_units, half_units, axis=0)
                for start in (0, units)
            ],
            axis=0,
        )
        tokens_two = after(tokens_two, bands, w_t, weights_half)
        blocks = (tokens, tokens_one, tokens_two, to_partner(tokens_two, "tensor", 4, 1))
        across = to_partner(after(weights_half, tokens_two), "tensor", 4, 2)

        attended = attend(scalars, blocks, w_t, bands)
        saved = (attended[0], *attended[5:])
        contexts = exchange_tensor(attended[1:5])
        across = after(across, attended[1])
        on = to_partner(across, "dp", dp_size, 1)
        normed_low, unit_one, recip_one = norm_in(scalars, contexts, tokens, w_out, norms)
        normed_two = to_partner(normed_low, "tensor", 4, 2)
        on = after(on, normed_low)

        def core_hop(array):
            return to_partner(array, "tensor", 4, 1)

        across_one, on_one = core_hop(across), core_hop(on)
        ups, downs = [
            (
                Joined((weights, which * units, units)),
                Joined((weights_one, which * units, units)),
                Joined(*[(a, which * half_units, half_units) for a in (across, on)]),
                Joined(*[(a, which * half_units, half_units) for a in (across_one, on_one)]),
            )
            for which in (0, 1)
        ]
        output, slope, summed_grad, branch_grad, norm_grads_two = feed(
            scalars, normed_low, unit_one, grad_output, norms, ups, downs
        )
        branch_two = to_partner(branch_grad, "tensor", 4, 2)
        branch_one = core_hop(branch_grad)
        normed_one = core_hop(normed_low)
        resid_grad, grad_w_out, norm_grads_one, *context_grads = feed_back(
            scalars,
            (slope, summed_grad, branch_grad),
            unit_one,
            recip_one,
            contexts,
            w_out,
            norms,
            ups,
            downs,
        )
        context_grads = exchange_tensor(context_grads)
        norm_rows = jnp.concatenate([norm_grads_one, norm_grads_two], axis=0)
        least = max(dp_size, 32)
        part = -(-(features + norm_rows.shape[0]) // (8 * least)) * least
        spare = jnp.zeros((8 * part - features - norm_rows.shape[0], features), BF16)
        small_kept, small_sent = halve(
            jnp.concatenate([grad_w_out, norm_rows.astype(BF16), spare], axis=0), "tensor", 1
        )
        small_got = core_hop(small_sent)
        normed_two, branch_two = after(normed_two, resid_grad), after(branch_two, resid_grad)
        normeds = (normed_low, normed_one, normed_two, core_hop(normed_two))
        branch_grads = (branch_grad, branch_one, branch_two, core_hop(branch_two))
        small = add(small_kept, after(small_got, branch_two))
        small_kept, small_sent = halve(small, "tensor", 2)
        small_got = to_partner(small_sent, "tensor", 4, 2)
        grad_up, grad_down = feed_weights(scalars, normeds, branch_grads, w_up, w_down)
        small = add(small_kept, after(small_got, grad_up))
        up = jnp.concatenate([grad_up, small[:part]], axis=0)
        down = jnp.concatenate([grad_down, small[part:]], axis=0)
        up_kept, up_sent = halve(up, "dp", first)
        down_kept, down_sent = halve(down, "dp", second)
        (up_got,), (down_got,) = dp_hop([up_sent], first), dp_hop([down_sent], second)
        context_grads = [after(context_grads[0], up_sent, down_sent), *context_grads[1:]]

        passed = attend_back(scalars, saved, context_grads, bands)
        up_kept, up_sent = halve(add(up_kept, after(up_got, passed[0])), "dp", second)
        down_kept, down_sent = halve(add(down_kept, after(down_got, passed[0])), "dp", first)
        (up_got,), (down_got,) = dp_hop([up_sent], second), dp_hop([down_sent], first)
        passed = [*passed[:6], after(passed[6], up_sent, down_sent)]
        shares = attend_steps(scalars, saved, passed)
        both = jnp.stack(
            [add(up_kept, after(up_got, shares)), add(down_kept, after(down_got, shares))]
        )
        kept, sent = halve(both, "dp", others[0])
        (got,) = dp_hop([sent], others[0])
        shares = after(shares, sent)
        low, high, *token_grads = attend_grads(
            scalars, passed, shares, blocks, w_t, max(dp_size, 16)
        )
        both = add(kept, after(got, low))
        for bit in others[1:]:
            kept, sent = halve(both, "dp", bit)
            (got,) = dp_hop([sent], bit)
            both = add(kept, got)
        low, high = after(low, both), after(high, both)
        both_got = dp_hop([both], others[-1])[0]
        low_kept, low_sent = halve(low, "dp", first)
        high_kept, high_sent = halve(high, "dp", second)
        (low_got,), (high_got,) = dp_hop([low_sent], first), dp_hop([high_sent], second)
        token_got = (core_hop(token_grads[3]), core_hop(token_grads[1]))
        away = add(token_grads[2], after(token_got[0], low_sent, high_sent))
        arrived = to_partner(away, "tensor", 4, 2)
        low_kept, low_sent = halve(add(low_kept, after(low_got, away)), "dp", second)
        high_kept, high_sent = halve(add(high_kept, after(high_got, away)), "dp", first)
        (low_got,), (high_got,) = dp_hop([low_sent], second), dp_hop([high_sent], first)
        both = rejoin(both, after(both_got, low_sent, high_sent), "dp", others[-1])
        for bit in reversed(others[:-1]):
            (got,) = dp_hop([both], bit)
            both = rejoin(both, got, "dp", bit)
        up, down = both[0], both[1]
        (up_got,), (down_got,) = dp_hop([up], second), dp_hop([down], first)
        wide = jnp.stack(
            [add(low_kept, after(low_got, both)), add(high_kept, after(high_got, both))]
        )
        for bit in others:
            (got,) = dp_hop([wide], bit)
            wide = add(wide, got)
        up = rejoin(up, after(up_got, wide), "dp", second)
        down = rejoin(down, after(down_got, wide), "dp", first)
        (up_got,), (down_got,) = dp_hop([up], first), dp_hop([down], second)
        wide = after(wide, up, down)
        low, high = wide[0], wide[1]
        (low_got,), (high_got,) = dp_hop([low], second), dp_hop([high], first)
        low, high = rejoin(low, low_got, "dp", second), rejoin(high, high_got, "dp", first)
        (low_got,), (high_got,) = dp_hop([low], first), dp_hop([high], second)
        up = rejoin(up, after(up_got, low), "dp", first)
        down = rejoin(down, after(down_got, low), "dp", second)
        small = jnp.concatenate([up[features:], down[units:]], axis=0)
        small = rejoin(small, to_partner(small, "tensor", 4, 2), "tensor", 2)
        small = rejoin(small, core_hop(small), "tensor", 1).astype(F32)
        here = token_grads[0].astype(F32) + token_got[1].astype(F32)
        grad_tokens = resid_grad + here + after(arrived, low_sent).astype(F32)
        qkv_wide = jnp.concatenate(
            [
                rejoin(low, low_got, "dp", first),
                rejoin(high, high_got, "dp", second),
            ],
            axis=0,
        ).astype(F32)
        grad_up, grad_down = up[:features].astype(F32), down[:units].astype(F32)
        return (
            output,
            grad_tokens,
            qkv_wide[:width].T,
            qkv_wide[width : 2 * width].T,
            qkv_wide[2 * width : 3 * width].T,
            qkv_wide[3 * width : 3 * width + heads, :KERNEL],
            small[:features],
            small[features],
            small[features + 1],
            grad_up,
            grad_down,
            small[features + 8],
            small[features + 9],
        )

    rows = P(("dp", "tensor"), None)
    columns = P(None, "tensor")
    in_specs = (
        rows,
        columns,
        columns,
        columns,
        P("tensor", None),
        P(),
        P(),
        P(),
        columns,
        P("tensor", None),
        P(),
        P(),
        P("dp", None),
        rows,
    )
    out_specs = (
        rows,
        rows,
        columns,
        columns,
        columns,
        P("tensor", None),
        P(),
        P(),
        P(),
        columns,
        P("tensor", None),
        P(),
        P(),
    )
    return jax.shard_map(shards, mesh=mesh, in_specs=in_specs, out_specs=out_specs, check_vma=False)
```

```python
import jax
import jax.numpy as jnp
from jax import lax
from jax.experimental import pallas as pl
from jax.experimental.pallas import tpu as pltpu
from jax.sharding import PartitionSpec as P

HEAD = 64
LANDMARKS = 64
NS_ITERS = 6
KERNEL = 33
SEQS = 3
MARKS = 192
REACH = KERNEL // 2
PAD = 128
BAND_IN = 512
BAND_OUT = 256
TILE = 640
AHEAD = 20
VMEM_LIMIT = 60 * 1024 * 1024
F32 = jnp.float32
BF16 = jnp.bfloat16


def dot_nn(a, b):
    return lax.dot_general(a, b, (((1,), (0,)), ((), ())), preferred_element_type=F32)


def dot_nt(a, b):
    return lax.dot_general(a, b, (((1,), (1,)), ((), ())), preferred_element_type=F32)


def dot_tn(a, b):
    return lax.dot_general(a, b, (((0,), (0,)), ((), ())), preferred_element_type=F32)


def split_low(a):
    high = a.astype(BF16)
    return (high, (a - high.astype(F32)).astype(BF16))


def dot_three(a, b, dot=dot_nn):
    a_high, a_low = a
    b_high, b_low = b
    return dot(a_high, b_high) + (dot(a_high, b_low) + dot(a_low, b_high))


def block_mask(dtype):
    rows = lax.broadcasted_iota(jnp.int32, (MARKS, MARKS), 0) // LANDMARKS
    columns = lax.broadcasted_iota(jnp.int32, (MARKS, MARKS), 1) // LANDMARKS
    return jnp.where(rows == columns, 1.0, 0.0).astype(dtype)


def spread(packed, mask):
    return jnp.concatenate([packed] * SEQS, axis=0) * mask


def spread_split(packed, mask):
    high, low = split_low(packed)
    return (spread(high, mask), spread(low, mask))


def fold(blocks):
    return (
        blocks[:LANDMARKS] + blocks[LANDMARKS : 2 * LANDMARKS] + blocks[2 * LANDMARKS :]
    )


def packed_identity():
    rows = lax.broadcasted_iota(jnp.int32, (LANDMARKS, MARKS), 0)
    columns = lax.broadcasted_iota(jnp.int32, (LANDMARKS, MARKS), 1) % LANDMARKS
    return jnp.where(rows == columns, 1.0, 0.0).astype(F32)


def sequence_of(places, first_end, second_end):
    return (places >= first_end).astype(jnp.int32) + (places >= second_end).astype(jnp.int32)


def lane_slice(start, width):
    return pl.ds(pl.multiple_of(start, 128), width)


def row_block(i, size):
    return pl.ds(pl.multiple_of(i * size, size), size)


class Layout:
    def __init__(self, scalars, group_size):
        self.first_end = scalars[0]
        self.second_end = scalars[0] + scalars[1]
        self.group_size = group_size
        self.tiles = group_size // TILE
        last = [
            (self.first_end - 1) // TILE,
            (self.second_end - 1) // TILE,
            self.tiles - 1,
        ]
        self.first_tile = [0, self.first_end // TILE, self.second_end // TILE]
        counts = [b - a + 1 for a, b in zip(self.first_tile, last, strict=True)]
        self.before = [0, counts[0], counts[0] + counts[1]]
        self.pairs = counts[0] + counts[1] + counts[2]

    def pick(self, sequence, values):
        return jnp.where(
            sequence == 0, values[0], jnp.where(sequence == 1, values[1], values[2])
        )

    def pair(self, p):
        sequence = (p >= self.before[1]).astype(jnp.int32) + (p >= self.before[2]).astype(
            jnp.int32
        )
        tile = p - self.pick(sequence, self.before) + self.pick(sequence, self.first_tile)
        start = self.pick(sequence, [0, self.first_end, self.second_end])
        end = self.pick(sequence, [self.first_end, self.second_end, self.group_size])
        return sequence, tile, start, end

    def own(self, tile, start, end):
        places = tile * TILE + lax.broadcasted_iota(jnp.int32, (LANDMARKS, TILE), 1)
        return (places >= start) & (places < end)

    def pool(self, tile, start, end):
        places = tile * TILE + lax.broadcasted_iota(jnp.int32, (1, TILE), 1)
        length = jnp.full((1, TILE), end - start, jnp.int32).astype(F32)
        numerator = ((places - start + 1) * LANDMARKS - 1).astype(F32) + length + 0.5
        segment = jnp.floor(numerator / length).astype(jnp.int32) - 1
        segment = jnp.where((places >= start) & (places < end), segment, -1)
        marks = lax.broadcasted_iota(jnp.int32, (LANDMARKS, TILE), 0)
        return jnp.where(marks == segment, 1.0, 0.0).astype(BF16)

    def counts(self):
        marks = lax.broadcasted_iota(jnp.int32, (MARKS, 1), 0)
        sequence = marks // LANDMARKS
        k = marks % LANDMARKS
        length = self.pick(
            sequence,
            [
                self.first_end,
                self.second_end - self.first_end,
                self.group_size - self.second_end,
            ],
        )
        upper = lax.shift_right_logical((k + 1) * length, 6)
        return (upper - lax.shift_right_logical(k * length, 6)).astype(F32)

    def same(self, start):
        into = start - PAD + lax.broadcasted_iota(jnp.int32, (BAND_IN, 1), 0)
        out = start + lax.broadcasted_iota(jnp.int32, (1, BAND_OUT), 1)
        return sequence_of(into, self.first_end, self.second_end) == sequence_of(
            out, self.first_end, self.second_end
        )


class Joined:
    def __init__(self, *pieces):
        self.pieces = pieces
        first = pieces[0][0]
        self.shape = (sum(rows for _, _, rows in pieces), first.shape[1])
        self.dtype = first.dtype

    def copies(self, sources, local):
        pairs, at = [], 0
        for source, (_, start, rows) in zip(sources, self.pieces, strict=True):
            pairs.append((source.at[start : start + rows, :], local.at[at : at + rows, :]))
            at += rows
        return pairs


class Io:
    def __init__(self, copies, inputs, outputs, targets, in_sems, out_sems):
        self.inputs, self.outputs = inputs, outputs
        self.arriving = [
            [
                pltpu.make_async_copy(source, local, in_sems.at[at])
                for source, local, at in group
            ]
            for group in copies
        ]
        self.leaving = [
            pltpu.make_async_copy(local, target, out_sems.at[i])
            for i, (local, target) in enumerate(zip(outputs, targets, strict=True))
        ]
        self.sent = set()
        self.started = 0
        self.waited = set()
        self.start_to(AHEAD)

    def start_to(self, end):
        for group in self.arriving[self.started : end]:
            for copy in group:
                copy.start()
        self.started = max(self.started, min(end, len(self.arriving)))

    def need(self, *which):
        self.start_to(max(which) + 1 + AHEAD)
        for i in which:
            if i not in self.waited:
                self.waited.add(i)
                for copy in self.arriving[i]:
                    copy.wait()
        return [self.inputs[i] for i in which]

    def send(self, *which):
        for i in which:
            self.sent.add(i)
            self.leaving[i].start()

    def close(self):
        self.need(*range(len(self.arriving)))
        self.send(*[i for i in range(len(self.leaving)) if i not in self.sent])
        for copy in self.leaving:
            copy.wait()


def local_call(kernel, name, scalars, operands, out_shape, scratch, gigaflops):
    anywhere = pl.BlockSpec(memory_space=pl.ANY)
    flat = [
        a
        for o in operands
        for a in ([piece[0] for piece in o.pieces] if isinstance(o, Joined) else [o])
    ]
    moved = sum(x.size * x.dtype.itemsize for x in (*flat, *out_shape))
    n_in, n_out, n_flat = len(operands), len(out_shape), len(flat)

    def body(scalar_ref, *refs):
        sources, refs = refs[:n_flat], refs[n_flat:]
        targets, refs = refs[:n_out], refs[n_out:]
        inputs, refs = refs[:n_in], refs[n_in:]
        outputs, refs = refs[:n_out], refs[n_out:]
        copies, at = [], 0
        for o, local in zip(operands, inputs, strict=True):
            count = len(o.pieces) if isinstance(o, Joined) else 1
            mine = sources[at : at + count]
            pairs = o.copies(mine, local) if isinstance(o, Joined) else [(mine[0], local)]
            copies.append([(a, b, at + i) for i, (a, b) in enumerate(pairs)])
            at += count
        io = Io(copies, inputs, outputs, targets, refs[0], refs[1])
        kernel(io, scalar_ref, *refs[2:])
        io.close()

    return pl.pallas_call(
        body,
        name=name,
        out_shape=out_shape,
        in_specs=[pl.BlockSpec(memory_space=pltpu.SMEM)] + [anywhere] * n_flat,
        out_specs=[anywhere] * n_out,
        scratch_shapes=[
            *[pltpu.VMEM(x.shape, x.dtype) for x in operands],
            *[pltpu.VMEM(x.shape, x.dtype) for x in out_shape],
            pltpu.SemaphoreType.DMA((n_flat,)),
            pltpu.SemaphoreType.DMA((n_out,)),
            *scratch,
        ],
        compiler_params=pltpu.CompilerParams(vmem_limit_bytes=VMEM_LIMIT),
        cost_estimate=pl.CostEstimate(
            flops=gigaflops * 1_000_000_000, bytes_accessed=moved, transcendentals=0
        ),
    )(scalars, *flat)


def shape_of(dtype, *shape):
    return jax.ShapeDtypeStruct(shape, dtype)


def wide(narrow):
    return jnp.concatenate([narrow] * (TILE // 128), axis=1)


def attend_kernel(
    io,
    scalars,
    context,
    scores,
    pooled,
    tops,
    totals,
    q_lands,
    k_lands,
    mvts,
):
    w_t, bands = io.inputs[0], io.inputs[5]
    qkv_t, c0, c1, c2, c3, land_out, mark_values_out, summary_out = io.outputs[:8]
    steps_out, among_out, inverse_out, lse_to, lse_from = io.outputs[8:]
    width = w_t.shape[0] // 3
    heads = width // HEAD
    block = io.inputs[1].shape[0]
    group_size = 4 * block
    layout = Layout(scalars, group_size)
    me = scalars[3]
    qk_scale = HEAD ** (-0.25)

    qkv_t[:, :PAD] = jnp.zeros((3 * width, PAD), BF16)
    qkv_t[:, PAD + group_size :] = jnp.zeros((3 * width, PAD), BF16)
    io.need(0)
    for at in range(4):
        x = io.need(1 + at)[0]
        lanes = lane_slice(PAD + (me ^ at) * block, block)
        qkv_t[: 2 * width, lanes] = (dot_nt(w_t[: 2 * width, :], x[...]) * qk_scale).astype(BF16)
        qkv_t[2 * width :, lanes] = dot_nt(w_t[2 * width :, :], x[...]).astype(BF16)
    io.send(0)

    pooled[...] = jnp.zeros_like(pooled)

    @pl.loop(0, layout.pairs)
    def _(p):
        sequence, tile, start, end = layout.pair(p)
        rows = row_block(sequence, LANDMARKS)
        pool = layout.pool(tile, start, end)
        pooled[rows, :] += dot_nt(pool, qkv_t[: 2 * width, lane_slice(PAD + tile * TILE, TILE)])

    pooled[...] = pooled[...] / layout.counts()
    land_t = pooled[...].T.astype(BF16)
    land_out[...] = land_t
    for h in range(heads):
        q_lands[h] = pooled[:, h * HEAD : (h + 1) * HEAD].astype(BF16)
        k_lands[h] = pooled[:, width + h * HEAD : width + (h + 1) * HEAD].astype(BF16)
    io.send(5)

    tops[...] = jnp.full(tops.shape, -1e30, F32)
    totals[...] = jnp.zeros_like(totals)
    summary_out[...] = jnp.zeros_like(summary_out)

    each = range(heads)

    def part_rows(part, h):
        return slice(part * width + h * HEAD, part * width + (h + 1) * HEAD)

    @pl.loop(0, layout.pairs)
    def _(p):
        sequence, tile, start, end = layout.pair(p)
        rows = row_block(sequence, LANDMARKS)
        own = layout.own(tile, start, end)
        padded = lane_slice(PAD + tile * TILE, TILE)
        raw = [dot_nn(q_lands[h, rows, :], qkv_t[part_rows(1, h), padded]) for h in each]
        masked = [jnp.where(own, raw[h], -1e30) for h in each]
        top = [tops[h, rows, :] for h in each]
        for lane in range(0, TILE, 128):
            top = [jnp.maximum(top[h], masked[h][:, lane : lane + 128]) for h in each]
        for h in each:
            scores[h, :, lane_slice(p * TILE, TILE)] = masked[h]
            tops[h, rows, :] = top[h]

    for h in range(heads):
        tops[h] = jnp.broadcast_to(jnp.max(tops[h], axis=1, keepdims=True), (MARKS, 128))

    @pl.loop(0, layout.pairs)
    def _(p):
        sequence, _, _, _ = layout.pair(p)
        rows = row_block(sequence, LANDMARKS)
        at = lane_slice(p * TILE, TILE)
        raised = [jnp.exp(scores[h, :, at] - wide(tops[h, rows, :])) for h in each]
        total = [totals[h, rows, :] for h in each]
        for lane in range(0, TILE, 128):
            total = [total[h] + raised[h][:, lane : lane + 128] for h in each]
        for h in each:
            scores[h, :, at] = raised[h]
            totals[h, rows, :] = total[h]

    for h in range(heads):
        total = jnp.broadcast_to(jnp.sum(totals[h], axis=1, keepdims=True), (MARKS, 128))
        lse_from[h] = tops[h] + jnp.log(total)
        totals[h] = 1.0 / total

    @pl.loop(0, layout.pairs)
    def _(p):
        sequence, tile, _, _ = layout.pair(p)
        rows = row_block(sequence, LANDMARKS)
        at = lane_slice(p * TILE, TILE)
        padded = lane_slice(PAD + tile * TILE, TILE)
        low = [(scores[h, :, at] * wide(totals[h, rows, :])).astype(BF16) for h in each]
        part = [dot_nt(low[h], qkv_t[part_rows(2, h), padded]) for h in each]
        part = [summary_out[h, rows, :] + part[h] for h in each]
        for h in each:
            summary_out[h, rows, :] = part[h]

    io.send(7, 12)
    mask_f = block_mask(F32)
    mask_b = block_mask(BF16)
    eye = packed_identity()
    amongs = []
    approxes = []
    for h in range(heads):
        raw = dot_nt(q_lands[h], k_lands[h])
        masked = jnp.where(mask_f > 0.0, raw, -1e30)
        row_top = jnp.max(masked, axis=1, keepdims=True)
        raised = jnp.exp(masked - row_top)
        among = raised / jnp.sum(raised, axis=1, keepdims=True)
        column_top = jnp.max(jnp.sum(among, axis=0, keepdims=True), axis=1, keepdims=True)
        packed = fold(among)
        among_out[h] = packed
        amongs.append(split_low(packed))
        approxes.append(fold(among.T) / column_top)

    for step in range(NS_ITERS):
        product = [
            dot_three(amongs[h], spread_split(approxes[h], mask_b)) for h in range(heads)
        ]
        split = [split_low(product[h]) for h in range(heads)]
        bracket = [7.0 * eye - product[h] for h in range(heads)]
        second = [
            15.0 * eye - dot_three(split[h], spread_split(bracket[h], mask_b))
            for h in range(heads)
        ]
        third = [
            13.0 * eye - dot_three(split[h], spread_split(second[h], mask_b))
            for h in range(heads)
        ]
        for h in range(heads):
            steps_out[h, 4 * step] = approxes[h]
            steps_out[h, 4 * step + 1] = product[h]
            steps_out[h, 4 * step + 2] = second[h]
            steps_out[h, 4 * step + 3] = third[h]
        approxes = [
            0.25 * dot_three(split_low(approxes[h]), spread_split(third[h], mask_b))
            for h in range(heads)
        ]

    for h in range(heads):
        inverse_out[h] = approxes[h]
        mark_values = dot_three(
            spread_split(approxes[h], mask_b), split_low(summary_out[h])
        )
        mark_values_out[h] = mark_values.astype(BF16)
        for s in range(SEQS):
            part = mark_values[s * LANDMARKS : (s + 1) * LANDMARKS, :]
            mvts[SEQS * h + s] = part.T.astype(BF16)
    io.send(6, 8, 9, 10)
    io.need(5)

    @pl.loop(0, group_size // BAND_OUT)
    def _(i):
        start = i * BAND_OUT
        same = jnp.where(layout.same(start), 1.0, 0.0).astype(BF16)
        smooth = [
            dot_nn(qkv_t[part_rows(2, h), lane_slice(start, BAND_IN)], bands[h] * same)
            for h in each
        ]
        for h in each:
            context[part_rows(0, h), lane_slice(start, BAND_OUT)] = smooth[h]

    @pl.loop(0, layout.pairs)
    def _(p):
        sequence, tile, start, end = layout.pair(p)
        rows = row_block(sequence, LANDMARKS)
        own = layout.own(tile, start, end)
        at = lane_slice(tile * TILE, TILE)
        padded = lane_slice(PAD + tile * TILE, TILE)
        raw = [dot_nn(k_lands[h, rows, :], qkv_t[part_rows(0, h), padded]) for h in each]
        top = [jnp.max(raw[h], axis=0, keepdims=True) for h in each]
        raised = [jnp.exp(raw[h] - top[h]) for h in each]
        total = [jnp.sum(raised[h], axis=0, keepdims=True) for h in each]
        low = [
            jnp.where(own, raised[h] * (1.0 / total[h]), 0.0).astype(BF16) for h in each
        ]
        blended = [dot_nn(mvts[SEQS * h + sequence], low[h]) for h in each]
        blended = [context[part_rows(0, h), at] + blended[h] for h in each]
        lse = [
            jnp.where(own[:1], top[h] + jnp.log(total[h]), lse_to[h : h + 1, at]) for h in each
        ]
        for h in each:
            lse_to[h : h + 1, at] = lse[h]
            context[part_rows(0, h), at] = blended[h]

    for at, out in enumerate((c0, c1, c2, c3)):
        out[...] = context[:, lane_slice((me ^ at) * block, block)].astype(BF16)


def attend(scalars, blocks, w_t, bands):
    block = blocks[0].shape[0]
    group_size = 4 * block
    width = w_t.shape[0] // 3
    heads = width // HEAD
    most_pairs = group_size // TILE + SEQS - 1
    return local_call(
        attend_kernel,
        "attend",
        scalars,
        (w_t, *blocks, bands),
        (
            shape_of(BF16, 3 * width, group_size + 2 * PAD),
            *[shape_of(BF16, width, block) for _ in range(4)],
            shape_of(BF16, 2 * width, MARKS),
            shape_of(BF16, heads, MARKS, HEAD),
            shape_of(F32, heads, MARKS, HEAD),
            shape_of(F32, heads, 4 * NS_ITERS, LANDMARKS, MARKS),
            shape_of(F32, heads, LANDMARKS, MARKS),
            shape_of(F32, heads, LANDMARKS, MARKS),
            shape_of(F32, heads, group_size),
            shape_of(F32, heads, MARKS, 128),
        ),
        [
            pltpu.VMEM((width, group_size), F32),
            pltpu.VMEM((heads, LANDMARKS, most_pairs * TILE), F32),
            pltpu.VMEM((MARKS, 2 * width), F32),
            pltpu.VMEM((heads, MARKS, 128), F32),
            pltpu.VMEM((heads, MARKS, 128), F32),
            pltpu.VMEM((heads, MARKS, HEAD), BF16),
            pltpu.VMEM((heads, MARKS, HEAD), BF16),
            pltpu.VMEM((SEQS * heads, HEAD, LANDMARKS), BF16),
        ],
        30,
    )


def attend_back_kernel(
    io,
    scalars,
    context_grad,
    partial_value,
    correlation,
    q_lands,
    k_lands,
    q_lands_t,
    k_lands_t,
    grad_summaries,
    grad_summaries_t,
    offsets,
):
    g_refs = io.inputs[:4]
    qkv_t, land_t, mark_values_in, summary_in = io.inputs[4:8]
    inverse_in, lse_to, lse_from = io.inputs[8:11]
    bands = io.inputs[11]
    grad_value, taps_out, partial_query, partial_key = io.outputs[:4]
    grad_q_land, grad_k_land, grad_mark = io.outputs[4:]
    width, block = g_refs[0].shape
    heads = width // HEAD
    group_size = 4 * block
    layout = Layout(scalars, group_size)
    me = scalars[3]
    each = range(heads)

    def part_rows(part, h):
        return slice(part * width + h * HEAD, part * width + (h + 1) * HEAD)

    io.need(*range(11))
    context_grad[:, :PAD] = jnp.zeros((width, PAD), BF16)
    context_grad[:, PAD + group_size :] = jnp.zeros((width, PAD), BF16)
    for at, g in enumerate(g_refs):
        context_grad[:, lane_slice(PAD + (me ^ at) * block, block)] = g[...]

    for h in range(heads):
        q_t = land_t[h * HEAD : (h + 1) * HEAD, :].astype(F32)
        k_t = land_t[width + h * HEAD : width + (h + 1) * HEAD, :].astype(F32)
        q_lands[h] = q_t.T.astype(BF16)
        k_lands[h] = k_t.T.astype(BF16)
        for s in range(SEQS):
            columns = slice(s * LANDMARKS, (s + 1) * LANDMARKS)
            q_lands_t[SEQS * h + s] = q_t[:, columns].astype(BF16)
            k_lands_t[SEQS * h + s] = k_t[:, columns].astype(BF16)

    for ref in (grad_k_land, grad_mark, grad_q_land, partial_query, partial_key, partial_value):
        ref[...] = jnp.zeros_like(ref)

    @pl.loop(0, layout.pairs)
    def _(p):
        sequence, tile, start, end = layout.pair(p)
        rows = row_block(sequence, LANDMARKS)
        own = layout.own(tile, start, end)
        at = lane_slice(tile * TILE, TILE)
        padded = lane_slice(PAD + tile * TILE, TILE)
        query = [qkv_t[part_rows(0, h), padded] for h in each]
        out_grad = [context_grad[part_rows(0, h), padded] for h in each]
        raw = [dot_nn(k_lands[h, rows, :], query[h]) for h in each]
        grad_to = [dot_nn(mark_values_in[h, rows, :], out_grad[h]) for h in each]
        probs = [
            jnp.exp(jnp.where(own, raw[h] - lse_to[h : h + 1, at], -1e30)) for h in each
        ]
        inner = [jnp.sum(grad_to[h] * probs[h], axis=0, keepdims=True) for h in each]
        grad_scores = [(probs[h] * (grad_to[h] - inner[h])).astype(BF16) for h in each]
        mark_part = [
            grad_mark[h, rows, :] + dot_nt(probs[h].astype(BF16), out_grad[h]) for h in each
        ]
        land_part = [
            grad_k_land[h, rows, :] + dot_nt(grad_scores[h], query[h]) for h in each
        ]
        query_part = [
            partial_query[part_rows(0, h), at]
            + dot_nn(k_lands_t[SEQS * h + sequence], grad_scores[h])
            for h in each
        ]
        for h in each:
            grad_mark[h, rows, :] = mark_part[h]
            grad_k_land[h, rows, :] = land_part[h]
            partial_query[part_rows(0, h), at] = query_part[h]

    io.send(2, 5, 6)
    mask_f = block_mask(F32)
    for h in range(heads):
        mark_split = split_low(grad_mark[h])
        summary = summary_in[h]
        inverse_blocks = spread(inverse_in[h], mask_f).T
        grad_summary = dot_three(split_low(inverse_blocks), mark_split)
        grad_low = grad_summary.astype(BF16)
        grad_summaries[h] = grad_low
        exact = grad_low.astype(F32)
        for s in range(SEQS):
            part = exact[s * LANDMARKS : (s + 1) * LANDMARKS, :]
            grad_summaries_t[SEQS * h + s] = part.T.astype(BF16)
        inner = jnp.sum(exact * summary, axis=1, keepdims=True)
        offsets[h] = jnp.broadcast_to(inner, (MARKS, 128))

    @pl.loop(0, layout.pairs)
    def _(p):
        sequence, tile, start, end = layout.pair(p)
        rows = row_block(sequence, LANDMARKS)
        own = layout.own(tile, start, end)
        at = lane_slice(tile * TILE, TILE)
        padded = lane_slice(PAD + tile * TILE, TILE)
        key = [qkv_t[part_rows(1, h), padded] for h in each]
        value = [qkv_t[part_rows(2, h), padded] for h in each]
        raw = [dot_nn(q_lands[h, rows, :], key[h]) for h in each]
        grad_from = [dot_nn(grad_summaries[h, rows, :], value[h]) for h in each]
        probs = [
            jnp.exp(jnp.where(own, raw[h] - wide(lse_from[h, rows, :]), -1e30)) for h in each
        ]
        grad_scores = [
            (probs[h] * (grad_from[h] - wide(offsets[h, rows, :]))).astype(BF16) for h in each
        ]
        value_part = [
            partial_value[part_rows(0, h), padded]
            + dot_nn(grad_summaries_t[SEQS * h + sequence], probs[h].astype(BF16))
            for h in each
        ]
        land_part = [grad_q_land[h, rows, :] + dot_nt(grad_scores[h], key[h]) for h in each]
        key_part = [
            partial_key[part_rows(0, h), at]
            + dot_nn(q_lands_t[SEQS * h + sequence], grad_scores[h])
            for h in each
        ]
        for h in each:
            partial_value[part_rows(0, h), padded] = value_part[h]
            grad_q_land[h, rows, :] = land_part[h]
            partial_key[part_rows(0, h), at] = key_part[h]

    io.send(3, 4)

    correlation[...] = jnp.zeros_like(correlation)
    io.need(11)

    @pl.loop(0, group_size // BAND_OUT)
    def _(i):
        start = i * BAND_OUT
        padded = lane_slice(PAD + start, BAND_OUT)
        around = lane_slice(start, BAND_IN)
        same = jnp.where(layout.same(start), 1.0, 0.0)
        same_b = same.astype(BF16)
        out_grad = [context_grad[part_rows(0, h), padded] for h in each]
        value_part = [
            partial_value[part_rows(0, h), around] + dot_nt(out_grad[h], bands[h] * same_b)
            for h in each
        ]
        across = [
            dot_tn(qkv_t[part_rows(2, h), around], out_grad[h]) * same for h in each
        ]
        parts = [
            (
                a[:128, :128] + a[128:256, 128:],
                a[128:256, :128] + a[256:384, 128:],
                a[256:384, :128] + a[384:, 128:],
            )
            for a in across
        ]
        for h in each:
            partial_value[part_rows(0, h), around] = value_part[h]
            for at in range(3):
                correlation[h, at] += parts[h][at]

    grad_value[...] = partial_value[:, PAD : PAD + group_size].astype(BF16)
    io.send(0)
    apart = lax.broadcasted_iota(jnp.int32, (128, 128), 0) - lax.broadcasted_iota(
        jnp.int32, (128, 128), 1
    )
    lanes = lax.broadcasted_iota(jnp.int32, (8, 128), 1)
    rows = lax.broadcasted_iota(jnp.int32, (8, 128), 0)
    taps = jnp.zeros((8, 128), F32)
    for h in range(heads):
        for tap in range(KERNEL):
            away = tap - REACH
            picked = jnp.where(apart == away, correlation[h, 1], 0.0)
            if away < 0:
                picked += jnp.where(apart == away + 128, correlation[h, 0], 0.0)
            if away > 0:
                picked += jnp.where(apart == away - 128, correlation[h, 2], 0.0)
            total = jnp.sum(
                jnp.sum(picked, axis=0, keepdims=True), axis=1, keepdims=True
            )
            taps = taps + jnp.where((lanes == tap) & (rows == h), total, 0.0)
    taps_out[...] = taps


def attend_steps_kernel(group_size, io, scalars):
    grad_mark_in, summary_in, among_in, steps_in = io.inputs[:4]
    land_t, grad_q_land, grad_k_land = io.inputs[4:]
    shares = io.outputs[0]
    heads = summary_in.shape[0]
    width = heads * HEAD
    layout = Layout(scalars, group_size)
    each = range(heads)
    mask_f = block_mask(F32)
    mask_b = block_mask(BF16)
    io.need(0, 1, 2)
    carried = [
        fold(dot_three(split_low(summary_in[h]), split_low(grad_mark_in[h]), dot_nt) * mask_f)
        for h in each
    ]
    io.need(*range(3, 7))
    eye = packed_identity()

    def spread_both(pair):
        return tuple(spread(a, mask_b) for a in pair)

    among_wide = [spread_split(among_in[h], mask_b) for h in each]
    among_grads = [jnp.zeros((LANDMARKS, MARKS), F32) for _ in each]
    for step in reversed(range(NS_ITERS)):
        approx = [split_low(steps_in[h, 4 * step]) for h in each]
        product = [steps_in[h, 4 * step + 1] for h in each]
        product_wide = [spread_split(product[h], mask_b) for h in each]
        grad = [split_low(carried[h]) for h in each]
        third = [
            split_low(0.25 * dot_three(grad[h], spread_both(approx[h]))) for h in each
        ]
        through = [
            dot_three(split_low(steps_in[h, 4 * step + 3]), spread_both(grad[h])) for h in each
        ]
        second = [split_low(-dot_three(third[h], product_wide[h])) for h in each]
        from_third = [
            dot_three(split_low(steps_in[h, 4 * step + 2]), spread_both(third[h]))
            for h in each
        ]
        first = [dot_three(second[h], product_wide[h]) for h in each]
        from_second = [
            dot_three(split_low(7.0 * eye - product[h]), spread_both(second[h])) for h in each
        ]
        grad_product = [
            split_low(first[h] - from_third[h] - from_second[h]) for h in each
        ]
        carried = [
            0.25 * through[h] + dot_three(grad_product[h], among_wide[h]) for h in each
        ]
        among_grads = [
            among_grads[h] + dot_three(approx[h], spread_both(grad_product[h])) for h in each
        ]

    for h in each:
        among = spread(among_in[h], mask_f)
        column_sums = jnp.sum(among, axis=0, keepdims=True)
        column_top = jnp.max(column_sums, axis=1, keepdims=True)
        start_grad = carried[h]
        start_blocks = spread(steps_in[h, 0], mask_f).T
        top_grad = -jnp.sum(
            jnp.sum(start_grad * fold(start_blocks), axis=1, keepdims=True),
            axis=0,
            keepdims=True,
        ) / column_top
        at_top = jnp.where(column_sums == column_top, 1.0, 0.0)
        shared = top_grad * at_top / jnp.sum(at_top, axis=1, keepdims=True)
        among_grad = spread(among_grads[h], mask_f).T + (
            spread(start_grad, mask_f) / column_top + shared * mask_f
        )
        inner = jnp.sum(among_grad * among, axis=1, keepdims=True)
        grad_scores = among * (among_grad - inner)
        high, low = split_low(grad_scores)
        back_high, back_low = split_low(grad_scores.T)
        q_land = land_t[h * HEAD : (h + 1) * HEAD, :].astype(F32).T.astype(BF16)
        k_land = land_t[width + h * HEAD : width + (h + 1) * HEAD, :].astype(F32).T.astype(BF16)
        q_total = grad_q_land[h] + (dot_nn(high, k_land) + dot_nn(low, k_land))
        k_total = grad_k_land[h] + (dot_nn(back_high, q_land) + dot_nn(back_low, q_land))
        counts = layout.counts()
        for which, total in enumerate((q_total, k_total)):
            share = total.astype(BF16).astype(F32) / counts
            for s in range(SEQS):
                part = share[s * LANDMARKS : (s + 1) * LANDMARKS, :].T
                shares[which, SEQS * h + s] = part.astype(BF16)


def attend_grads_kernel(io, scalars, grad_qkv, grad_w_t):
    grad_value, taps, partial_query, partial_key, shares, w_t = io.inputs[:6]
    x_refs = io.inputs[6:]
    low_out, high_out, d_refs = io.outputs[0], io.outputs[1], io.outputs[2:]
    width, group_size = partial_query.shape
    heads = width // HEAD
    block, features = x_refs[0].shape
    half = low_out.shape[0]
    me = scalars[3]
    qk_scale = HEAD ** (-0.25)
    layout = Layout(scalars, group_size)
    each = range(heads)

    def part_rows(part, h):
        return slice(part * width + h * HEAD, part * width + (h + 1) * HEAD)

    io.need(0, 2, 3, 4)

    @pl.loop(0, layout.pairs)
    def _(p):
        sequence, tile, start, end = layout.pair(p)
        at = lane_slice(tile * TILE, TILE)
        pool = layout.pool(tile, start, end)
        query = [
            partial_query[part_rows(0, h), at] + dot_nn(shares[0, SEQS * h + sequence], pool)
            for h in each
        ]
        key = [
            partial_key[part_rows(0, h), at] + dot_nn(shares[1, SEQS * h + sequence], pool)
            for h in each
        ]
        for h in each:
            partial_query[part_rows(0, h), at] = query[h]
            partial_key[part_rows(0, h), at] = key[h]

    grad_qkv[:width, :] = partial_query[...].astype(BF16)
    grad_qkv[width : 2 * width, :] = partial_key[...].astype(BF16)
    grad_qkv[2 * width :, :] = grad_value[...]

    io.need(1, 5)
    for at in (3, 1, 2, 0):
        x = io.need(6 + at)[0]
        lanes = lane_slice((me ^ at) * block, block)
        part = dot_nn(grad_qkv[:, lanes], x[...])
        if at == 3:
            grad_w_t[...] = part
        else:
            grad_w_t[...] += part

    def put(start, value):
        end = start + value.shape[0]
        if start < half:
            low_out[start : min(end, half), :] = value[: min(end, half) - start]
        if end > half:
            high_out[max(start, half) - half : end - half, :] = value[max(start, half) - start :]

    put(0, (grad_w_t[: 2 * width] * qk_scale).astype(BF16))
    put(2 * width, grad_w_t[2 * width :].astype(BF16))
    put(3 * width, jnp.zeros((2 * half - 3 * width, features), BF16))
    start = 3 * width - half
    high_out[start : start + 16, :128] = jnp.concatenate(
        [taps[...], jnp.zeros((8, 128), F32)], axis=0
    ).astype(BF16)
    io.send(0, 1)

    for at in (3, 1, 2, 0):
        d = d_refs[at]
        lanes = lane_slice((me ^ at) * block, block)
        scaled = dot_tn(grad_qkv[: 2 * width, lanes], w_t[: 2 * width, :])
        plain = dot_tn(grad_qkv[2 * width :, lanes], w_t[2 * width :, :])
        d[...] = (scaled * qk_scale + plain).astype(BF16)
        io.send(2 + at)


def attend_back(scalars, saved, grads, bands):
    qkv_t, land_t, mark_values, summary, steps, among, inverse, lse_to, lse_from = saved
    width, block = grads[0].shape
    group_size = 4 * block
    heads = width // HEAD
    lands = pltpu.VMEM((heads, MARKS, HEAD), BF16)
    lands_t = pltpu.VMEM((SEQS * heads, HEAD, LANDMARKS), BF16)
    return local_call(
        attend_back_kernel,
        "attend_back",
        scalars,
        (*grads, qkv_t, land_t, mark_values, summary, inverse, lse_to, lse_from, bands),
        (
            shape_of(BF16, width, group_size),
            shape_of(F32, 8, 128),
            shape_of(F32, width, group_size),
            shape_of(F32, width, group_size),
            *[shape_of(F32, heads, MARKS, HEAD) for _ in range(3)],
        ),
        [
            pltpu.VMEM((width, group_size + 2 * PAD), BF16),
            pltpu.VMEM((width, group_size + 2 * PAD), F32),
            pltpu.VMEM((heads, 3, 128, 128), F32),
            lands,
            lands,
            lands_t,
            lands_t,
            lands,
            lands_t,
            pltpu.VMEM((heads, MARKS, 128), F32),
        ],
        8,
    )


def attend_steps(scalars, saved, passed):
    qkv_t, land_t, mark_values, summary, steps, among, inverse, lse_to, lse_from = saved
    grad_q_land, grad_k_land, grad_mark = passed[4:]
    heads = summary.shape[0]

    def kernel(*refs):
        attend_steps_kernel(qkv_t.shape[1] - 2 * PAD, *refs)

    return local_call(
        kernel,
        "attend_steps",
        scalars,
        (grad_mark, summary, among, steps, land_t, grad_q_land, grad_k_land),
        (shape_of(BF16, 2, SEQS * heads, HEAD, LANDMARKS),),
        [],
        5,
    )[0]


def attend_grads(scalars, passed, shares, blocks, w_t, multiple):
    grad_value, taps, partial_query, partial_key = passed[:4]
    block, features = blocks[0].shape
    width, group_size = partial_query.shape
    heads = width // HEAD
    half = -(-(w_t.shape[0] + 16) // (2 * multiple)) * multiple
    return local_call(
        attend_grads_kernel,
        "attend_grads",
        scalars,
        (
            grad_value,
            taps,
            partial_query,
            partial_key,
            shares,
            w_t,
            *blocks,
        ),
        (
            shape_of(BF16, half, features),
            shape_of(BF16, half, features),
            *[shape_of(BF16, block, features) for _ in range(4)],
        ),
        [
            pltpu.VMEM((3 * width, group_size), BF16),
            pltpu.VMEM(w_t.shape, F32),
        ],
        8,
    )


def gelu_and_slope(values):
    z = jnp.abs(values) * 0.7071067811865476
    t = pl.reciprocal(1.0 + 0.3275911 * z)
    poly = t * 1.061405429 - 1.453152027
    for coefficient in (1.421413741, -0.284496736, 0.254829592):
        poly = poly * t + coefficient
    bell = jnp.exp(-z * z)
    half_tail = (0.5 * t) * poly * bell
    below = jnp.where(values >= 0.0, 1.0 - half_tail, half_tail)
    return values * below, below + values * (bell * 0.3989422804014327)


def unit_norm(values):
    row_mean = jnp.mean(values, axis=-1, keepdims=True)
    centered = values - row_mean
    spread_out = jnp.mean(centered * centered, axis=-1, keepdims=True)
    recip = lax.rsqrt(spread_out + 1e-05)
    return (centered * recip, recip)


def unit_back(grad, unit, recip):
    mean_grad = jnp.mean(grad, axis=-1, keepdims=True)
    mean_cross = jnp.mean(grad * unit, axis=-1, keepdims=True)
    return recip * (grad - mean_grad - unit * mean_cross)


ROWS = 320
UNITS = 768


def norm_in_kernel(io, scalars):
    contexts, (tokens, w_out, norms) = io.inputs[:4], io.inputs[4:]
    normed_out, unit_one, recip_one = io.outputs
    me = scalars[3]
    width, block = contexts[0].shape
    io.need(*range(7))

    resid = tokens[...].astype(F32)
    for at, c in enumerate(contexts):
        resid += dot_tn(c[...], w_out[row_block(me ^ at, width), :])
    unit, recip = unit_norm(resid)
    unit_one[...] = unit
    recip_one[...] = jnp.broadcast_to(recip, (block, 128))
    normed_out[...] = (unit * norms[0:1, :] + norms[1:2, :]).astype(BF16)


def feed_kernel(io, scalars, hidden):
    normed_low, norms = io.inputs[:2]
    ups, downs = io.inputs[2:6], io.inputs[6:10]
    unit_one, grad_output = io.inputs[10:]
    output, slope, summed_grad, branch_grad, norm_grads = io.outputs
    block, features = normed_low.shape
    units = ups[0].shape[0]
    norm_grads[...] = jnp.zeros_like(norm_grads)
    io.need(0, 1)

    for s, up in enumerate(ups):
        io.need(2 + s)

        @pl.loop(0, units // UNITS)
        def _(j):
            target = lane_slice(s * units + j * UNITS, UNITS)
            value, derivative = gelu_and_slope(
                dot_nt(normed_low[...], up[row_block(j, UNITS), :])
            )
            hidden[:, target] = value.astype(BF16)
            slope[:, target] = derivative.astype(BF16)

    io.send(1)
    io.need(*range(6, 12))

    @pl.loop(0, block // ROWS)
    def _(i):
        rows = row_block(i, ROWS)
        total = unit_one[rows, :] * norms[0:1, :] + norms[1:2, :]
        for s, down in enumerate(downs):
            total += dot_nn(hidden[rows, s * units : (s + 1) * units], down[...])
        unit, recip = unit_norm(total)
        output[rows, :] = unit * norms[2:3, :] + norms[3:4, :]
        top = grad_output[rows, :].astype(F32)
        norm_grads[0:1, :] += jnp.sum(top * unit, axis=0, keepdims=True)
        norm_grads[1:2, :] += jnp.sum(top, axis=0, keepdims=True)
        grad = unit_back(top * norms[2:3, :], unit, recip)
        summed_grad[rows, :] = grad
        branch_grad[rows, :] = grad.astype(BF16)


def feed_back_kernel(io, scalars, grad_pre, attended_grad):
    branch_grad, norms = io.inputs[:2]
    downs, slope = io.inputs[2:6], io.inputs[6]
    ups = io.inputs[7:11]
    summed_grad, unit_one, recip_one, w_out = io.inputs[11:15]
    contexts = io.inputs[15:19]
    resid_grad, grad_w_out, norm_grads = io.outputs[:3]
    targets = io.outputs[3:]
    me = scalars[3]
    width, block = contexts[0].shape
    units = ups[0].shape[0]
    norm_grads[...] = jnp.zeros_like(norm_grads)
    io.need(0, 1, 2, 6)

    for s, down in enumerate(downs):
        io.need(2 + s)

        @pl.loop(0, units // UNITS)
        def _(j):
            target = lane_slice(s * units + j * UNITS, UNITS)
            grad = dot_nt(branch_grad[...], down[row_block(j, UNITS), :])
            grad_pre[:, target] = (slope[:, target] * grad).astype(BF16)

    io.need(*range(7, 19))

    @pl.loop(0, block // ROWS)
    def _(i):
        rows = row_block(i, ROWS)
        total = summed_grad[rows, :]
        for s, up in enumerate(ups):
            total += dot_nn(grad_pre[rows, s * units : (s + 1) * units], up[...])
        unit = unit_one[rows, :]
        norm_grads[0:1, :] += jnp.sum(total * unit, axis=0, keepdims=True)
        norm_grads[1:2, :] += jnp.sum(total, axis=0, keepdims=True)
        grad = unit_back(total * norms[0:1, :], unit, recip_one[rows, :1])
        resid_grad[rows, :] = grad
        attended_grad[rows, :] = grad.astype(BF16)

    for at in (3, 2, 1, 0):
        rows = row_block(me ^ at, width)
        targets[at][...] = dot_nt(w_out[rows, :], attended_grad[...]).astype(BF16)
        io.send(3 + at)
    for at, c in enumerate(contexts):
        rows = row_block(me ^ at, width)
        grad_w_out[rows, :] = dot_nn(c[...], attended_grad[...]).astype(BF16)


def norm_in(scalars, contexts, tokens, w_out, norms):
    block, features = tokens.shape
    return local_call(
        norm_in_kernel,
        "norm_in",
        scalars,
        (*contexts, tokens, w_out, norms),
        (
            shape_of(BF16, block, features),
            shape_of(F32, block, features),
            shape_of(F32, block, 128),
        ),
        [],
        6,
    )


def feed(scalars, normed_low, unit_one, grad_output, norms, ups, downs):
    block, features = normed_low.shape
    units = ups[0].shape[0]
    return local_call(
        feed_kernel,
        "feed",
        scalars,
        (normed_low, norms, *ups, *downs, unit_one, grad_output),
        (
            shape_of(F32, block, features),
            shape_of(BF16, block, 4 * units),
            shape_of(F32, block, features),
            shape_of(BF16, block, features),
            shape_of(F32, 8, features),
        ),
        [pltpu.VMEM((block, 4 * units), BF16)],
        22,
    )


def feed_back(scalars, fed, unit_one, recip_one, contexts, w_out, norms, ups, downs):
    slope, summed_grad, branch_grad = fed
    width, block = contexts[0].shape
    features = w_out.shape[0]
    units = ups[0].shape[0]
    return local_call(
        feed_back_kernel,
        "feed_back",
        scalars,
        (
            branch_grad,
            norms,
            *downs,
            slope,
            *ups,
            summed_grad,
            unit_one,
            recip_one,
            w_out,
            *contexts,
        ),
        (
            shape_of(F32, block, features),
            shape_of(BF16, features, features),
            shape_of(F32, 8, features),
            *[shape_of(BF16, width, block) for _ in range(4)],
        ),
        [
            pltpu.VMEM((block, 4 * units), BF16),
            pltpu.VMEM((block, features), BF16),
        ],
        20,
    )


def feed_weights_kernel(io, scalars, pre, grad_hidden, up_total, down_total):
    up, down = io.inputs[0], io.inputs[1]
    grad_up, grad_down = io.outputs
    units = up.shape[1]

    def into(at, j):
        n, b = io.inputs[2 + 2 * at], io.inputs[3 + 2 * at]
        columns = lane_slice(j * UNITS, UNITS)
        pre[at % 2, :, columns] = dot_nn(n[...], up[:, columns])
        grad_hidden[at % 2, :, columns] = dot_nt(b[...], down[row_block(j, UNITS), :])

    def out_of(at, j):
        n, b = io.inputs[2 + 2 * at], io.inputs[3 + 2 * at]
        columns = lane_slice(j * UNITS, UNITS)
        rows = row_block(j, UNITS)
        value, derivative = gelu_and_slope(pre[at % 2, :, columns])
        grad_pre = (derivative * grad_hidden[at % 2, :, columns]).astype(BF16)
        down_part = dot_tn(value.astype(BF16), b[...])
        up_part = dot_tn(grad_pre, n[...])
        if at == 0:
            down_total[rows, :] = down_part
            up_total[rows, :] = up_part
        elif at < 3:
            down_total[rows, :] += down_part
            up_total[rows, :] += up_part
        else:
            grad_down[rows, :] = (down_total[rows, :] + down_part).astype(BF16)
            grad_up[:, columns] = (up_total[rows, :] + up_part).T.astype(BF16)

    io.need(0, 1)
    for at in range(5):
        if at < 4:
            io.need(2 + 2 * at, 3 + 2 * at)

        @pl.loop(0, units // UNITS)
        def _(j):
            if at < 4:
                into(at, j)
            if at > 0:
                out_of(at - 1, j)


def feed_weights(scalars, normeds, branch_grads, up, down):
    features, units = up.shape
    block = normeds[0].shape[0]
    between = [a for pair in zip(normeds, branch_grads, strict=True) for a in pair]
    return local_call(
        feed_weights_kernel,
        "feed_weights",
        scalars,
        (up, down, *between),
        (shape_of(BF16, features, units), shape_of(BF16, units, features)),
        [
            pltpu.VMEM((2, block, units), F32),
            pltpu.VMEM((2, block, units), F32),
            pltpu.VMEM((units, features), F32),
            pltpu.VMEM((units, features), F32),
        ],
        25,
    )


def to_partner(array, axis, size, bit):
    return lax.ppermute(array, axis, [(i, i ^ bit) for i in range(size)])


def exchange_tensor(blocks):
    return (
        blocks[0],
        to_partner(blocks[1], "tensor", 4, 1),
        to_partner(blocks[2], "tensor", 4, 2),
        to_partner(blocks[3], "tensor", 4, 3),
    )


def make_bands(conv_weight):
    apart = (
        lax.broadcasted_iota(jnp.int32, (BAND_IN, BAND_OUT), 0)
        - PAD
        - lax.broadcasted_iota(jnp.int32, (BAND_IN, BAND_OUT), 1)
        + REACH
    )
    band = jnp.zeros((conv_weight.shape[0], BAND_IN, BAND_OUT), F32)
    for tap in range(KERNEL):
        band = jnp.where(apart[None] == tap, conv_weight[:, tap][:, None, None], band)
    return band.astype(BF16)


def after(array, *others):
    return lax.optimization_barrier((array, *others))[0]


def hop(arrays, axis, size, bit):
    columns = arrays[0].shape[-1]
    flat = [a.reshape(-1, columns) for a in arrays]
    got = to_partner(jnp.concatenate(flat, axis=0) if len(flat) > 1 else flat[0], axis, size, bit)
    parts, start = [], 0
    for array, rows in zip(arrays, flat, strict=True):
        parts.append(got[start : start + rows.shape[0]].reshape(array.shape))
        start += rows.shape[0]
    return parts


def is_upper(axis, bit):
    return (lax.axis_index(axis) & bit) != 0


def halve(array, axis, bit):
    rows = array.shape[-2] // 2
    low, high = array[..., :rows, :], array[..., rows:, :]
    upper = is_upper(axis, bit)
    return jnp.where(upper, high, low), jnp.where(upper, low, high)


def add(kept, got):
    return (kept.astype(F32) + got.astype(F32)).astype(kept.dtype)


def rejoin(array, got, axis, bit):
    upper = is_upper(axis, bit)
    return jnp.concatenate(
        [jnp.where(upper, got, array), jnp.where(upper, array, got)], axis=-2
    )


def solution(mesh):
    dp_size = mesh.shape["dp"]
    first, second, *others = [1 << b for b in range(dp_size.bit_length() - 1)]

    def dp_hop(arrays, bit):
        return hop(arrays, "dp", dp_size, bit)

    def shards(
        tokens,
        w_query,
        w_key,
        w_value,
        conv_weight,
        w_out,
        gain_one,
        shift_one,
        w_up,
        w_down,
        gain_two,
        shift_two,
        lengths,
        grad_output,
    ):
        width = w_query.shape[1]
        heads = width // HEAD
        features, units = w_up.shape
        me = lax.axis_index("tensor").astype(jnp.int32)
        scalars = jnp.concatenate([lengths[0], me[None]])
        w_t = jnp.concatenate([w_query.T, w_key.T, w_value.T], axis=0)
        bands = make_bands(conv_weight)
        norms = jnp.stack([gain_one, shift_one, gain_two, shift_two])
        tokens_two = to_partner(tokens, "tensor", 4, 2)
        tokens_one = to_partner(tokens, "tensor", 4, 1)
        weights = jnp.concatenate([w_up.T, w_down], axis=0)
        weights_one = to_partner(weights, "tensor", 4, 1)
        turn = lax.axis_index("dp") & 1
        half_units = units // 2
        weights_half = jnp.concatenate(
            [
                lax.dynamic_slice_in_dim(weights, start + turn * half_units, half_units, axis=0)
                for start in (0, units)
            ],
            axis=0,
        )
        tokens_two = after(tokens_two, bands, w_t, weights_half, weights, norms)
        blocks = (tokens, tokens_one, tokens_two, to_partner(tokens_two, "tensor", 4, 1))
        across = to_partner(after(weights_half, tokens_two), "tensor", 4, 2)

        attended = attend(scalars, blocks, w_t, bands)
        saved = (attended[0], *attended[5:])
        contexts = exchange_tensor(attended[1:5])
        across = after(across, attended[1])
        on = to_partner(across, "dp", dp_size, 1)
        normed_low, unit_one, recip_one = norm_in(scalars, contexts, tokens, w_out, norms)
        normed_two = to_partner(normed_low, "tensor", 4, 2)
        on = after(on, normed_low)

        def core_hop(array):
            return to_partner(array, "tensor", 4, 1)

        across_one, on_one = core_hop(across), core_hop(on)
        ups, downs = [
            (
                Joined((weights, which * units, units)),
                Joined((weights_one, which * units, units)),
                Joined(*[(a, which * half_units, half_units) for a in (across, on)]),
                Joined(*[(a, which * half_units, half_units) for a in (across_one, on_one)]),
            )
            for which in (0, 1)
        ]
        output, slope, summed_grad, branch_grad, norm_grads_two = feed(
            scalars, normed_low, unit_one, grad_output, norms, ups, downs
        )
        branch_two = to_partner(branch_grad, "tensor", 4, 2)
        branch_one = core_hop(branch_grad)
        normed_one = core_hop(normed_low)
        resid_grad, grad_w_out, norm_grads_one, *context_grads = feed_back(
            scalars,
            (slope, summed_grad, branch_grad),
            unit_one,
            recip_one,
            contexts,
            w_out,
            norms,
            ups,
            downs,
        )
        context_grads = exchange_tensor(context_grads)
        norm_rows = jnp.concatenate([norm_grads_one, norm_grads_two], axis=0)
        least = max(dp_size, 32)
        part = -(-(features + norm_rows.shape[0]) // (8 * least)) * least
        spare = jnp.zeros((8 * part - features - norm_rows.shape[0], features), BF16)
        small_kept, small_sent = halve(
            jnp.concatenate([grad_w_out, norm_rows.astype(BF16), spare], axis=0), "tensor", 1
        )
        small_got = core_hop(small_sent)
        normed_two, branch_two = after(normed_two, resid_grad), after(branch_two, resid_grad)
        normeds = (normed_low, normed_one, normed_two, core_hop(normed_two))
        branch_grads = (branch_grad, branch_one, branch_two, core_hop(branch_two))
        small = add(small_kept, after(small_got, branch_two))
        small_kept, small_sent = halve(small, "tensor", 2)
        small_got = to_partner(small_sent, "tensor", 4, 2)
        grad_up, grad_down = feed_weights(scalars, normeds, branch_grads, w_up, w_down)
        small = add(small_kept, after(small_got, grad_up))

        def with_part(grad, rows):
            pieces = [a.reshape(dp_size, -1, features) for a in (grad, rows)]
            return jnp.concatenate(pieces, axis=1).reshape(-1, features)

        def without_part(array):
            pieces = array.reshape(-1, (units + part) // dp_size, features)
            cut = units // dp_size
            return [
                a.reshape(-1, features) for a in (pieces[:, :cut], pieces[:, cut:])
            ]

        up, down = with_part(grad_up, small[:part]), with_part(grad_down, small[part:])
        up_kept, up_sent = halve(up, "dp", first)
        down_kept, down_sent = halve(down, "dp", second)
        (up_got,), (down_got,) = dp_hop([up_sent], first), dp_hop([down_sent], second)
        context_grads = [after(context_grads[0], up_sent, down_sent), *context_grads[1:]]

        passed = attend_back(scalars, saved, context_grads, bands)
        up_kept, up_sent = halve(add(up_kept, after(up_got, passed[0])), "dp", second)
        down_kept, down_sent = halve(add(down_kept, after(down_got, passed[0])), "dp", first)
        (up_got,), (down_got,) = dp_hop([up_sent], second), dp_hop([down_sent], first)
        passed = [*passed[:6], after(passed[6], up_sent, down_sent)]
        shares = attend_steps(scalars, saved, passed)
        both = jnp.stack(
            [add(up_kept, after(up_got, shares)), add(down_kept, after(down_got, shares))]
        )
        kept, sent = halve(both, "dp", others[0])
        (got,) = dp_hop([sent], others[0])
        shares = after(shares, sent)
        low, high, *token_grads = attend_grads(
            scalars, passed, shares, blocks, w_t, max(dp_size, 16)
        )
        both = add(kept, after(got, low))
        for bit in others[1:]:
            kept, sent = halve(both, "dp", bit)
            (got,) = dp_hop([sent], bit)
            both = add(kept, got)
        low, high = after(low, both), after(high, both)
        both_got = dp_hop([both], others[-1])[0]
        low_kept, low_sent = halve(low, "dp", first)
        high_kept, high_sent = halve(high, "dp", second)
        (low_got,), (high_got,) = dp_hop([low_sent], first), dp_hop([high_sent], second)
        token_got = (core_hop(token_grads[3]), core_hop(token_grads[1]))
        away = add(token_grads[2], after(token_got[0], low_sent, high_sent))
        arrived = to_partner(away, "tensor", 4, 2)
        low_kept, low_sent = halve(add(low_kept, after(low_got, away)), "dp", second)
        high_kept, high_sent = halve(add(high_kept, after(high_got, away)), "dp", first)
        (low_got,), (high_got,) = dp_hop([low_sent], second), dp_hop([high_sent], first)
        both = rejoin(both, after(both_got, low_sent, high_sent), "dp", others[-1])
        for bit in reversed(others[:-1]):
            (got,) = dp_hop([both], bit)
            both = rejoin(both, got, "dp", bit)
        up, down = both[0], both[1]
        (up_got,), (down_got,) = dp_hop([up], second), dp_hop([down], first)
        wide = jnp.stack([add(low_kept, low_got), add(high_kept, high_got)])
        kept_wide = wide
        (wide_got,) = dp_hop([wide], others[0])
        up = rejoin(up, after(up_got, arrived), "dp", second)
        down = rejoin(down, down_got, "dp", first)
        (up, small_up), (down, small_down) = without_part(up), without_part(down)
        (up_got,), (down_got,) = dp_hop([up], first), dp_hop([down], second)
        wide = add(kept_wide, after(wide_got, up, down))
        for bit in others[1:]:
            (wide_got,) = dp_hop([wide], bit)
            wide = add(wide, wide_got)
        low, high = wide[0], wide[1]
        low_got, down_part_got = dp_hop([low, small_down], second)
        high_got, up_part_got = dp_hop([high, small_up], first)
        here = token_grads[0].astype(F32) + token_got[1].astype(F32)
        grad_tokens = resid_grad + here + after(arrived, low, high).astype(F32)
        small = jnp.concatenate(
            [
                rejoin(small_up, up_part_got, "dp", first),
                rejoin(small_down, down_part_got, "dp", second),
            ],
            axis=0,
        )
        small_got = to_partner(small, "tensor", 4, 2)
        low, high = rejoin(low, low_got, "dp", second), rejoin(high, high_got, "dp", first)
        (low_got,), (high_got,) = dp_hop([low], first), dp_hop([high], second)
        grad_up = rejoin(up, after(up_got, low), "dp", first).astype(F32)
        grad_down = rejoin(down, after(down_got, high), "dp", second).astype(F32)
        small = rejoin(small, after(small_got, low, high), "tensor", 2)
        small_got = core_hop(small)
        low_got, high_got = after(low_got, grad_up), after(high_got, grad_down)
        small = rejoin(small, small_got, "tensor", 1)
        grad_w_out = small[:features].astype(F32)
        norm_rows = small[features : features + 16].astype(F32)
        qkv_wide = jnp.concatenate(
            [
                rejoin(low, low_got, "dp", first),
                rejoin(high, high_got, "dp", second),
            ],
            axis=0,
        ).astype(F32)
        return (
            output,
            grad_tokens,
            qkv_wide[:width].T,
            qkv_wide[width : 2 * width].T,
            qkv_wide[2 * width : 3 * width].T,
            qkv_wide[3 * width : 3 * width + heads, :KERNEL],
            grad_w_out,
            norm_rows[0],
            norm_rows[1],
            grad_up,
            grad_down,
            norm_rows[8],
            norm_rows[9],
        )

    rows = P(("dp", "tensor"), None)
    columns = P(None, "tensor")
    in_specs = (
        rows,
        columns,
        columns,
        columns,
        P("tensor", None),
        P(),
        P(),
        P(),
        columns,
        P("tensor", None),
        P(),
        P(),
        P("dp", None),
        rows,
    )
    out_specs = (
        rows,
        rows,
        columns,
        columns,
        columns,
        P("tensor", None),
        P(),
        P(),
        P(),
        columns,
        P("tensor", None),
        P(),
        P(),
    )
    return jax.shard_map(shards, mesh=mesh, in_specs=in_specs, out_specs=out_specs, check_vma=False)
```

```python
import jax
import jax.numpy as jnp
from jax import lax
from jax.experimental import pallas as pl
from jax.experimental.pallas import tpu as pltpu
from jax.sharding import PartitionSpec as P

HEAD = 64
LANDMARKS = 64
NS_ITERS = 6
KERNEL = 33
SEQS = 3
MARKS = 192
REACH = KERNEL // 2
PAD = 128
BAND_IN = 512
BAND_OUT = 256
TILE = 640
AHEAD = 20
VMEM_LIMIT = 60 * 1024 * 1024
F32 = jnp.float32
BF16 = jnp.bfloat16


def dot_nn(a, b):
    return lax.dot_general(a, b, (((1,), (0,)), ((), ())), preferred_element_type=F32)


def dot_nt(a, b):
    return lax.dot_general(a, b, (((1,), (1,)), ((), ())), preferred_element_type=F32)


def dot_tn(a, b):
    return lax.dot_general(a, b, (((0,), (0,)), ((), ())), preferred_element_type=F32)


def split_low(a):
    high = a.astype(BF16)
    return (high, (a - high.astype(F32)).astype(BF16))


def dot_three(a, b, dot=dot_nn):
    a_high, a_low = a
    b_high, b_low = b
    return dot(a_high, b_high) + (dot(a_high, b_low) + dot(a_low, b_high))


def block_mask(dtype):
    rows = lax.broadcasted_iota(jnp.int32, (MARKS, MARKS), 0) // LANDMARKS
    columns = lax.broadcasted_iota(jnp.int32, (MARKS, MARKS), 1) // LANDMARKS
    return jnp.where(rows == columns, 1.0, 0.0).astype(dtype)


def spread(packed, mask):
    return jnp.concatenate([packed] * SEQS, axis=0) * mask


def spread_split(packed, mask):
    high, low = split_low(packed)
    return (spread(high, mask), spread(low, mask))


def fold(blocks):
    return (
        blocks[:LANDMARKS] + blocks[LANDMARKS : 2 * LANDMARKS] + blocks[2 * LANDMARKS :]
    )


def packed_identity():
    rows = lax.broadcasted_iota(jnp.int32, (LANDMARKS, MARKS), 0)
    columns = lax.broadcasted_iota(jnp.int32, (LANDMARKS, MARKS), 1) % LANDMARKS
    return jnp.where(rows == columns, 1.0, 0.0).astype(F32)


def sequence_of(places, first_end, second_end):
    return (places >= first_end).astype(jnp.int32) + (places >= second_end).astype(jnp.int32)


def lane_slice(start, width):
    return pl.ds(pl.multiple_of(start, 128), width)


def row_block(i, size):
    return pl.ds(pl.multiple_of(i * size, size), size)


class Layout:
    def __init__(self, scalars, group_size):
        self.first_end = scalars[0]
        self.second_end = scalars[0] + scalars[1]
        self.group_size = group_size
        self.tiles = group_size // TILE
        last = [
            (self.first_end - 1) // TILE,
            (self.second_end - 1) // TILE,
            self.tiles - 1,
        ]
        self.first_tile = [0, self.first_end // TILE, self.second_end // TILE]
        counts = [b - a + 1 for a, b in zip(self.first_tile, last, strict=True)]
        self.before = [0, counts[0], counts[0] + counts[1]]
        self.pairs = counts[0] + counts[1] + counts[2]

    def pick(self, sequence, values):
        return jnp.where(
            sequence == 0, values[0], jnp.where(sequence == 1, values[1], values[2])
        )

    def pair(self, p):
        sequence = (p >= self.before[1]).astype(jnp.int32) + (p >= self.before[2]).astype(
            jnp.int32
        )
        tile = p - self.pick(sequence, self.before) + self.pick(sequence, self.first_tile)
        start = self.pick(sequence, [0, self.first_end, self.second_end])
        end = self.pick(sequence, [self.first_end, self.second_end, self.group_size])
        return sequence, tile, start, end

    def own(self, tile, start, end):
        places = tile * TILE + lax.broadcasted_iota(jnp.int32, (LANDMARKS, TILE), 1)
        return (places >= start) & (places < end)

    def pool(self, tile, start, end):
        places = tile * TILE + lax.broadcasted_iota(jnp.int32, (1, TILE), 1)
        length = jnp.full((1, TILE), end - start, jnp.int32).astype(F32)
        numerator = ((places - start + 1) * LANDMARKS - 1).astype(F32) + length + 0.5
        segment = jnp.floor(numerator / length).astype(jnp.int32) - 1
        segment = jnp.where((places >= start) & (places < end), segment, -1)
        marks = lax.broadcasted_iota(jnp.int32, (LANDMARKS, TILE), 0)
        return jnp.where(marks == segment, 1.0, 0.0).astype(BF16)

    def counts(self):
        marks = lax.broadcasted_iota(jnp.int32, (MARKS, 1), 0)
        sequence = marks // LANDMARKS
        k = marks % LANDMARKS
        length = self.pick(
            sequence,
            [
                self.first_end,
                self.second_end - self.first_end,
                self.group_size - self.second_end,
            ],
        )
        upper = lax.shift_right_logical((k + 1) * length, 6)
        return (upper - lax.shift_right_logical(k * length, 6)).astype(F32)

    def same(self, start):
        into = start - PAD + lax.broadcasted_iota(jnp.int32, (BAND_IN, 1), 0)
        out = start + lax.broadcasted_iota(jnp.int32, (1, BAND_OUT), 1)
        return sequence_of(into, self.first_end, self.second_end) == sequence_of(
            out, self.first_end, self.second_end
        )


class Joined:
    def __init__(self, *pieces):
        self.pieces = pieces
        first = pieces[0][0]
        self.shape = (sum(rows for _, _, rows in pieces), first.shape[1])
        self.dtype = first.dtype

    def copies(self, sources, local):
        pairs, at = [], 0
        for source, (_, start, rows) in zip(sources, self.pieces, strict=True):
            pairs.append((source.at[start : start + rows, :], local.at[at : at + rows, :]))
            at += rows
        return pairs


class Io:
    def __init__(self, copies, inputs, outputs, targets, in_sems, out_sems):
        self.inputs, self.outputs = inputs, outputs
        self.arriving = [
            [
                pltpu.make_async_copy(source, local, in_sems.at[at])
                for source, local, at in group
            ]
            for group in copies
        ]
        self.leaving = [
            pltpu.make_async_copy(local, target, out_sems.at[i])
            for i, (local, target) in enumerate(zip(outputs, targets, strict=True))
        ]
        self.sent = set()
        self.started = 0
        self.waited = set()
        self.start_to(AHEAD)

    def start_to(self, end):
        for group in self.arriving[self.started : end]:
            for copy in group:
                copy.start()
        self.started = max(self.started, min(end, len(self.arriving)))

    def need(self, *which):
        self.start_to(max(which) + 1 + AHEAD)
        for i in which:
            if i not in self.waited:
                self.waited.add(i)
                for copy in self.arriving[i]:
                    copy.wait()
        return [self.inputs[i] for i in which]

    def send(self, *which):
        for i in which:
            self.sent.add(i)
            self.leaving[i].start()

    def close(self):
        self.need(*range(len(self.arriving)))
        self.send(*[i for i in range(len(self.leaving)) if i not in self.sent])
        for copy in self.leaving:
            copy.wait()


def local_call(kernel, name, scalars, operands, out_shape, scratch, gigaflops):
    anywhere = pl.BlockSpec(memory_space=pl.ANY)
    flat = [
        a
        for o in operands
        for a in ([piece[0] for piece in o.pieces] if isinstance(o, Joined) else [o])
    ]
    moved = sum(x.size * x.dtype.itemsize for x in (*flat, *out_shape))
    n_in, n_out, n_flat = len(operands), len(out_shape), len(flat)

    def body(scalar_ref, *refs):
        sources, refs = refs[:n_flat], refs[n_flat:]
        targets, refs = refs[:n_out], refs[n_out:]
        inputs, refs = refs[:n_in], refs[n_in:]
        outputs, refs = refs[:n_out], refs[n_out:]
        copies, at = [], 0
        for o, local in zip(operands, inputs, strict=True):
            count = len(o.pieces) if isinstance(o, Joined) else 1
            mine = sources[at : at + count]
            pairs = o.copies(mine, local) if isinstance(o, Joined) else [(mine[0], local)]
            copies.append([(a, b, at + i) for i, (a, b) in enumerate(pairs)])
            at += count
        io = Io(copies, inputs, outputs, targets, refs[0], refs[1])
        kernel(io, scalar_ref, *refs[2:])
        io.close()

    return pl.pallas_call(
        body,
        name=name,
        out_shape=out_shape,
        in_specs=[pl.BlockSpec(memory_space=pltpu.SMEM)] + [anywhere] * n_flat,
        out_specs=[anywhere] * n_out,
        scratch_shapes=[
            *[pltpu.VMEM(x.shape, x.dtype) for x in operands],
            *[pltpu.VMEM(x.shape, x.dtype) for x in out_shape],
            pltpu.SemaphoreType.DMA((n_flat,)),
            pltpu.SemaphoreType.DMA((n_out,)),
            *scratch,
        ],
        compiler_params=pltpu.CompilerParams(vmem_limit_bytes=VMEM_LIMIT),
        cost_estimate=pl.CostEstimate(
            flops=gigaflops * 1_000_000_000, bytes_accessed=moved, transcendentals=0
        ),
    )(scalars, *flat)


def shape_of(dtype, *shape):
    return jax.ShapeDtypeStruct(shape, dtype)


def wide(narrow):
    return jnp.concatenate([narrow] * (TILE // 128), axis=1)


def attend_kernel(
    io,
    scalars,
    context,
    scores,
    pooled,
    tops,
    totals,
    q_lands,
    k_lands,
    mvts,
):
    w_t, bands = io.inputs[0], io.inputs[5]
    qkv_t, c0, c1, c2, c3, land_out, mark_values_out, summary_out = io.outputs[:8]
    steps_out, among_out, inverse_out, lse_to, lse_from = io.outputs[8:]
    width = w_t.shape[0] // 3
    heads = width // HEAD
    block = io.inputs[1].shape[0]
    group_size = 4 * block
    layout = Layout(scalars, group_size)
    me = scalars[3]
    qk_scale = HEAD ** (-0.25)

    qkv_t[:, :PAD] = jnp.zeros((3 * width, PAD), BF16)
    qkv_t[:, PAD + group_size :] = jnp.zeros((3 * width, PAD), BF16)
    io.need(0)
    for at in range(4):
        x = io.need(1 + at)[0]
        lanes = lane_slice(PAD + (me ^ at) * block, block)
        qkv_t[: 2 * width, lanes] = (dot_nt(w_t[: 2 * width, :], x[...]) * qk_scale).astype(BF16)
        qkv_t[2 * width :, lanes] = dot_nt(w_t[2 * width :, :], x[...]).astype(BF16)
    io.send(0)

    pooled[...] = jnp.zeros_like(pooled)

    @pl.loop(0, layout.pairs)
    def _(p):
        sequence, tile, start, end = layout.pair(p)
        rows = row_block(sequence, LANDMARKS)
        pool = layout.pool(tile, start, end)
        pooled[rows, :] += dot_nt(pool, qkv_t[: 2 * width, lane_slice(PAD + tile * TILE, TILE)])

    pooled[...] = pooled[...] / layout.counts()
    land_t = pooled[...].T.astype(BF16)
    land_out[...] = land_t
    for h in range(heads):
        q_lands[h] = pooled[:, h * HEAD : (h + 1) * HEAD].astype(BF16)
        k_lands[h] = pooled[:, width + h * HEAD : width + (h + 1) * HEAD].astype(BF16)
    io.send(5)

    tops[...] = jnp.full(tops.shape, -1e30, F32)
    totals[...] = jnp.zeros_like(totals)
    summary_out[...] = jnp.zeros_like(summary_out)

    each = range(heads)

    def part_rows(part, h):
        return slice(part * width + h * HEAD, part * width + (h + 1) * HEAD)

    @pl.loop(0, layout.pairs)
    def _(p):
        sequence, tile, start, end = layout.pair(p)
        rows = row_block(sequence, LANDMARKS)
        own = layout.own(tile, start, end)
        padded = lane_slice(PAD + tile * TILE, TILE)
        raw = [dot_nn(q_lands[h, rows, :], qkv_t[part_rows(1, h), padded]) for h in each]
        masked = [jnp.where(own, raw[h], -1e30) for h in each]
        top = [tops[h, rows, :] for h in each]
        for lane in range(0, TILE, 128):
            top = [jnp.maximum(top[h], masked[h][:, lane : lane + 128]) for h in each]
        for h in each:
            scores[h, :, lane_slice(p * TILE, TILE)] = masked[h]
            tops[h, rows, :] = top[h]

    for h in range(heads):
        tops[h] = jnp.broadcast_to(jnp.max(tops[h], axis=1, keepdims=True), (MARKS, 128))

    @pl.loop(0, layout.pairs)
    def _(p):
        sequence, _, _, _ = layout.pair(p)
        rows = row_block(sequence, LANDMARKS)
        at = lane_slice(p * TILE, TILE)
        raised = [jnp.exp(scores[h, :, at] - wide(tops[h, rows, :])) for h in each]
        total = [totals[h, rows, :] for h in each]
        for lane in range(0, TILE, 128):
            total = [total[h] + raised[h][:, lane : lane + 128] for h in each]
        for h in each:
            scores[h, :, at] = raised[h]
            totals[h, rows, :] = total[h]

    for h in range(heads):
        total = jnp.broadcast_to(jnp.sum(totals[h], axis=1, keepdims=True), (MARKS, 128))
        lse_from[h] = tops[h] + jnp.log(total)
        totals[h] = 1.0 / total

    @pl.loop(0, layout.pairs)
    def _(p):
        sequence, tile, _, _ = layout.pair(p)
        rows = row_block(sequence, LANDMARKS)
        at = lane_slice(p * TILE, TILE)
        padded = lane_slice(PAD + tile * TILE, TILE)
        low = [(scores[h, :, at] * wide(totals[h, rows, :])).astype(BF16) for h in each]
        part = [dot_nt(low[h], qkv_t[part_rows(2, h), padded]) for h in each]
        part = [summary_out[h, rows, :] + part[h] for h in each]
        for h in each:
            summary_out[h, rows, :] = part[h]

    io.send(7, 12)
    mask_f = block_mask(F32)
    mask_b = block_mask(BF16)
    eye = packed_identity()
    amongs = []
    approxes = []
    for h in range(heads):
        raw = dot_nt(q_lands[h], k_lands[h])
        masked = jnp.where(mask_f > 0.0, raw, -1e30)
        row_top = jnp.max(masked, axis=1, keepdims=True)
        raised = jnp.exp(masked - row_top)
        among = raised / jnp.sum(raised, axis=1, keepdims=True)
        column_top = jnp.max(jnp.sum(among, axis=0, keepdims=True), axis=1, keepdims=True)
        packed = fold(among)
        among_out[h] = packed
        amongs.append(split_low(packed))
        approxes.append(fold(among.T) / column_top)

    io.need(5)

    def convolve(start):
        same = jnp.where(layout.same(start), 1.0, 0.0).astype(BF16)
        smooth = [
            dot_nn(qkv_t[part_rows(2, h), start : start + BAND_IN], bands[h] * same)
            for h in each
        ]
        for h in each:
            context[part_rows(0, h), start : start + BAND_OUT] = smooth[h]

    starts = list(range(0, group_size, BAND_OUT))
    for step in range(NS_ITERS):
        product = [
            dot_three(amongs[h], spread_split(approxes[h], mask_b)) for h in range(heads)
        ]
        split = [split_low(product[h]) for h in range(heads)]
        bracket = [7.0 * eye - product[h] for h in range(heads)]
        second = [
            15.0 * eye - dot_three(split[h], spread_split(bracket[h], mask_b))
            for h in range(heads)
        ]
        third = [
            13.0 * eye - dot_three(split[h], spread_split(second[h], mask_b))
            for h in range(heads)
        ]
        for start in starts[step::NS_ITERS]:
            convolve(start)
        for h in range(heads):
            steps_out[h, 4 * step] = approxes[h]
            steps_out[h, 4 * step + 1] = product[h]
            steps_out[h, 4 * step + 2] = second[h]
            steps_out[h, 4 * step + 3] = third[h]
        approxes = [
            0.25 * dot_three(split_low(approxes[h]), spread_split(third[h], mask_b))
            for h in range(heads)
        ]

    for h in range(heads):
        inverse_out[h] = approxes[h]
        mark_values = dot_three(
            spread_split(approxes[h], mask_b), split_low(summary_out[h])
        )
        mark_values_out[h] = mark_values.astype(BF16)
        for s in range(SEQS):
            part = mark_values[s * LANDMARKS : (s + 1) * LANDMARKS, :]
            mvts[SEQS * h + s] = part.T.astype(BF16)
    io.send(6, 8, 9, 10)
    @pl.loop(0, layout.pairs)
    def _(p):
        sequence, tile, start, end = layout.pair(p)
        rows = row_block(sequence, LANDMARKS)
        own = layout.own(tile, start, end)
        at = lane_slice(tile * TILE, TILE)
        padded = lane_slice(PAD + tile * TILE, TILE)
        raw = [dot_nn(k_lands[h, rows, :], qkv_t[part_rows(0, h), padded]) for h in each]
        top = [jnp.max(raw[h], axis=0, keepdims=True) for h in each]
        raised = [jnp.exp(raw[h] - top[h]) for h in each]
        total = [jnp.sum(raised[h], axis=0, keepdims=True) for h in each]
        low = [
            jnp.where(own, raised[h] * (1.0 / total[h]), 0.0).astype(BF16) for h in each
        ]
        blended = [dot_nn(mvts[SEQS * h + sequence], low[h]) for h in each]
        blended = [context[part_rows(0, h), at] + blended[h] for h in each]
        lse = [
            jnp.where(own[:1], top[h] + jnp.log(total[h]), lse_to[h : h + 1, at]) for h in each
        ]
        for h in each:
            lse_to[h : h + 1, at] = lse[h]
            context[part_rows(0, h), at] = blended[h]

    for at, out in enumerate((c0, c1, c2, c3)):
        out[...] = context[:, lane_slice((me ^ at) * block, block)].astype(BF16)


def attend(scalars, blocks, w_t, bands):
    block = blocks[0].shape[0]
    group_size = 4 * block
    width = w_t.shape[0] // 3
    heads = width // HEAD
    most_pairs = group_size // TILE + SEQS - 1
    return local_call(
        attend_kernel,
        "attend",
        scalars,
        (w_t, *blocks, bands),
        (
            shape_of(BF16, 3 * width, group_size + 2 * PAD),
            *[shape_of(BF16, width, block) for _ in range(4)],
            shape_of(BF16, 2 * width, MARKS),
            shape_of(BF16, heads, MARKS, HEAD),
            shape_of(F32, heads, MARKS, HEAD),
            shape_of(F32, heads, 4 * NS_ITERS, LANDMARKS, MARKS),
            shape_of(F32, heads, LANDMARKS, MARKS),
            shape_of(F32, heads, LANDMARKS, MARKS),
            shape_of(F32, heads, group_size),
            shape_of(F32, heads, MARKS, 128),
        ),
        [
            pltpu.VMEM((width, group_size), F32),
            pltpu.VMEM((heads, LANDMARKS, most_pairs * TILE), F32),
            pltpu.VMEM((MARKS, 2 * width), F32),
            pltpu.VMEM((heads, MARKS, 128), F32),
            pltpu.VMEM((heads, MARKS, 128), F32),
            pltpu.VMEM((heads, MARKS, HEAD), BF16),
            pltpu.VMEM((heads, MARKS, HEAD), BF16),
            pltpu.VMEM((SEQS * heads, HEAD, LANDMARKS), BF16),
        ],
        30,
    )


def attend_back_kernel(
    io,
    scalars,
    context_grad,
    partial_value,
    correlation,
    q_lands,
    k_lands,
    q_lands_t,
    k_lands_t,
    grad_summaries,
    grad_summaries_t,
    offsets,
):
    g_refs = io.inputs[:4]
    qkv_t, land_t, mark_values_in, summary_in = io.inputs[4:8]
    inverse_in, lse_to, lse_from = io.inputs[8:11]
    bands = io.inputs[11]
    grad_value, taps_out, partial_query, partial_key = io.outputs[:4]
    grad_q_land, grad_k_land, grad_mark = io.outputs[4:]
    width, block = g_refs[0].shape
    heads = width // HEAD
    group_size = 4 * block
    layout = Layout(scalars, group_size)
    me = scalars[3]
    each = range(heads)

    def part_rows(part, h):
        return slice(part * width + h * HEAD, part * width + (h + 1) * HEAD)

    io.need(*range(11))
    context_grad[:, :PAD] = jnp.zeros((width, PAD), BF16)
    context_grad[:, PAD + group_size :] = jnp.zeros((width, PAD), BF16)
    for at, g in enumerate(g_refs):
        context_grad[:, lane_slice(PAD + (me ^ at) * block, block)] = g[...]

    for h in range(heads):
        q_t = land_t[h * HEAD : (h + 1) * HEAD, :].astype(F32)
        k_t = land_t[width + h * HEAD : width + (h + 1) * HEAD, :].astype(F32)
        q_lands[h] = q_t.T.astype(BF16)
        k_lands[h] = k_t.T.astype(BF16)
        for s in range(SEQS):
            columns = slice(s * LANDMARKS, (s + 1) * LANDMARKS)
            q_lands_t[SEQS * h + s] = q_t[:, columns].astype(BF16)
            k_lands_t[SEQS * h + s] = k_t[:, columns].astype(BF16)

    for ref in (grad_k_land, grad_mark, grad_q_land, partial_query, partial_key, partial_value):
        ref[...] = jnp.zeros_like(ref)

    @pl.loop(0, layout.pairs)
    def _(p):
        sequence, tile, start, end = layout.pair(p)
        rows = row_block(sequence, LANDMARKS)
        own = layout.own(tile, start, end)
        at = lane_slice(tile * TILE, TILE)
        padded = lane_slice(PAD + tile * TILE, TILE)
        query = [qkv_t[part_rows(0, h), padded] for h in each]
        out_grad = [context_grad[part_rows(0, h), padded] for h in each]
        raw = [dot_nn(k_lands[h, rows, :], query[h]) for h in each]
        grad_to = [dot_nn(mark_values_in[h, rows, :], out_grad[h]) for h in each]
        probs = [
            jnp.exp(jnp.where(own, raw[h] - lse_to[h : h + 1, at], -1e30)) for h in each
        ]
        inner = [jnp.sum(grad_to[h] * probs[h], axis=0, keepdims=True) for h in each]
        grad_scores = [(probs[h] * (grad_to[h] - inner[h])).astype(BF16) for h in each]
        mark_part = [
            grad_mark[h, rows, :] + dot_nt(probs[h].astype(BF16), out_grad[h]) for h in each
        ]
        land_part = [
            grad_k_land[h, rows, :] + dot_nt(grad_scores[h], query[h]) for h in each
        ]
        query_part = [
            partial_query[part_rows(0, h), at]
            + dot_nn(k_lands_t[SEQS * h + sequence], grad_scores[h])
            for h in each
        ]
        for h in each:
            grad_mark[h, rows, :] = mark_part[h]
            grad_k_land[h, rows, :] = land_part[h]
            partial_query[part_rows(0, h), at] = query_part[h]

    io.send(2, 5, 6)
    mask_f = block_mask(F32)
    for h in range(heads):
        mark_split = split_low(grad_mark[h])
        summary = summary_in[h]
        inverse_blocks = spread(inverse_in[h], mask_f).T
        grad_summary = dot_three(split_low(inverse_blocks), mark_split)
        grad_low = grad_summary.astype(BF16)
        grad_summaries[h] = grad_low
        exact = grad_low.astype(F32)
        for s in range(SEQS):
            part = exact[s * LANDMARKS : (s + 1) * LANDMARKS, :]
            grad_summaries_t[SEQS * h + s] = part.T.astype(BF16)
        inner = jnp.sum(exact * summary, axis=1, keepdims=True)
        offsets[h] = jnp.broadcast_to(inner, (MARKS, 128))

    @pl.loop(0, layout.pairs)
    def _(p):
        sequence, tile, start, end = layout.pair(p)
        rows = row_block(sequence, LANDMARKS)
        own = layout.own(tile, start, end)
        at = lane_slice(tile * TILE, TILE)
        padded = lane_slice(PAD + tile * TILE, TILE)
        key = [qkv_t[part_rows(1, h), padded] for h in each]
        value = [qkv_t[part_rows(2, h), padded] for h in each]
        raw = [dot_nn(q_lands[h, rows, :], key[h]) for h in each]
        grad_from = [dot_nn(grad_summaries[h, rows, :], value[h]) for h in each]
        probs = [
            jnp.exp(jnp.where(own, raw[h] - wide(lse_from[h, rows, :]), -1e30)) for h in each
        ]
        grad_scores = [
            (probs[h] * (grad_from[h] - wide(offsets[h, rows, :]))).astype(BF16) for h in each
        ]
        value_part = [
            partial_value[part_rows(0, h), padded]
            + dot_nn(grad_summaries_t[SEQS * h + sequence], probs[h].astype(BF16))
            for h in each
        ]
        land_part = [grad_q_land[h, rows, :] + dot_nt(grad_scores[h], key[h]) for h in each]
        key_part = [
            partial_key[part_rows(0, h), at]
            + dot_nn(q_lands_t[SEQS * h + sequence], grad_scores[h])
            for h in each
        ]
        for h in each:
            partial_value[part_rows(0, h), padded] = value_part[h]
            grad_q_land[h, rows, :] = land_part[h]
            partial_key[part_rows(0, h), at] = key_part[h]

    io.send(3, 4)

    correlation[...] = jnp.zeros_like(correlation)
    io.need(11)

    @pl.loop(0, group_size // BAND_OUT)
    def _(i):
        start = i * BAND_OUT
        padded = lane_slice(PAD + start, BAND_OUT)
        around = lane_slice(start, BAND_IN)
        same = jnp.where(layout.same(start), 1.0, 0.0)
        same_b = same.astype(BF16)
        out_grad = [context_grad[part_rows(0, h), padded] for h in each]
        value_part = [
            partial_value[part_rows(0, h), around] + dot_nt(out_grad[h], bands[h] * same_b)
            for h in each
        ]
        across = [
            dot_tn(qkv_t[part_rows(2, h), around], out_grad[h]) * same for h in each
        ]
        parts = [
            (
                a[:128, :128] + a[128:256, 128:],
                a[128:256, :128] + a[256:384, 128:],
                a[256:384, :128] + a[384:, 128:],
            )
            for a in across
        ]
        for h in each:
            partial_value[part_rows(0, h), around] = value_part[h]
            for at in range(3):
                correlation[h, at] += parts[h][at]

    grad_value[...] = partial_value[:, PAD : PAD + group_size].astype(BF16)
    io.send(0)
    apart = lax.broadcasted_iota(jnp.int32, (128, 128), 0) - lax.broadcasted_iota(
        jnp.int32, (128, 128), 1
    )
    lanes = lax.broadcasted_iota(jnp.int32, (8, 128), 1)
    rows = lax.broadcasted_iota(jnp.int32, (8, 128), 0)
    taps = jnp.zeros((8, 128), F32)
    for h in range(heads):
        for tap in range(KERNEL):
            away = tap - REACH
            picked = jnp.where(apart == away, correlation[h, 1], 0.0)
            if away < 0:
                picked += jnp.where(apart == away + 128, correlation[h, 0], 0.0)
            if away > 0:
                picked += jnp.where(apart == away - 128, correlation[h, 2], 0.0)
            total = jnp.sum(
                jnp.sum(picked, axis=0, keepdims=True), axis=1, keepdims=True
            )
            taps = taps + jnp.where((lanes == tap) & (rows == h), total, 0.0)
    taps_out[...] = taps


def attend_steps_kernel(group_size, io, scalars):
    grad_mark_in, summary_in, among_in, steps_in = io.inputs[:4]
    land_t, grad_q_land, grad_k_land = io.inputs[4:]
    shares = io.outputs[0]
    heads = summary_in.shape[0]
    width = heads * HEAD
    layout = Layout(scalars, group_size)
    each = range(heads)
    mask_f = block_mask(F32)
    mask_b = block_mask(BF16)
    io.need(0, 1, 2)
    carried = [
        fold(dot_three(split_low(summary_in[h]), split_low(grad_mark_in[h]), dot_nt) * mask_f)
        for h in each
    ]
    io.need(*range(3, 7))
    eye = packed_identity()

    def spread_both(pair):
        return tuple(spread(a, mask_b) for a in pair)

    among_wide = [spread_split(among_in[h], mask_b) for h in each]
    among_grads = [jnp.zeros((LANDMARKS, MARKS), F32) for _ in each]
    for step in reversed(range(NS_ITERS)):
        approx = [split_low(steps_in[h, 4 * step]) for h in each]
        product = [steps_in[h, 4 * step + 1] for h in each]
        product_wide = [spread_split(product[h], mask_b) for h in each]
        grad = [split_low(carried[h]) for h in each]
        third = [
            split_low(0.25 * dot_three(grad[h], spread_both(approx[h]))) for h in each
        ]
        through = [
            dot_three(split_low(steps_in[h, 4 * step + 3]), spread_both(grad[h])) for h in each
        ]
        second = [split_low(-dot_three(third[h], product_wide[h])) for h in each]
        from_third = [
            dot_three(split_low(steps_in[h, 4 * step + 2]), spread_both(third[h]))
            for h in each
        ]
        first = [dot_three(second[h], product_wide[h]) for h in each]
        from_second = [
            dot_three(split_low(7.0 * eye - product[h]), spread_both(second[h])) for h in each
        ]
        grad_product = [
            split_low(first[h] - from_third[h] - from_second[h]) for h in each
        ]
        carried = [
            0.25 * through[h] + dot_three(grad_product[h], among_wide[h]) for h in each
        ]
        among_grads = [
            among_grads[h] + dot_three(approx[h], spread_both(grad_product[h])) for h in each
        ]

    for h in each:
        among = spread(among_in[h], mask_f)
        column_sums = jnp.sum(among, axis=0, keepdims=True)
        column_top = jnp.max(column_sums, axis=1, keepdims=True)
        start_grad = carried[h]
        start_blocks = spread(steps_in[h, 0], mask_f).T
        top_grad = -jnp.sum(
            jnp.sum(start_grad * fold(start_blocks), axis=1, keepdims=True),
            axis=0,
            keepdims=True,
        ) / column_top
        at_top = jnp.where(column_sums == column_top, 1.0, 0.0)
        shared = top_grad * at_top / jnp.sum(at_top, axis=1, keepdims=True)
        among_grad = spread(among_grads[h], mask_f).T + (
            spread(start_grad, mask_f) / column_top + shared * mask_f
        )
        inner = jnp.sum(among_grad * among, axis=1, keepdims=True)
        grad_scores = among * (among_grad - inner)
        high, low = split_low(grad_scores)
        back_high, back_low = split_low(grad_scores.T)
        q_land = land_t[h * HEAD : (h + 1) * HEAD, :].astype(F32).T.astype(BF16)
        k_land = land_t[width + h * HEAD : width + (h + 1) * HEAD, :].astype(F32).T.astype(BF16)
        q_total = grad_q_land[h] + (dot_nn(high, k_land) + dot_nn(low, k_land))
        k_total = grad_k_land[h] + (dot_nn(back_high, q_land) + dot_nn(back_low, q_land))
        counts = layout.counts()
        for which, total in enumerate((q_total, k_total)):
            share = total.astype(BF16).astype(F32) / counts
            for s in range(SEQS):
                part = share[s * LANDMARKS : (s + 1) * LANDMARKS, :].T
                shares[which, SEQS * h + s] = part.astype(BF16)


def attend_grads_kernel(io, scalars, grad_qkv, grad_w_t):
    grad_value, taps, partial_query, partial_key, shares, w_t = io.inputs[:6]
    x_refs = io.inputs[6:]
    low_out, high_out, d_refs = io.outputs[0], io.outputs[1], io.outputs[2:]
    width, group_size = partial_query.shape
    heads = width // HEAD
    block, features = x_refs[0].shape
    half = low_out.shape[0]
    me = scalars[3]
    qk_scale = HEAD ** (-0.25)
    layout = Layout(scalars, group_size)
    each = range(heads)

    def part_rows(part, h):
        return slice(part * width + h * HEAD, part * width + (h + 1) * HEAD)

    io.need(0, 2, 3, 4)

    @pl.loop(0, layout.pairs)
    def _(p):
        sequence, tile, start, end = layout.pair(p)
        at = lane_slice(tile * TILE, TILE)
        pool = layout.pool(tile, start, end)
        query = [
            partial_query[part_rows(0, h), at] + dot_nn(shares[0, SEQS * h + sequence], pool)
            for h in each
        ]
        key = [
            partial_key[part_rows(0, h), at] + dot_nn(shares[1, SEQS * h + sequence], pool)
            for h in each
        ]
        for h in each:
            partial_query[part_rows(0, h), at] = query[h]
            partial_key[part_rows(0, h), at] = key[h]

    grad_qkv[:width, :] = partial_query[...].astype(BF16)
    grad_qkv[width : 2 * width, :] = partial_key[...].astype(BF16)
    grad_qkv[2 * width :, :] = grad_value[...]

    io.need(1, 5)
    for at in (3, 1, 2, 0):
        x = io.need(6 + at)[0]
        lanes = lane_slice((me ^ at) * block, block)
        part = dot_nn(grad_qkv[:, lanes], x[...])
        if at == 3:
            grad_w_t[...] = part
        else:
            grad_w_t[...] += part

    def put(start, value):
        end = start + value.shape[0]
        if start < half:
            low_out[start : min(end, half), :] = value[: min(end, half) - start]
        if end > half:
            high_out[max(start, half) - half : end - half, :] = value[max(start, half) - start :]

    put(0, (grad_w_t[: 2 * width] * qk_scale).astype(BF16))
    put(2 * width, grad_w_t[2 * width :].astype(BF16))
    put(3 * width, jnp.zeros((2 * half - 3 * width, features), BF16))
    start = 3 * width - half
    high_out[start : start + 16, :128] = jnp.concatenate(
        [taps[...], jnp.zeros((8, 128), F32)], axis=0
    ).astype(BF16)
    io.send(0, 1)

    for at in (3, 1, 2, 0):
        d = d_refs[at]
        lanes = lane_slice((me ^ at) * block, block)
        scaled = dot_tn(grad_qkv[: 2 * width, lanes], w_t[: 2 * width, :])
        plain = dot_tn(grad_qkv[2 * width :, lanes], w_t[2 * width :, :])
        d[...] = (scaled * qk_scale + plain).astype(BF16)
        io.send(2 + at)


def attend_back(scalars, saved, grads, bands):
    qkv_t, land_t, mark_values, summary, steps, among, inverse, lse_to, lse_from = saved
    width, block = grads[0].shape
    group_size = 4 * block
    heads = width // HEAD
    lands = pltpu.VMEM((heads, MARKS, HEAD), BF16)
    lands_t = pltpu.VMEM((SEQS * heads, HEAD, LANDMARKS), BF16)
    return local_call(
        attend_back_kernel,
        "attend_back",
        scalars,
        (*grads, qkv_t, land_t, mark_values, summary, inverse, lse_to, lse_from, bands),
        (
            shape_of(BF16, width, group_size),
            shape_of(F32, 8, 128),
            shape_of(F32, width, group_size),
            shape_of(F32, width, group_size),
            *[shape_of(F32, heads, MARKS, HEAD) for _ in range(3)],
        ),
        [
            pltpu.VMEM((width, group_size + 2 * PAD), BF16),
            pltpu.VMEM((width, group_size + 2 * PAD), F32),
            pltpu.VMEM((heads, 3, 128, 128), F32),
            lands,
            lands,
            lands_t,
            lands_t,
            lands,
            lands_t,
            pltpu.VMEM((heads, MARKS, 128), F32),
        ],
        8,
    )


def attend_steps(scalars, saved, passed):
    qkv_t, land_t, mark_values, summary, steps, among, inverse, lse_to, lse_from = saved
    grad_q_land, grad_k_land, grad_mark = passed[4:]
    heads = summary.shape[0]

    def kernel(*refs):
        attend_steps_kernel(qkv_t.shape[1] - 2 * PAD, *refs)

    return local_call(
        kernel,
        "attend_steps",
        scalars,
        (grad_mark, summary, among, steps, land_t, grad_q_land, grad_k_land),
        (shape_of(BF16, 2, SEQS * heads, HEAD, LANDMARKS),),
        [],
        5,
    )[0]


def attend_grads(scalars, passed, shares, blocks, w_t, multiple):
    grad_value, taps, partial_query, partial_key = passed[:4]
    block, features = blocks[0].shape
    width, group_size = partial_query.shape
    heads = width // HEAD
    half = -(-(w_t.shape[0] + 16) // (2 * multiple)) * multiple
    return local_call(
        attend_grads_kernel,
        "attend_grads",
        scalars,
        (
            grad_value,
            taps,
            partial_query,
            partial_key,
            shares,
            w_t,
            *blocks,
        ),
        (
            shape_of(BF16, half, features),
            shape_of(BF16, half, features),
            *[shape_of(BF16, block, features) for _ in range(4)],
        ),
        [
            pltpu.VMEM((3 * width, group_size), BF16),
            pltpu.VMEM(w_t.shape, F32),
        ],
        8,
    )


def gelu_and_slope(values):
    z = jnp.abs(values) * 0.7071067811865476
    t = pl.reciprocal(1.0 + 0.3275911 * z)
    poly = t * 1.061405429 - 1.453152027
    for coefficient in (1.421413741, -0.284496736, 0.254829592):
        poly = poly * t + coefficient
    bell = jnp.exp(-z * z)
    half_tail = (0.5 * t) * poly * bell
    below = jnp.where(values >= 0.0, 1.0 - half_tail, half_tail)
    return values * below, below + values * (bell * 0.3989422804014327)


def unit_norm(values):
    row_mean = jnp.mean(values, axis=-1, keepdims=True)
    centered = values - row_mean
    spread_out = jnp.mean(centered * centered, axis=-1, keepdims=True)
    recip = lax.rsqrt(spread_out + 1e-05)
    return (centered * recip, recip)


def unit_back(grad, unit, recip):
    mean_grad = jnp.mean(grad, axis=-1, keepdims=True)
    mean_cross = jnp.mean(grad * unit, axis=-1, keepdims=True)
    return recip * (grad - mean_grad - unit * mean_cross)


ROWS = 320
UNITS = 768
PART = 768


def norm_in_kernel(io, scalars):
    contexts, (tokens, w_out, norms) = io.inputs[:4], io.inputs[4:]
    normed_out, unit_one, recip_one = io.outputs
    me = scalars[3]
    width, block = contexts[0].shape
    io.need(*range(7))

    resid = tokens[...].astype(F32)
    for at, c in enumerate(contexts):
        resid += dot_tn(c[...], w_out[row_block(me ^ at, width), :])
    unit, recip = unit_norm(resid)
    unit_one[...] = unit
    recip_one[...] = jnp.broadcast_to(recip, (block, 128))
    normed_out[...] = (unit * norms[0:1, :] + norms[1:2, :]).astype(BF16)


def feed_kernel(io, scalars, hidden):
    normed_low, norms = io.inputs[:2]
    ups, downs = io.inputs[2:6], io.inputs[6:10]
    unit_one, grad_output = io.inputs[10:]
    output, slope, summed_grad, branch_grad, norm_grads = io.outputs
    block, features = normed_low.shape
    units = ups[0].shape[0]
    norm_grads[...] = jnp.zeros_like(norm_grads)
    io.need(0, 1)

    for s, up in enumerate(ups):
        io.need(2 + s)

        @pl.loop(0, units // UNITS)
        def _(j):
            target = lane_slice(s * units + j * UNITS, UNITS)
            value, derivative = gelu_and_slope(
                dot_nt(normed_low[...], up[row_block(j, UNITS), :])
            )
            hidden[:, target] = value.astype(BF16)
            slope[:, target] = derivative.astype(BF16)

    io.send(1)
    io.need(*range(6, 12))

    @pl.loop(0, block // ROWS)
    def _(i):
        rows = row_block(i, ROWS)
        total = unit_one[rows, :] * norms[0:1, :] + norms[1:2, :]
        for s, down in enumerate(downs):
            total += dot_nn(hidden[rows, s * units : (s + 1) * units], down[...])
        unit, recip = unit_norm(total)
        output[rows, :] = unit * norms[2:3, :] + norms[3:4, :]
        top = grad_output[rows, :].astype(F32)
        norm_grads[0:1, :] += jnp.sum(top * unit, axis=0, keepdims=True)
        norm_grads[1:2, :] += jnp.sum(top, axis=0, keepdims=True)
        grad = unit_back(top * norms[2:3, :], unit, recip)
        summed_grad[rows, :] = grad
        branch_grad[rows, :] = grad.astype(BF16)


def feed_back_kernel(io, scalars, grad_pre, attended_grad):
    branch_grad, norms = io.inputs[:2]
    downs, slope = io.inputs[2:6], io.inputs[6]
    ups = io.inputs[7:11]
    summed_grad, unit_one, recip_one, w_out = io.inputs[11:15]
    contexts = io.inputs[15:19]
    resid_grad, grad_w_out, norm_grads = io.outputs[:3]
    targets = io.outputs[3:]
    me = scalars[3]
    width, block = contexts[0].shape
    units = ups[0].shape[0]
    norm_grads[...] = jnp.zeros_like(norm_grads)
    io.need(0, 1, 2, 6)

    for s, down in enumerate(downs):
        io.need(2 + s)

        @pl.loop(0, units // UNITS)
        def _(j):
            target = lane_slice(s * units + j * UNITS, UNITS)
            grad = dot_nt(branch_grad[...], down[row_block(j, UNITS), :])
            grad_pre[:, target] = (slope[:, target] * grad).astype(BF16)

    io.need(*range(7, 19))

    @pl.loop(0, block // ROWS)
    def _(i):
        rows = row_block(i, ROWS)
        total = summed_grad[rows, :]
        for s, up in enumerate(ups):
            total += dot_nn(grad_pre[rows, s * units : (s + 1) * units], up[...])
        unit = unit_one[rows, :]
        norm_grads[0:1, :] += jnp.sum(total * unit, axis=0, keepdims=True)
        norm_grads[1:2, :] += jnp.sum(total, axis=0, keepdims=True)
        grad = unit_back(total * norms[0:1, :], unit, recip_one[rows, :1])
        resid_grad[rows, :] = grad
        attended_grad[rows, :] = grad.astype(BF16)

    for at in (3, 2, 1, 0):
        rows = row_block(me ^ at, width)
        targets[at][...] = dot_nt(w_out[rows, :], attended_grad[...]).astype(BF16)
        io.send(3 + at)
    for at, c in enumerate(contexts):
        rows = row_block(me ^ at, width)
        grad_w_out[rows, :] = dot_nn(c[...], attended_grad[...]).astype(BF16)


def norm_in(scalars, contexts, tokens, w_out, norms):
    block, features = tokens.shape
    return local_call(
        norm_in_kernel,
        "norm_in",
        scalars,
        (*contexts, tokens, w_out, norms),
        (
            shape_of(BF16, block, features),
            shape_of(F32, block, features),
            shape_of(F32, block, 128),
        ),
        [],
        6,
    )


def feed(scalars, normed_low, unit_one, grad_output, norms, ups, downs):
    block, features = normed_low.shape
    units = ups[0].shape[0]
    return local_call(
        feed_kernel,
        "feed",
        scalars,
        (normed_low, norms, *ups, *downs, unit_one, grad_output),
        (
            shape_of(F32, block, features),
            shape_of(BF16, block, 4 * units),
            shape_of(F32, block, features),
            shape_of(BF16, block, features),
            shape_of(F32, 8, features),
        ),
        [pltpu.VMEM((block, 4 * units), BF16)],
        22,
    )


def feed_back(scalars, fed, unit_one, recip_one, contexts, w_out, norms, ups, downs):
    slope, summed_grad, branch_grad = fed
    width, block = contexts[0].shape
    features = w_out.shape[0]
    units = ups[0].shape[0]
    return local_call(
        feed_back_kernel,
        "feed_back",
        scalars,
        (
            branch_grad,
            norms,
            *downs,
            slope,
            *ups,
            summed_grad,
            unit_one,
            recip_one,
            w_out,
            *contexts,
        ),
        (
            shape_of(F32, block, features),
            shape_of(BF16, features, features),
            shape_of(F32, 8, features),
            *[shape_of(BF16, width, block) for _ in range(4)],
        ),
        [
            pltpu.VMEM((block, 4 * units), BF16),
            pltpu.VMEM((block, features), BF16),
        ],
        20,
    )


def feed_weights_kernel(io, scalars, pre, grad_hidden, up_total, down_total):
    up_t, down = io.inputs[0], io.inputs[1]
    grad_up, grad_down = io.outputs
    units = up_t.shape[0]

    def into(at, j):
        n, b = io.inputs[2 + 2 * at], io.inputs[3 + 2 * at]
        rows = row_block(j, PART)
        pre[at % 2, rows, :] = dot_nt(up_t[rows, :], n[...])
        grad_hidden[at % 2, rows, :] = dot_nt(down[rows, :], b[...])

    def out_of(at, j):
        n, b = io.inputs[2 + 2 * at], io.inputs[3 + 2 * at]
        rows = row_block(j, PART)
        value, derivative = gelu_and_slope(pre[at % 2, rows, :])
        grad_pre = (derivative * grad_hidden[at % 2, rows, :]).astype(BF16)
        down_part = dot_nn(value.astype(BF16), b[...])
        up_part = dot_nn(grad_pre, n[...])
        if at == 0:
            down_total[rows, :] = down_part
            up_total[rows, :] = up_part
        elif at < 3:
            down_total[rows, :] += down_part
            up_total[rows, :] += up_part
        else:
            grad_down[rows, :] = (down_total[rows, :] + down_part).astype(BF16)
            grad_up[:, lane_slice(j * PART, PART)] = (
                (up_total[rows, :] + up_part).T.astype(BF16)
            )

    io.need(0, 1)
    for at in range(5):
        if at < 4:
            io.need(2 + 2 * at, 3 + 2 * at)

        @pl.loop(0, units // PART)
        def _(j):
            if at < 4:
                into(at, j)
            if at > 0:
                out_of(at - 1, j)


def feed_weights(scalars, normeds, branch_grads, weights):
    units, features = weights.shape[0] // 2, weights.shape[1]
    block = normeds[0].shape[0]
    between = [a for pair in zip(normeds, branch_grads, strict=True) for a in pair]
    return local_call(
        feed_weights_kernel,
        "feed_weights",
        scalars,
        (Joined((weights, 0, units)), Joined((weights, units, units)), *between),
        (shape_of(BF16, features, units), shape_of(BF16, units, features)),
        [
            pltpu.VMEM((2, units, block), F32),
            pltpu.VMEM((2, units, block), F32),
            pltpu.VMEM((units, features), F32),
            pltpu.VMEM((units, features), F32),
        ],
        25,
    )


def to_partner(array, axis, size, bit):
    return lax.ppermute(array, axis, [(i, i ^ bit) for i in range(size)])


def exchange_tensor(blocks):
    return (
        blocks[0],
        to_partner(blocks[1], "tensor", 4, 1),
        to_partner(blocks[2], "tensor", 4, 2),
        to_partner(blocks[3], "tensor", 4, 3),
    )


def make_bands(conv_weight):
    apart = (
        lax.broadcasted_iota(jnp.int32, (BAND_IN, BAND_OUT), 0)
        - PAD
        - lax.broadcasted_iota(jnp.int32, (BAND_IN, BAND_OUT), 1)
        + REACH
    )
    band = jnp.zeros((conv_weight.shape[0], BAND_IN, BAND_OUT), F32)
    for tap in range(KERNEL):
        band = jnp.where(apart[None] == tap, conv_weight[:, tap][:, None, None], band)
    return band.astype(BF16)


def after(array, *others):
    return lax.optimization_barrier((array, *others))[0]


def hop(arrays, axis, size, bit):
    columns = arrays[0].shape[-1]
    flat = [a.reshape(-1, columns) for a in arrays]
    got = to_partner(jnp.concatenate(flat, axis=0) if len(flat) > 1 else flat[0], axis, size, bit)
    parts, start = [], 0
    for array, rows in zip(arrays, flat, strict=True):
        parts.append(got[start : start + rows.shape[0]].reshape(array.shape))
        start += rows.shape[0]
    return parts


def is_upper(axis, bit):
    return (lax.axis_index(axis) & bit) != 0


def halve(array, axis, bit):
    rows = array.shape[-2] // 2
    low, high = array[..., :rows, :], array[..., rows:, :]
    upper = is_upper(axis, bit)
    return jnp.where(upper, high, low), jnp.where(upper, low, high)


def add(kept, got):
    return (kept.astype(F32) + got.astype(F32)).astype(kept.dtype)


def rejoin(array, got, axis, bit):
    upper = is_upper(axis, bit)
    return jnp.concatenate(
        [jnp.where(upper, got, array), jnp.where(upper, array, got)], axis=-2
    )


def solution(mesh):
    dp_size = mesh.shape["dp"]
    first, second, *others = [1 << b for b in range(dp_size.bit_length() - 1)]

    def dp_hop(arrays, bit):
        return hop(arrays, "dp", dp_size, bit)

    def shards(
        tokens,
        w_query,
        w_key,
        w_value,
        conv_weight,
        w_out,
        gain_one,
        shift_one,
        w_up,
        w_down,
        gain_two,
        shift_two,
        lengths,
        grad_output,
    ):
        width = w_query.shape[1]
        heads = width // HEAD
        features, units = w_up.shape
        me = lax.axis_index("tensor").astype(jnp.int32)
        scalars = jnp.concatenate([lengths[0], me[None]])
        w_t = jnp.concatenate([w_query.T, w_key.T, w_value.T], axis=0)
        bands = make_bands(conv_weight)
        norms = jnp.stack([gain_one, shift_one, gain_two, shift_two])
        tokens_two = to_partner(tokens, "tensor", 4, 2)
        tokens_one = to_partner(tokens, "tensor", 4, 1)
        weights = jnp.concatenate([w_up.T, w_down], axis=0)
        weights_one = to_partner(weights, "tensor", 4, 1)
        turn = lax.axis_index("dp") & 1
        half_units = units // 2
        weights_half = jnp.concatenate(
            [
                lax.dynamic_slice_in_dim(weights, start + turn * half_units, half_units, axis=0)
                for start in (0, units)
            ],
            axis=0,
        )
        tokens_two = after(tokens_two, bands, w_t, weights_half, weights, norms)
        blocks = (tokens, tokens_one, tokens_two, to_partner(tokens_two, "tensor", 4, 1))
        across = to_partner(after(weights_half, tokens_two), "tensor", 4, 2)

        attended = attend(scalars, blocks, w_t, bands)
        saved = (attended[0], *attended[5:])
        contexts = exchange_tensor(attended[1:5])
        across = after(across, attended[1])
        on = to_partner(across, "dp", dp_size, 1)
        normed_low, unit_one, recip_one = norm_in(scalars, contexts, tokens, w_out, norms)
        normed_two = to_partner(normed_low, "tensor", 4, 2)
        on = after(on, normed_low)

        def core_hop(array):
            return to_partner(array, "tensor", 4, 1)

        across_one, on_one = core_hop(across), core_hop(on)
        ups, downs = [
            (
                Joined((weights, which * units, units)),
                Joined((weights_one, which * units, units)),
                Joined(*[(a, which * half_units, half_units) for a in (across, on)]),
                Joined(*[(a, which * half_units, half_units) for a in (across_one, on_one)]),
            )
            for which in (0, 1)
        ]
        output, slope, summed_grad, branch_grad, norm_grads_two = feed(
            scalars, normed_low, unit_one, grad_output, norms, ups, downs
        )
        branch_two = to_partner(branch_grad, "tensor", 4, 2)
        branch_one = core_hop(branch_grad)
        normed_one = core_hop(normed_low)
        resid_grad, grad_w_out, norm_grads_one, *context_grads = feed_back(
            scalars,
            (slope, summed_grad, branch_grad),
            unit_one,
            recip_one,
            contexts,
            w_out,
            norms,
            ups,
            downs,
        )
        context_grads = exchange_tensor(context_grads)
        norm_rows = jnp.concatenate([norm_grads_one, norm_grads_two], axis=0)
        least = max(dp_size, 32)
        part = -(-(features + norm_rows.shape[0]) // (8 * least)) * least
        spare = jnp.zeros((8 * part - features - norm_rows.shape[0], features), BF16)
        small_kept, small_sent = halve(
            jnp.concatenate([grad_w_out, norm_rows.astype(BF16), spare], axis=0), "tensor", 1
        )
        small_got = core_hop(small_sent)
        normed_two, branch_two = after(normed_two, resid_grad), after(branch_two, resid_grad)
        normeds = (normed_low, normed_one, normed_two, core_hop(normed_two))
        branch_grads = (branch_grad, branch_one, branch_two, core_hop(branch_two))
        small = add(small_kept, after(small_got, branch_two))
        small_kept, small_sent = halve(small, "tensor", 2)
        small_got = to_partner(small_sent, "tensor", 4, 2)
        grad_up, grad_down = feed_weights(scalars, normeds, branch_grads, weights)
        small = add(small_kept, after(small_got, grad_up))

        def with_part(grad, rows):
            pieces = [a.reshape(dp_size, -1, features) for a in (grad, rows)]
            return jnp.concatenate(pieces, axis=1).reshape(-1, features)

        def without_part(array):
            pieces = array.reshape(-1, (units + part) // dp_size, features)
            cut = units // dp_size
            return [
                a.reshape(-1, features) for a in (pieces[:, :cut], pieces[:, cut:])
            ]

        up, down = with_part(grad_up, small[:part]), with_part(grad_down, small[part:])
        up_kept, up_sent = halve(up, "dp", first)
        down_kept, down_sent = halve(down, "dp", second)
        (up_got,), (down_got,) = dp_hop([up_sent], first), dp_hop([down_sent], second)
        context_grads = [after(context_grads[0], up_sent, down_sent), *context_grads[1:]]

        passed = attend_back(scalars, saved, context_grads, bands)
        up_kept, up_sent = halve(add(up_kept, after(up_got, passed[0])), "dp", second)
        down_kept, down_sent = halve(add(down_kept, after(down_got, passed[0])), "dp", first)
        (up_got,), (down_got,) = dp_hop([up_sent], second), dp_hop([down_sent], first)
        passed = [*passed[:6], after(passed[6], up_sent, down_sent)]
        shares = attend_steps(scalars, saved, passed)
        both = jnp.stack(
            [add(up_kept, after(up_got, shares)), add(down_kept, after(down_got, shares))]
        )
        kept, sent = halve(both, "dp", others[0])
        (got,) = dp_hop([sent], others[0])
        shares = after(shares, sent)
        low, high, *token_grads = attend_grads(
            scalars, passed, shares, blocks, w_t, max(dp_size, 16)
        )
        both = add(kept, after(got, low))
        for bit in others[1:]:
            kept, sent = halve(both, "dp", bit)
            (got,) = dp_hop([sent], bit)
            both = add(kept, got)
        low, high = after(low, both), after(high, both)
        both_got = dp_hop([both], others[-1])[0]
        low_kept, low_sent = halve(low, "dp", first)
        high_kept, high_sent = halve(high, "dp", second)
        (low_got,), (high_got,) = dp_hop([low_sent], first), dp_hop([high_sent], second)
        token_got = (core_hop(token_grads[3]), core_hop(token_grads[1]))
        away = add(token_grads[2], after(token_got[0], low_sent, high_sent))
        arrived = to_partner(away, "tensor", 4, 2)
        low_kept, low_sent = halve(add(low_kept, after(low_got, away)), "dp", second)
        high_kept, high_sent = halve(add(high_kept, after(high_got, away)), "dp", first)
        (low_got,), (high_got,) = dp_hop([low_sent], second), dp_hop([high_sent], first)
        both = rejoin(both, after(both_got, low_sent, high_sent), "dp", others[-1])
        for bit in reversed(others[:-1]):
            (got,) = dp_hop([both], bit)
            both = rejoin(both, got, "dp", bit)
        up, down = both[0], both[1]
        (up_got,), (down_got,) = dp_hop([up], second), dp_hop([down], first)
        wide = jnp.stack([add(low_kept, low_got), add(high_kept, high_got)])
        kept_wide = wide
        (wide_got,) = dp_hop([wide], others[0])
        up = rejoin(up, after(up_got, arrived), "dp", second)
        down = rejoin(down, down_got, "dp", first)
        (up, small_up), (down, small_down) = without_part(up), without_part(down)
        (up_got,), (down_got,) = dp_hop([up], first), dp_hop([down], second)
        wide = add(kept_wide, after(wide_got, up, down))
        for bit in others[1:]:
            (wide_got,) = dp_hop([wide], bit)
            wide = add(wide, wide_got)
        low, high = wide[0], wide[1]
        low_got, down_part_got = dp_hop([low, small_down], second)
        high_got, up_part_got = dp_hop([high, small_up], first)
        here = token_grads[0].astype(F32) + token_got[1].astype(F32)
        grad_tokens = resid_grad + here + after(arrived, low, high).astype(F32)
        small = jnp.concatenate(
            [
                rejoin(small_up, up_part_got, "dp", first),
                rejoin(small_down, down_part_got, "dp", second),
            ],
            axis=0,
        )
        small_got = to_partner(small, "tensor", 4, 2)
        low, high = rejoin(low, low_got, "dp", second), rejoin(high, high_got, "dp", first)
        (low_got,), (high_got,) = dp_hop([low], first), dp_hop([high], second)
        grad_up = rejoin(up, after(up_got, low), "dp", first).astype(F32)
        grad_down = rejoin(down, after(down_got, high), "dp", second).astype(F32)
        small = rejoin(small, after(small_got, low, high), "tensor", 2)
        small_got = core_hop(small)
        low_got, high_got = after(low_got, grad_up), after(high_got, grad_down)
        small = rejoin(small, small_got, "tensor", 1)
        grad_w_out = small[:features].astype(F32)
        norm_rows = small[features : features + 16].astype(F32)
        qkv_wide = jnp.concatenate(
            [
                rejoin(low, low_got, "dp", first),
                rejoin(high, high_got, "dp", second),
            ],
            axis=0,
        ).astype(F32)
        return (
            output,
            grad_tokens,
            qkv_wide[:width].T,
            qkv_wide[width : 2 * width].T,
            qkv_wide[2 * width : 3 * width].T,
            qkv_wide[3 * width : 3 * width + heads, :KERNEL],
            grad_w_out,
            norm_rows[0],
            norm_rows[1],
            grad_up,
            grad_down,
            norm_rows[8],
            norm_rows[9],
        )

    rows = P(("dp", "tensor"), None)
    columns = P(None, "tensor")
    in_specs = (
        rows,
        columns,
        columns,
        columns,
        P("tensor", None),
        P(),
        P(),
        P(),
        columns,
        P("tensor", None),
        P(),
        P(),
        P("dp", None),
        rows,
    )
    out_specs = (
        rows,
        rows,
        columns,
        columns,
        columns,
        P("tensor", None),
        P(),
        P(),
        P(),
        columns,
        P("tensor", None),
        P(),
        P(),
    )
    return jax.shard_map(shards, mesh=mesh, in_specs=in_specs, out_specs=out_specs, check_vma=False)
```

```python
import jax
import jax.numpy as jnp
from jax import lax
from jax.experimental import pallas as pl
from jax.experimental.pallas import tpu as pltpu
from jax.sharding import PartitionSpec as P

HEAD = 64
LANDMARKS = 64
NS_ITERS = 6
KERNEL = 33
SEQS = 3
MARKS = 192
REACH = KERNEL // 2
PAD = 128
BAND_IN = 512
BAND_OUT = 256
TILE = 640
AHEAD = 20
VMEM_LIMIT = 60 * 1024 * 1024
F32 = jnp.float32
BF16 = jnp.bfloat16


def dot_nn(a, b):
    return lax.dot_general(a, b, (((1,), (0,)), ((), ())), preferred_element_type=F32)


def dot_nt(a, b):
    return lax.dot_general(a, b, (((1,), (1,)), ((), ())), preferred_element_type=F32)


def dot_tn(a, b):
    return lax.dot_general(a, b, (((0,), (0,)), ((), ())), preferred_element_type=F32)


def split_low(a):
    high = a.astype(BF16)
    return (high, (a - high.astype(F32)).astype(BF16))


def dot_three(a, b, dot=dot_nn):
    a_high, a_low = a
    b_high, b_low = b
    return dot(a_high, b_high) + (dot(a_high, b_low) + dot(a_low, b_high))


def block_mask(dtype):
    rows = lax.broadcasted_iota(jnp.int32, (MARKS, MARKS), 0) // LANDMARKS
    columns = lax.broadcasted_iota(jnp.int32, (MARKS, MARKS), 1) // LANDMARKS
    return jnp.where(rows == columns, 1.0, 0.0).astype(dtype)


def spread(packed, mask):
    return jnp.concatenate([packed] * SEQS, axis=0) * mask


def spread_split(packed, mask):
    high, low = split_low(packed)
    return (spread(high, mask), spread(low, mask))


def fold(blocks):
    return (
        blocks[:LANDMARKS] + blocks[LANDMARKS : 2 * LANDMARKS] + blocks[2 * LANDMARKS :]
    )


def packed_identity():
    rows = lax.broadcasted_iota(jnp.int32, (LANDMARKS, MARKS), 0)
    columns = lax.broadcasted_iota(jnp.int32, (LANDMARKS, MARKS), 1) % LANDMARKS
    return jnp.where(rows == columns, 1.0, 0.0).astype(F32)


def sequence_of(places, first_end, second_end):
    return (places >= first_end).astype(jnp.int32) + (places >= second_end).astype(jnp.int32)


def lane_slice(start, width):
    return pl.ds(pl.multiple_of(start, 128), width)


def row_block(i, size):
    return pl.ds(pl.multiple_of(i * size, size), size)


class Layout:
    def __init__(self, scalars, group_size):
        self.first_end = scalars[0]
        self.second_end = scalars[0] + scalars[1]
        self.group_size = group_size
        self.tiles = group_size // TILE
        last = [
            (self.first_end - 1) // TILE,
            (self.second_end - 1) // TILE,
            self.tiles - 1,
        ]
        self.first_tile = [0, self.first_end // TILE, self.second_end // TILE]
        counts = [b - a + 1 for a, b in zip(self.first_tile, last, strict=True)]
        self.before = [0, counts[0], counts[0] + counts[1]]
        self.pairs = counts[0] + counts[1] + counts[2]

    def pick(self, sequence, values):
        return jnp.where(
            sequence == 0, values[0], jnp.where(sequence == 1, values[1], values[2])
        )

    def pair(self, p):
        sequence = (p >= self.before[1]).astype(jnp.int32) + (p >= self.before[2]).astype(
            jnp.int32
        )
        tile = p - self.pick(sequence, self.before) + self.pick(sequence, self.first_tile)
        start = self.pick(sequence, [0, self.first_end, self.second_end])
        end = self.pick(sequence, [self.first_end, self.second_end, self.group_size])
        return sequence, tile, start, end

    def own(self, tile, start, end):
        places = tile * TILE + lax.broadcasted_iota(jnp.int32, (LANDMARKS, TILE), 1)
        return (places >= start) & (places < end)

    def pool(self, tile, start, end):
        places = tile * TILE + lax.broadcasted_iota(jnp.int32, (1, TILE), 1)
        length = jnp.full((1, TILE), end - start, jnp.int32).astype(F32)
        numerator = ((places - start + 1) * LANDMARKS - 1).astype(F32) + length + 0.5
        segment = jnp.floor(numerator / length).astype(jnp.int32) - 1
        segment = jnp.where((places >= start) & (places < end), segment, -1)
        marks = lax.broadcasted_iota(jnp.int32, (LANDMARKS, TILE), 0)
        return jnp.where(marks == segment, 1.0, 0.0).astype(BF16)

    def counts(self):
        marks = lax.broadcasted_iota(jnp.int32, (MARKS, 1), 0)
        sequence = marks // LANDMARKS
        k = marks % LANDMARKS
        length = self.pick(
            sequence,
            [
                self.first_end,
                self.second_end - self.first_end,
                self.group_size - self.second_end,
            ],
        )
        upper = lax.shift_right_logical((k + 1) * length, 6)
        return (upper - lax.shift_right_logical(k * length, 6)).astype(F32)

    def same(self, start):
        into = start - PAD + lax.broadcasted_iota(jnp.int32, (BAND_IN, 1), 0)
        out = start + lax.broadcasted_iota(jnp.int32, (1, BAND_OUT), 1)
        return sequence_of(into, self.first_end, self.second_end) == sequence_of(
            out, self.first_end, self.second_end
        )


class Joined:
    def __init__(self, *pieces):
        self.pieces = pieces
        first = pieces[0][0]
        self.shape = (sum(rows for _, _, rows in pieces), first.shape[1])
        self.dtype = first.dtype

    def copies(self, sources, local):
        pairs, at = [], 0
        for source, (_, start, rows) in zip(sources, self.pieces, strict=True):
            pairs.append((source.at[start : start + rows, :], local.at[at : at + rows, :]))
            at += rows
        return pairs


class Io:
    def __init__(self, copies, inputs, outputs, targets, in_sems, out_sems):
        self.inputs, self.outputs = inputs, outputs
        self.arriving = [
            [
                pltpu.make_async_copy(source, local, in_sems.at[at])
                for source, local, at in group
            ]
            for group in copies
        ]
        self.leaving = [
            pltpu.make_async_copy(local, target, out_sems.at[i])
            for i, (local, target) in enumerate(zip(outputs, targets, strict=True))
        ]
        self.sent = set()
        self.started = 0
        self.waited = set()
        self.start_to(AHEAD)

    def start_to(self, end):
        for group in self.arriving[self.started : end]:
            for copy in group:
                copy.start()
        self.started = max(self.started, min(end, len(self.arriving)))

    def need(self, *which):
        self.start_to(max(which) + 1 + AHEAD)
        for i in which:
            if i not in self.waited:
                self.waited.add(i)
                for copy in self.arriving[i]:
                    copy.wait()
        return [self.inputs[i] for i in which]

    def send(self, *which):
        for i in which:
            self.sent.add(i)
            self.leaving[i].start()

    def close(self):
        self.need(*range(len(self.arriving)))
        self.send(*[i for i in range(len(self.leaving)) if i not in self.sent])
        for copy in self.leaving:
            copy.wait()


def local_call(kernel, name, scalars, operands, out_shape, scratch, gigaflops):
    anywhere = pl.BlockSpec(memory_space=pl.ANY)
    flat = [
        a
        for o in operands
        for a in ([piece[0] for piece in o.pieces] if isinstance(o, Joined) else [o])
    ]
    moved = sum(x.size * x.dtype.itemsize for x in (*flat, *out_shape))
    n_in, n_out, n_flat = len(operands), len(out_shape), len(flat)

    def body(scalar_ref, *refs):
        sources, refs = refs[:n_flat], refs[n_flat:]
        targets, refs = refs[:n_out], refs[n_out:]
        inputs, refs = refs[:n_in], refs[n_in:]
        outputs, refs = refs[:n_out], refs[n_out:]
        copies, at = [], 0
        for o, local in zip(operands, inputs, strict=True):
            count = len(o.pieces) if isinstance(o, Joined) else 1
            mine = sources[at : at + count]
            pairs = o.copies(mine, local) if isinstance(o, Joined) else [(mine[0], local)]
            copies.append([(a, b, at + i) for i, (a, b) in enumerate(pairs)])
            at += count
        io = Io(copies, inputs, outputs, targets, refs[0], refs[1])
        kernel(io, scalar_ref, *refs[2:])
        io.close()

    return pl.pallas_call(
        body,
        name=name,
        out_shape=out_shape,
        in_specs=[pl.BlockSpec(memory_space=pltpu.SMEM)] + [anywhere] * n_flat,
        out_specs=[anywhere] * n_out,
        scratch_shapes=[
            *[pltpu.VMEM(x.shape, x.dtype) for x in operands],
            *[pltpu.VMEM(x.shape, x.dtype) for x in out_shape],
            pltpu.SemaphoreType.DMA((n_flat,)),
            pltpu.SemaphoreType.DMA((n_out,)),
            *scratch,
        ],
        compiler_params=pltpu.CompilerParams(vmem_limit_bytes=VMEM_LIMIT),
        cost_estimate=pl.CostEstimate(
            flops=gigaflops * 1_000_000_000, bytes_accessed=moved, transcendentals=0
        ),
    )(scalars, *flat)


def shape_of(dtype, *shape):
    return jax.ShapeDtypeStruct(shape, dtype)


def wide(narrow):
    return jnp.concatenate([narrow] * (TILE // 128), axis=1)


def attend_kernel(
    io,
    scalars,
    context,
    scores,
    pooled,
    tops,
    totals,
    q_lands,
    k_lands,
    mvts,
):
    w_t, bands = io.inputs[0], io.inputs[5]
    qkv_t, c0, c1, c2, c3, land_out, mark_values_out, summary_out = io.outputs[:8]
    steps_out, among_out, inverse_out, lse_to, lse_from = io.outputs[8:]
    width = w_t.shape[0] // 3
    heads = width // HEAD
    block = io.inputs[1].shape[0]
    group_size = 4 * block
    layout = Layout(scalars, group_size)
    me = scalars[3]
    qk_scale = HEAD ** (-0.25)

    qkv_t[:, :PAD] = jnp.zeros((3 * width, PAD), BF16)
    qkv_t[:, PAD + group_size :] = jnp.zeros((3 * width, PAD), BF16)
    io.need(0)
    for at in range(4):
        x = io.need(1 + at)[0]
        lanes = lane_slice(PAD + (me ^ at) * block, block)
        qkv_t[: 2 * width, lanes] = (dot_nt(w_t[: 2 * width, :], x[...]) * qk_scale).astype(BF16)
        qkv_t[2 * width :, lanes] = dot_nt(w_t[2 * width :, :], x[...]).astype(BF16)
    io.send(0)

    pooled[...] = jnp.zeros_like(pooled)

    @pl.loop(0, layout.pairs)
    def _(p):
        sequence, tile, start, end = layout.pair(p)
        rows = row_block(sequence, LANDMARKS)
        pool = layout.pool(tile, start, end)
        pooled[rows, :] += dot_nt(pool, qkv_t[: 2 * width, lane_slice(PAD + tile * TILE, TILE)])

    pooled[...] = pooled[...] / layout.counts()
    land_t = pooled[...].T.astype(BF16)
    land_out[...] = land_t
    for h in range(heads):
        q_lands[h] = pooled[:, h * HEAD : (h + 1) * HEAD].astype(BF16)
        k_lands[h] = pooled[:, width + h * HEAD : width + (h + 1) * HEAD].astype(BF16)
    io.send(5)

    tops[...] = jnp.full(tops.shape, -1e30, F32)
    totals[...] = jnp.zeros_like(totals)
    summary_out[...] = jnp.zeros_like(summary_out)

    each = range(heads)

    def part_rows(part, h):
        return slice(part * width + h * HEAD, part * width + (h + 1) * HEAD)

    @pl.loop(0, layout.pairs)
    def _(p):
        sequence, tile, start, end = layout.pair(p)
        rows = row_block(sequence, LANDMARKS)
        own = layout.own(tile, start, end)
        padded = lane_slice(PAD + tile * TILE, TILE)
        raw = [dot_nn(q_lands[h, rows, :], qkv_t[part_rows(1, h), padded]) for h in each]
        masked = [jnp.where(own, raw[h], -1e30) for h in each]
        top = [tops[h, rows, :] for h in each]
        for lane in range(0, TILE, 128):
            top = [jnp.maximum(top[h], masked[h][:, lane : lane + 128]) for h in each]
        for h in each:
            scores[h, :, lane_slice(p * TILE, TILE)] = masked[h]
            tops[h, rows, :] = top[h]

    for h in range(heads):
        tops[h] = jnp.broadcast_to(jnp.max(tops[h], axis=1, keepdims=True), (MARKS, 128))

    @pl.loop(0, layout.pairs)
    def _(p):
        sequence, _, _, _ = layout.pair(p)
        rows = row_block(sequence, LANDMARKS)
        at = lane_slice(p * TILE, TILE)
        raised = [jnp.exp(scores[h, :, at] - wide(tops[h, rows, :])) for h in each]
        total = [totals[h, rows, :] for h in each]
        for lane in range(0, TILE, 128):
            total = [total[h] + raised[h][:, lane : lane + 128] for h in each]
        for h in each:
            scores[h, :, at] = raised[h]
            totals[h, rows, :] = total[h]

    for h in range(heads):
        total = jnp.broadcast_to(jnp.sum(totals[h], axis=1, keepdims=True), (MARKS, 128))
        lse_from[h] = tops[h] + jnp.log(total)
        totals[h] = 1.0 / total

    @pl.loop(0, layout.pairs)
    def _(p):
        sequence, tile, _, _ = layout.pair(p)
        rows = row_block(sequence, LANDMARKS)
        at = lane_slice(p * TILE, TILE)
        padded = lane_slice(PAD + tile * TILE, TILE)
        low = [(scores[h, :, at] * wide(totals[h, rows, :])).astype(BF16) for h in each]
        part = [dot_nt(low[h], qkv_t[part_rows(2, h), padded]) for h in each]
        part = [summary_out[h, rows, :] + part[h] for h in each]
        for h in each:
            summary_out[h, rows, :] = part[h]

    io.send(7, 12)
    mask_f = block_mask(F32)
    mask_b = block_mask(BF16)
    eye = packed_identity()
    amongs = []
    approxes = []
    for h in range(heads):
        raw = dot_nt(q_lands[h], k_lands[h])
        masked = jnp.where(mask_f > 0.0, raw, -1e30)
        row_top = jnp.max(masked, axis=1, keepdims=True)
        raised = jnp.exp(masked - row_top)
        among = raised / jnp.sum(raised, axis=1, keepdims=True)
        column_top = jnp.max(jnp.sum(among, axis=0, keepdims=True), axis=1, keepdims=True)
        packed = fold(among)
        among_out[h] = packed
        amongs.append(split_low(packed))
        approxes.append(fold(among.T) / column_top)

    io.need(5)

    def convolve(start):
        same = jnp.where(layout.same(start), 1.0, 0.0).astype(BF16)
        smooth = [
            dot_nn(qkv_t[part_rows(2, h), start : start + BAND_IN], bands[h] * same)
            for h in each
        ]
        for h in each:
            context[part_rows(0, h), start : start + BAND_OUT] = smooth[h]

    starts = list(range(0, group_size, BAND_OUT))
    for step in range(NS_ITERS):
        product = [
            dot_three(amongs[h], spread_split(approxes[h], mask_b)) for h in range(heads)
        ]
        split = [split_low(product[h]) for h in range(heads)]
        bracket = [7.0 * eye - product[h] for h in range(heads)]
        second = [
            15.0 * eye - dot_three(split[h], spread_split(bracket[h], mask_b))
            for h in range(heads)
        ]
        third = [
            13.0 * eye - dot_three(split[h], spread_split(second[h], mask_b))
            for h in range(heads)
        ]
        for start in starts[step::NS_ITERS]:
            convolve(start)
        for h in range(heads):
            steps_out[h, 4 * step] = approxes[h]
            steps_out[h, 4 * step + 1] = product[h]
            steps_out[h, 4 * step + 2] = second[h]
            steps_out[h, 4 * step + 3] = third[h]
        approxes = [
            0.25 * dot_three(split_low(approxes[h]), spread_split(third[h], mask_b))
            for h in range(heads)
        ]

    for h in range(heads):
        inverse_out[h] = approxes[h]
        mark_values = dot_three(
            spread_split(approxes[h], mask_b), split_low(summary_out[h])
        )
        mark_values_out[h] = mark_values.astype(BF16)
        for s in range(SEQS):
            part = mark_values[s * LANDMARKS : (s + 1) * LANDMARKS, :]
            mvts[SEQS * h + s] = part.T.astype(BF16)
    io.send(6, 8, 9, 10)
    @pl.loop(0, layout.pairs)
    def _(p):
        sequence, tile, start, end = layout.pair(p)
        rows = row_block(sequence, LANDMARKS)
        own = layout.own(tile, start, end)
        at = lane_slice(tile * TILE, TILE)
        padded = lane_slice(PAD + tile * TILE, TILE)
        raw = [dot_nn(k_lands[h, rows, :], qkv_t[part_rows(0, h), padded]) for h in each]
        top = [jnp.max(raw[h], axis=0, keepdims=True) for h in each]
        raised = [jnp.exp(raw[h] - top[h]) for h in each]
        total = [jnp.sum(raised[h], axis=0, keepdims=True) for h in each]
        low = [
            jnp.where(own, raised[h] * (1.0 / total[h]), 0.0).astype(BF16) for h in each
        ]
        blended = [dot_nn(mvts[SEQS * h + sequence], low[h]) for h in each]
        blended = [context[part_rows(0, h), at] + blended[h] for h in each]
        lse = [
            jnp.where(own[:1], top[h] + jnp.log(total[h]), lse_to[h : h + 1, at]) for h in each
        ]
        for h in each:
            lse_to[h : h + 1, at] = lse[h]
            context[part_rows(0, h), at] = blended[h]

    for at, out in enumerate((c0, c1, c2, c3)):
        out[...] = context[:, lane_slice((me ^ at) * block, block)].astype(BF16)


def attend(scalars, blocks, w_t, bands):
    block = blocks[0].shape[0]
    group_size = 4 * block
    width = w_t.shape[0] // 3
    heads = width // HEAD
    most_pairs = group_size // TILE + SEQS - 1
    return local_call(
        attend_kernel,
        "attend",
        scalars,
        (w_t, *blocks, bands),
        (
            shape_of(BF16, 3 * width, group_size + 2 * PAD),
            *[shape_of(BF16, width, block) for _ in range(4)],
            shape_of(BF16, 2 * width, MARKS),
            shape_of(BF16, heads, MARKS, HEAD),
            shape_of(F32, heads, MARKS, HEAD),
            shape_of(F32, heads, 4 * NS_ITERS, LANDMARKS, MARKS),
            shape_of(F32, heads, LANDMARKS, MARKS),
            shape_of(F32, heads, LANDMARKS, MARKS),
            shape_of(F32, heads, group_size),
            shape_of(F32, heads, MARKS, 128),
        ),
        [
            pltpu.VMEM((width, group_size), F32),
            pltpu.VMEM((heads, LANDMARKS, most_pairs * TILE), F32),
            pltpu.VMEM((MARKS, 2 * width), F32),
            pltpu.VMEM((heads, MARKS, 128), F32),
            pltpu.VMEM((heads, MARKS, 128), F32),
            pltpu.VMEM((heads, MARKS, HEAD), BF16),
            pltpu.VMEM((heads, MARKS, HEAD), BF16),
            pltpu.VMEM((SEQS * heads, HEAD, LANDMARKS), BF16),
        ],
        30,
    )


def attend_back_kernel(
    io,
    scalars,
    context_grad,
    partial_value,
    correlation,
    q_lands,
    k_lands,
    q_lands_t,
    k_lands_t,
    grad_summaries,
    grad_summaries_t,
    offsets,
):
    g_refs = io.inputs[:4]
    qkv_t, land_t, mark_values_in, summary_in = io.inputs[4:8]
    inverse_in, lse_to, lse_from = io.inputs[8:11]
    bands = io.inputs[11]
    grad_value, taps_out, partial_query, partial_key = io.outputs[:4]
    grad_q_land, grad_k_land, grad_mark = io.outputs[4:]
    width, block = g_refs[0].shape
    heads = width // HEAD
    group_size = 4 * block
    layout = Layout(scalars, group_size)
    me = scalars[3]
    each = range(heads)

    def part_rows(part, h):
        return slice(part * width + h * HEAD, part * width + (h + 1) * HEAD)

    io.need(*range(11))
    context_grad[:, :PAD] = jnp.zeros((width, PAD), BF16)
    context_grad[:, PAD + group_size :] = jnp.zeros((width, PAD), BF16)
    for at, g in enumerate(g_refs):
        context_grad[:, lane_slice(PAD + (me ^ at) * block, block)] = g[...]

    for h in range(heads):
        q_t = land_t[h * HEAD : (h + 1) * HEAD, :].astype(F32)
        k_t = land_t[width + h * HEAD : width + (h + 1) * HEAD, :].astype(F32)
        q_lands[h] = q_t.T.astype(BF16)
        k_lands[h] = k_t.T.astype(BF16)
        for s in range(SEQS):
            columns = slice(s * LANDMARKS, (s + 1) * LANDMARKS)
            q_lands_t[SEQS * h + s] = q_t[:, columns].astype(BF16)
            k_lands_t[SEQS * h + s] = k_t[:, columns].astype(BF16)

    for ref in (grad_k_land, grad_mark, grad_q_land, partial_query, partial_key, partial_value):
        ref[...] = jnp.zeros_like(ref)

    @pl.loop(0, layout.pairs)
    def _(p):
        sequence, tile, start, end = layout.pair(p)
        rows = row_block(sequence, LANDMARKS)
        own = layout.own(tile, start, end)
        at = lane_slice(tile * TILE, TILE)
        padded = lane_slice(PAD + tile * TILE, TILE)
        query = [qkv_t[part_rows(0, h), padded] for h in each]
        out_grad = [context_grad[part_rows(0, h), padded] for h in each]
        raw = [dot_nn(k_lands[h, rows, :], query[h]) for h in each]
        grad_to = [dot_nn(mark_values_in[h, rows, :], out_grad[h]) for h in each]
        probs = [
            jnp.exp(jnp.where(own, raw[h] - lse_to[h : h + 1, at], -1e30)) for h in each
        ]
        inner = [jnp.sum(grad_to[h] * probs[h], axis=0, keepdims=True) for h in each]
        grad_scores = [(probs[h] * (grad_to[h] - inner[h])).astype(BF16) for h in each]
        mark_part = [
            grad_mark[h, rows, :] + dot_nt(probs[h].astype(BF16), out_grad[h]) for h in each
        ]
        land_part = [
            grad_k_land[h, rows, :] + dot_nt(grad_scores[h], query[h]) for h in each
        ]
        query_part = [
            partial_query[part_rows(0, h), at]
            + dot_nn(k_lands_t[SEQS * h + sequence], grad_scores[h])
            for h in each
        ]
        for h in each:
            grad_mark[h, rows, :] = mark_part[h]
            grad_k_land[h, rows, :] = land_part[h]
            partial_query[part_rows(0, h), at] = query_part[h]

    io.send(2, 5, 6)
    mask_f = block_mask(F32)
    for h in range(heads):
        mark_split = split_low(grad_mark[h])
        summary = summary_in[h]
        inverse_blocks = spread(inverse_in[h], mask_f).T
        grad_summary = dot_three(split_low(inverse_blocks), mark_split)
        grad_low = grad_summary.astype(BF16)
        grad_summaries[h] = grad_low
        exact = grad_low.astype(F32)
        for s in range(SEQS):
            part = exact[s * LANDMARKS : (s + 1) * LANDMARKS, :]
            grad_summaries_t[SEQS * h + s] = part.T.astype(BF16)
        inner = jnp.sum(exact * summary, axis=1, keepdims=True)
        offsets[h] = jnp.broadcast_to(inner, (MARKS, 128))

    @pl.loop(0, layout.pairs)
    def _(p):
        sequence, tile, start, end = layout.pair(p)
        rows = row_block(sequence, LANDMARKS)
        own = layout.own(tile, start, end)
        at = lane_slice(tile * TILE, TILE)
        padded = lane_slice(PAD + tile * TILE, TILE)
        key = [qkv_t[part_rows(1, h), padded] for h in each]
        value = [qkv_t[part_rows(2, h), padded] for h in each]
        raw = [dot_nn(q_lands[h, rows, :], key[h]) for h in each]
        grad_from = [dot_nn(grad_summaries[h, rows, :], value[h]) for h in each]
        probs = [
            jnp.exp(jnp.where(own, raw[h] - wide(lse_from[h, rows, :]), -1e30)) for h in each
        ]
        grad_scores = [
            (probs[h] * (grad_from[h] - wide(offsets[h, rows, :]))).astype(BF16) for h in each
        ]
        value_part = [
            partial_value[part_rows(0, h), padded]
            + dot_nn(grad_summaries_t[SEQS * h + sequence], probs[h].astype(BF16))
            for h in each
        ]
        land_part = [grad_q_land[h, rows, :] + dot_nt(grad_scores[h], key[h]) for h in each]
        key_part = [
            partial_key[part_rows(0, h), at]
            + dot_nn(q_lands_t[SEQS * h + sequence], grad_scores[h])
            for h in each
        ]
        for h in each:
            partial_value[part_rows(0, h), padded] = value_part[h]
            grad_q_land[h, rows, :] = land_part[h]
            partial_key[part_rows(0, h), at] = key_part[h]

    io.send(3, 4)

    correlation[...] = jnp.zeros_like(correlation)
    io.need(11)

    @pl.loop(0, group_size // BAND_OUT)
    def _(i):
        start = i * BAND_OUT
        padded = lane_slice(PAD + start, BAND_OUT)
        around = lane_slice(start, BAND_IN)
        same = jnp.where(layout.same(start), 1.0, 0.0)
        same_b = same.astype(BF16)
        out_grad = [context_grad[part_rows(0, h), padded] for h in each]
        value_part = [
            partial_value[part_rows(0, h), around] + dot_nt(out_grad[h], bands[h] * same_b)
            for h in each
        ]
        across = [
            dot_tn(qkv_t[part_rows(2, h), around], out_grad[h]) * same for h in each
        ]
        parts = [
            (
                a[:128, :128] + a[128:256, 128:],
                a[128:256, :128] + a[256:384, 128:],
                a[256:384, :128] + a[384:, 128:],
            )
            for a in across
        ]
        for h in each:
            partial_value[part_rows(0, h), around] = value_part[h]
            for at in range(3):
                correlation[h, at] += parts[h][at]

    grad_value[...] = partial_value[:, PAD : PAD + group_size].astype(BF16)
    io.send(0)
    apart = lax.broadcasted_iota(jnp.int32, (128, 128), 0) - lax.broadcasted_iota(
        jnp.int32, (128, 128), 1
    )
    lanes = lax.broadcasted_iota(jnp.int32, (8, 128), 1)
    rows = lax.broadcasted_iota(jnp.int32, (8, 128), 0)
    taps = jnp.zeros((8, 128), F32)
    for h in range(heads):
        for tap in range(KERNEL):
            away = tap - REACH
            picked = jnp.where(apart == away, correlation[h, 1], 0.0)
            if away < 0:
                picked += jnp.where(apart == away + 128, correlation[h, 0], 0.0)
            if away > 0:
                picked += jnp.where(apart == away - 128, correlation[h, 2], 0.0)
            total = jnp.sum(
                jnp.sum(picked, axis=0, keepdims=True), axis=1, keepdims=True
            )
            taps = taps + jnp.where((lanes == tap) & (rows == h), total, 0.0)
    taps_out[...] = taps


def attend_steps_kernel(group_size, io, scalars):
    grad_mark_in, summary_in, among_in, steps_in = io.inputs[:4]
    land_t, grad_q_land, grad_k_land = io.inputs[4:]
    shares = io.outputs[0]
    heads = summary_in.shape[0]
    width = heads * HEAD
    layout = Layout(scalars, group_size)
    each = range(heads)
    mask_f = block_mask(F32)
    mask_b = block_mask(BF16)
    io.need(0, 1, 2)
    carried = [
        fold(dot_three(split_low(summary_in[h]), split_low(grad_mark_in[h]), dot_nt) * mask_f)
        for h in each
    ]
    io.need(*range(3, 7))
    eye = packed_identity()

    def spread_both(pair):
        return tuple(spread(a, mask_b) for a in pair)

    among_wide = [spread_split(among_in[h], mask_b) for h in each]
    among_grads = [jnp.zeros((LANDMARKS, MARKS), F32) for _ in each]
    for step in reversed(range(NS_ITERS)):
        approx = [split_low(steps_in[h, 4 * step]) for h in each]
        product = [steps_in[h, 4 * step + 1] for h in each]
        product_wide = [spread_split(product[h], mask_b) for h in each]
        grad = [split_low(carried[h]) for h in each]
        third = [
            split_low(0.25 * dot_three(grad[h], spread_both(approx[h]))) for h in each
        ]
        through = [
            dot_three(split_low(steps_in[h, 4 * step + 3]), spread_both(grad[h])) for h in each
        ]
        second = [split_low(-dot_three(third[h], product_wide[h])) for h in each]
        from_third = [
            dot_three(split_low(steps_in[h, 4 * step + 2]), spread_both(third[h]))
            for h in each
        ]
        first = [dot_three(second[h], product_wide[h]) for h in each]
        from_second = [
            dot_three(split_low(7.0 * eye - product[h]), spread_both(second[h])) for h in each
        ]
        grad_product = [
            split_low(first[h] - from_third[h] - from_second[h]) for h in each
        ]
        carried = [
            0.25 * through[h] + dot_three(grad_product[h], among_wide[h]) for h in each
        ]
        among_grads = [
            among_grads[h] + dot_three(approx[h], spread_both(grad_product[h])) for h in each
        ]

    for h in each:
        among = spread(among_in[h], mask_f)
        column_sums = jnp.sum(among, axis=0, keepdims=True)
        column_top = jnp.max(column_sums, axis=1, keepdims=True)
        start_grad = carried[h]
        start_blocks = spread(steps_in[h, 0], mask_f).T
        top_grad = -jnp.sum(
            jnp.sum(start_grad * fold(start_blocks), axis=1, keepdims=True),
            axis=0,
            keepdims=True,
        ) / column_top
        at_top = jnp.where(column_sums == column_top, 1.0, 0.0)
        shared = top_grad * at_top / jnp.sum(at_top, axis=1, keepdims=True)
        among_grad = spread(among_grads[h], mask_f).T + (
            spread(start_grad, mask_f) / column_top + shared * mask_f
        )
        inner = jnp.sum(among_grad * among, axis=1, keepdims=True)
        grad_scores = among * (among_grad - inner)
        high, low = split_low(grad_scores)
        back_high, back_low = split_low(grad_scores.T)
        q_land = land_t[h * HEAD : (h + 1) * HEAD, :].astype(F32).T.astype(BF16)
        k_land = land_t[width + h * HEAD : width + (h + 1) * HEAD, :].astype(F32).T.astype(BF16)
        q_total = grad_q_land[h] + (dot_nn(high, k_land) + dot_nn(low, k_land))
        k_total = grad_k_land[h] + (dot_nn(back_high, q_land) + dot_nn(back_low, q_land))
        counts = layout.counts()
        for which, total in enumerate((q_total, k_total)):
            share = total.astype(BF16).astype(F32) / counts
            for s in range(SEQS):
                part = share[s * LANDMARKS : (s + 1) * LANDMARKS, :].T
                shares[which, SEQS * h + s] = part.astype(BF16)


def attend_grads_kernel(io, scalars, grad_qkv, grad_w_t):
    grad_value, taps, partial_query, partial_key, shares, w_t = io.inputs[:6]
    x_refs = io.inputs[6:]
    low_out, high_out, d_refs = io.outputs[0], io.outputs[1], io.outputs[2:]
    width, group_size = partial_query.shape
    heads = width // HEAD
    block, features = x_refs[0].shape
    half = low_out.shape[0]
    me = scalars[3]
    qk_scale = HEAD ** (-0.25)
    layout = Layout(scalars, group_size)
    each = range(heads)

    def part_rows(part, h):
        return slice(part * width + h * HEAD, part * width + (h + 1) * HEAD)

    io.need(0, 2, 3, 4)

    @pl.loop(0, layout.pairs)
    def _(p):
        sequence, tile, start, end = layout.pair(p)
        at = lane_slice(tile * TILE, TILE)
        pool = layout.pool(tile, start, end)
        query = [
            partial_query[part_rows(0, h), at] + dot_nn(shares[0, SEQS * h + sequence], pool)
            for h in each
        ]
        key = [
            partial_key[part_rows(0, h), at] + dot_nn(shares[1, SEQS * h + sequence], pool)
            for h in each
        ]
        for h in each:
            partial_query[part_rows(0, h), at] = query[h]
            partial_key[part_rows(0, h), at] = key[h]

    grad_qkv[:width, :] = partial_query[...].astype(BF16)
    grad_qkv[width : 2 * width, :] = partial_key[...].astype(BF16)
    grad_qkv[2 * width :, :] = grad_value[...]

    io.need(1, 5)
    for at in (3, 1, 2, 0):
        x = io.need(6 + at)[0]
        lanes = lane_slice((me ^ at) * block, block)
        part = dot_nn(grad_qkv[:, lanes], x[...])
        if at == 3:
            grad_w_t[...] = part
        else:
            grad_w_t[...] += part

    def put(start, value):
        end = start + value.shape[0]
        if start < half:
            low_out[start : min(end, half), :] = value[: min(end, half) - start]
        if end > half:
            high_out[max(start, half) - half : end - half, :] = value[max(start, half) - start :]

    put(0, (grad_w_t[: 2 * width] * qk_scale).astype(BF16))
    put(2 * width, grad_w_t[2 * width :].astype(BF16))
    put(3 * width, jnp.zeros((2 * half - 3 * width, features), BF16))
    start = 3 * width - half
    high_out[start : start + 16, :128] = jnp.concatenate(
        [taps[...], jnp.zeros((8, 128), F32)], axis=0
    ).astype(BF16)
    io.send(0, 1)

    for at in (3, 1, 2, 0):
        d = d_refs[at]
        lanes = lane_slice((me ^ at) * block, block)
        scaled = dot_tn(grad_qkv[: 2 * width, lanes], w_t[: 2 * width, :])
        plain = dot_tn(grad_qkv[2 * width :, lanes], w_t[2 * width :, :])
        d[...] = (scaled * qk_scale + plain).astype(BF16)
        io.send(2 + at)


def attend_back(scalars, saved, grads, bands):
    qkv_t, land_t, mark_values, summary, steps, among, inverse, lse_to, lse_from = saved
    width, block = grads[0].shape
    group_size = 4 * block
    heads = width // HEAD
    lands = pltpu.VMEM((heads, MARKS, HEAD), BF16)
    lands_t = pltpu.VMEM((SEQS * heads, HEAD, LANDMARKS), BF16)
    return local_call(
        attend_back_kernel,
        "attend_back",
        scalars,
        (*grads, qkv_t, land_t, mark_values, summary, inverse, lse_to, lse_from, bands),
        (
            shape_of(BF16, width, group_size),
            shape_of(F32, 8, 128),
            shape_of(F32, width, group_size),
            shape_of(F32, width, group_size),
            *[shape_of(F32, heads, MARKS, HEAD) for _ in range(3)],
        ),
        [
            pltpu.VMEM((width, group_size + 2 * PAD), BF16),
            pltpu.VMEM((width, group_size + 2 * PAD), F32),
            pltpu.VMEM((heads, 3, 128, 128), F32),
            lands,
            lands,
            lands_t,
            lands_t,
            lands,
            lands_t,
            pltpu.VMEM((heads, MARKS, 128), F32),
        ],
        8,
    )


def attend_steps(scalars, saved, passed):
    qkv_t, land_t, mark_values, summary, steps, among, inverse, lse_to, lse_from = saved
    grad_q_land, grad_k_land, grad_mark = passed[4:]
    heads = summary.shape[0]

    def kernel(*refs):
        attend_steps_kernel(qkv_t.shape[1] - 2 * PAD, *refs)

    return local_call(
        kernel,
        "attend_steps",
        scalars,
        (grad_mark, summary, among, steps, land_t, grad_q_land, grad_k_land),
        (shape_of(BF16, 2, SEQS * heads, HEAD, LANDMARKS),),
        [],
        5,
    )[0]


def attend_grads(scalars, passed, shares, blocks, w_t, multiple):
    grad_value, taps, partial_query, partial_key = passed[:4]
    block, features = blocks[0].shape
    width, group_size = partial_query.shape
    heads = width // HEAD
    half = -(-(w_t.shape[0] + 16) // (2 * multiple)) * multiple
    return local_call(
        attend_grads_kernel,
        "attend_grads",
        scalars,
        (
            grad_value,
            taps,
            partial_query,
            partial_key,
            shares,
            w_t,
            *blocks,
        ),
        (
            shape_of(BF16, half, features),
            shape_of(BF16, half, features),
            *[shape_of(BF16, block, features) for _ in range(4)],
        ),
        [
            pltpu.VMEM((3 * width, group_size), BF16),
            pltpu.VMEM(w_t.shape, F32),
        ],
        8,
    )


def gelu_and_slope(values):
    z = jnp.abs(values) * 0.7071067811865476
    t = pl.reciprocal(1.0 + 0.3275911 * z)
    poly = t * 1.061405429 - 1.453152027
    for coefficient in (1.421413741, -0.284496736, 0.254829592):
        poly = poly * t + coefficient
    bell = jnp.exp(-z * z)
    half_tail = (0.5 * t) * poly * bell
    below = jnp.where(values >= 0.0, 1.0 - half_tail, half_tail)
    return values * below, below + values * (bell * 0.3989422804014327)


def unit_norm(values):
    row_mean = jnp.mean(values, axis=-1, keepdims=True)
    centered = values - row_mean
    spread_out = jnp.mean(centered * centered, axis=-1, keepdims=True)
    recip = lax.rsqrt(spread_out + 1e-05)
    return (centered * recip, recip)


def unit_back(grad, unit, recip):
    mean_grad = jnp.mean(grad, axis=-1, keepdims=True)
    mean_cross = jnp.mean(grad * unit, axis=-1, keepdims=True)
    return recip * (grad - mean_grad - unit * mean_cross)


ROWS = 320
PART = 768


def norm_in_kernel(io, scalars):
    contexts, (tokens, w_out, norms) = io.inputs[:4], io.inputs[4:]
    normed_out, unit_one, recip_one = io.outputs
    me = scalars[3]
    width, block = contexts[0].shape
    io.need(*range(7))

    resid = tokens[...].astype(F32)
    for at, c in enumerate(contexts):
        resid += dot_tn(c[...], w_out[row_block(me ^ at, width), :])
    unit, recip = unit_norm(resid)
    unit_one[...] = unit
    recip_one[...] = jnp.broadcast_to(recip, (block, 128))
    normed_out[...] = (unit * norms[0:1, :] + norms[1:2, :]).astype(BF16)


def feed_first_kernel(io, scalars, hidden):
    count = len(io.outputs) - 1
    normed_low, ups, downs = io.inputs[0], io.inputs[1 : 1 + count], io.inputs[1 + count :]
    slopes, partial = io.outputs[:count], io.outputs[count]
    block = normed_low.shape[0]
    units = ups[0].shape[0]
    io.need(0)
    for s, up in enumerate(ups):
        io.need(1 + s)
        value, derivative = gelu_and_slope(dot_nt(normed_low[...], up[...]))
        hidden[:, s * units : (s + 1) * units] = value.astype(BF16)
        slopes[s][...] = derivative.astype(BF16)
        io.send(s)
    io.need(*range(1 + count, 1 + 2 * count))

    @pl.loop(0, block // ROWS)
    def _(i):
        rows = row_block(i, ROWS)
        total = dot_nn(hidden[rows, :units], downs[0][...])
        for s in range(1, count):
            total += dot_nn(hidden[rows, s * units : (s + 1) * units], downs[s][...])
        partial[rows, :] = total


def feed_kernel(io, scalars, hidden):
    normed_low, up, down, partial, unit_one, norms, grad_output = io.inputs
    output, slope, summed_grad, branch_grad, norm_grads = io.outputs
    block = normed_low.shape[0]
    norm_grads[...] = jnp.zeros_like(norm_grads)
    io.need(0, 1)
    value, derivative = gelu_and_slope(dot_nt(normed_low[...], up[...]))
    hidden[...] = value.astype(BF16)
    slope[...] = derivative.astype(BF16)
    io.send(1)
    io.need(2, 3, 4, 5, 6)

    @pl.loop(0, block // ROWS)
    def _(i):
        rows = row_block(i, ROWS)
        total = unit_one[rows, :] * norms[0:1, :] + norms[1:2, :]
        total += partial[rows, :] + dot_nn(hidden[rows, :], down[...])
        unit, recip = unit_norm(total)
        output[rows, :] = unit * norms[2:3, :] + norms[3:4, :]
        top = grad_output[rows, :].astype(F32)
        norm_grads[0:1, :] += jnp.sum(top * unit, axis=0, keepdims=True)
        norm_grads[1:2, :] += jnp.sum(top, axis=0, keepdims=True)
        grad = unit_back(top * norms[2:3, :], unit, recip)
        summed_grad[rows, :] = grad
        branch_grad[rows, :] = grad.astype(BF16)


def feed_back_kernel(io, scalars, grad_pre, attended_grad):
    branch_grad, norms = io.inputs[:2]
    downs, slopes = io.inputs[2:10:2], io.inputs[3:10:2]
    ups = io.inputs[10:14]
    summed_grad, unit_one, recip_one, w_out = io.inputs[14:18]
    contexts = io.inputs[18:22]
    resid_grad, grad_w_out, norm_grads = io.outputs[:3]
    targets = io.outputs[3:]
    me = scalars[3]
    width, block = contexts[0].shape
    units = ups[0].shape[0]
    norm_grads[...] = jnp.zeros_like(norm_grads)
    io.need(0, 1)

    for s, (down, slope) in enumerate(zip(downs, slopes, strict=True)):
        io.need(2 + 2 * s, 3 + 2 * s)
        grad = dot_nt(branch_grad[...], down[...])
        grad_pre[:, s * units : (s + 1) * units] = (slope[...].astype(F32) * grad).astype(BF16)

    io.need(*range(10, 22))

    @pl.loop(0, block // ROWS)
    def _(i):
        rows = row_block(i, ROWS)
        total = summed_grad[rows, :]
        for s, up in enumerate(ups):
            total += dot_nn(grad_pre[rows, s * units : (s + 1) * units], up[...])
        unit = unit_one[rows, :]
        norm_grads[0:1, :] += jnp.sum(total * unit, axis=0, keepdims=True)
        norm_grads[1:2, :] += jnp.sum(total, axis=0, keepdims=True)
        grad = unit_back(total * norms[0:1, :], unit, recip_one[rows, :1])
        resid_grad[rows, :] = grad
        attended_grad[rows, :] = grad.astype(BF16)

    for at in (3, 2, 1, 0):
        rows = row_block(me ^ at, width)
        targets[at][...] = dot_nt(w_out[rows, :], attended_grad[...]).astype(BF16)
        io.send(3 + at)
    for at, c in enumerate(contexts):
        rows = row_block(me ^ at, width)
        grad_w_out[rows, :] = dot_nn(c[...], attended_grad[...]).astype(BF16)


def norm_in(scalars, contexts, tokens, w_out, norms):
    block, features = tokens.shape
    return local_call(
        norm_in_kernel,
        "norm_in",
        scalars,
        (*contexts, tokens, w_out, norms),
        (
            shape_of(BF16, block, features),
            shape_of(F32, block, features),
            shape_of(F32, block, 128),
        ),
        [],
        6,
    )


def feed_first(scalars, normed_low, ups, downs):
    block, features = normed_low.shape
    units = ups[0].shape[0]
    return local_call(
        feed_first_kernel,
        "feed_first",
        scalars,
        (normed_low, *ups, *downs),
        (
            *[shape_of(BF16, block, units) for _ in ups],
            shape_of(F32, block, features),
        ),
        [pltpu.VMEM((block, len(ups) * units), BF16)],
        15,
    )


def feed(scalars, normed_low, up, down, partial, unit_one, norms, grad_output):
    block, features = normed_low.shape
    units = up.shape[0]
    return local_call(
        feed_kernel,
        "feed",
        scalars,
        (normed_low, up, down, partial, unit_one, norms, grad_output),
        (
            shape_of(F32, block, features),
            shape_of(BF16, block, units),
            shape_of(F32, block, features),
            shape_of(BF16, block, features),
            shape_of(F32, 8, features),
        ),
        [pltpu.VMEM((block, units), BF16)],
        8,
    )


def feed_back(scalars, fed, unit_one, recip_one, contexts, w_out, norms, ups, downs):
    slopes, summed_grad, branch_grad = fed
    width, block = contexts[0].shape
    features = w_out.shape[0]
    units = ups[0].shape[0]
    return local_call(
        feed_back_kernel,
        "feed_back",
        scalars,
        (
            branch_grad,
            norms,
            *[a for pair in zip(downs, slopes, strict=True) for a in pair],
            *ups,
            summed_grad,
            unit_one,
            recip_one,
            w_out,
            *contexts,
        ),
        (
            shape_of(F32, block, features),
            shape_of(BF16, features, features),
            shape_of(F32, 8, features),
            *[shape_of(BF16, width, block) for _ in range(4)],
        ),
        [
            pltpu.VMEM((block, 4 * units), BF16),
            pltpu.VMEM((block, features), BF16),
        ],
        20,
    )


def feed_weights_kernel(io, scalars, pre, grad_hidden, up_total, down_total):
    up_t, down = io.inputs[0], io.inputs[1]
    grad_up, grad_down = io.outputs
    units = up_t.shape[0]

    def into(at, j):
        n, b = io.inputs[2 + 2 * at], io.inputs[3 + 2 * at]
        rows = row_block(j, PART)
        pre[at % 2, rows, :] = dot_nt(up_t[rows, :], n[...])
        grad_hidden[at % 2, rows, :] = dot_nt(down[rows, :], b[...])

    def out_of(at, j):
        n, b = io.inputs[2 + 2 * at], io.inputs[3 + 2 * at]
        rows = row_block(j, PART)
        value, derivative = gelu_and_slope(pre[at % 2, rows, :])
        grad_pre = (derivative * grad_hidden[at % 2, rows, :]).astype(BF16)
        down_part = dot_nn(value.astype(BF16), b[...])
        up_part = dot_nn(grad_pre, n[...])
        if at == 0:
            down_total[rows, :] = down_part
            up_total[rows, :] = up_part
        elif at < 3:
            down_total[rows, :] += down_part
            up_total[rows, :] += up_part
        else:
            grad_down[rows, :] = (down_total[rows, :] + down_part).astype(BF16)
            grad_up[:, lane_slice(j * PART, PART)] = (
                (up_total[rows, :] + up_part).T.astype(BF16)
            )

    io.need(0, 1)
    for at in range(5):
        if at < 4:
            io.need(2 + 2 * at, 3 + 2 * at)

        @pl.loop(0, units // PART)
        def _(j):
            if at < 4:
                into(at, j)
            if at > 0:
                out_of(at - 1, j)


def feed_weights(scalars, normeds, branch_grads, weights):
    units, features = weights.shape[0] // 2, weights.shape[1]
    block = normeds[0].shape[0]
    between = [a for pair in zip(normeds, branch_grads, strict=True) for a in pair]
    return local_call(
        feed_weights_kernel,
        "feed_weights",
        scalars,
        (Joined((weights, 0, units)), Joined((weights, units, units)), *between),
        (shape_of(BF16, features, units), shape_of(BF16, units, features)),
        [
            pltpu.VMEM((2, units, block), F32),
            pltpu.VMEM((2, units, block), F32),
            pltpu.VMEM((units, features), F32),
            pltpu.VMEM((units, features), F32),
        ],
        25,
    )


def to_partner(array, axis, size, bit):
    return lax.ppermute(array, axis, [(i, i ^ bit) for i in range(size)])


def exchange_tensor(blocks):
    return (
        blocks[0],
        to_partner(blocks[1], "tensor", 4, 1),
        to_partner(blocks[2], "tensor", 4, 2),
        to_partner(blocks[3], "tensor", 4, 3),
    )


def make_bands(conv_weight):
    apart = (
        lax.broadcasted_iota(jnp.int32, (BAND_IN, BAND_OUT), 0)
        - PAD
        - lax.broadcasted_iota(jnp.int32, (BAND_IN, BAND_OUT), 1)
        + REACH
    )
    band = jnp.zeros((conv_weight.shape[0], BAND_IN, BAND_OUT), F32)
    for tap in range(KERNEL):
        band = jnp.where(apart[None] == tap, conv_weight[:, tap][:, None, None], band)
    return band.astype(BF16)


def after(array, *others):
    return lax.optimization_barrier((array, *others))[0]


def hop(arrays, axis, size, bit):
    columns = arrays[0].shape[-1]
    flat = [a.reshape(-1, columns) for a in arrays]
    got = to_partner(jnp.concatenate(flat, axis=0) if len(flat) > 1 else flat[0], axis, size, bit)
    parts, start = [], 0
    for array, rows in zip(arrays, flat, strict=True):
        parts.append(got[start : start + rows.shape[0]].reshape(array.shape))
        start += rows.shape[0]
    return parts


def is_upper(axis, bit):
    return (lax.axis_index(axis) & bit) != 0


def halve(array, axis, bit):
    rows = array.shape[-2] // 2
    low, high = array[..., :rows, :], array[..., rows:, :]
    upper = is_upper(axis, bit)
    return jnp.where(upper, high, low), jnp.where(upper, low, high)


def add(kept, got):
    return (kept.astype(F32) + got.astype(F32)).astype(kept.dtype)


def rejoin(array, got, axis, bit):
    upper = is_upper(axis, bit)
    return jnp.concatenate(
        [jnp.where(upper, got, array), jnp.where(upper, array, got)], axis=-2
    )


def solution(mesh):
    dp_size = mesh.shape["dp"]
    first, second, *others = [1 << b for b in range(dp_size.bit_length() - 1)]

    def dp_hop(arrays, bit):
        return hop(arrays, "dp", dp_size, bit)

    def shards(
        tokens,
        w_query,
        w_key,
        w_value,
        conv_weight,
        w_out,
        gain_one,
        shift_one,
        w_up,
        w_down,
        gain_two,
        shift_two,
        lengths,
        grad_output,
    ):
        width = w_query.shape[1]
        heads = width // HEAD
        features, units = w_up.shape
        me = lax.axis_index("tensor").astype(jnp.int32)
        scalars = jnp.concatenate([lengths[0], me[None]])
        w_t = jnp.concatenate([w_query.T, w_key.T, w_value.T], axis=0)
        bands = make_bands(conv_weight)
        norms = jnp.stack([gain_one, shift_one, gain_two, shift_two])
        tokens_two = to_partner(tokens, "tensor", 4, 2)
        tokens_one = to_partner(tokens, "tensor", 4, 1)
        weights = jnp.concatenate([w_up.T, w_down], axis=0)
        weights_one = to_partner(weights, "tensor", 4, 1)
        turn = lax.axis_index("dp") & 1
        half_units = units // 2
        weights_half = jnp.concatenate(
            [
                lax.dynamic_slice_in_dim(weights, start + turn * half_units, half_units, axis=0)
                for start in (0, units)
            ],
            axis=0,
        )
        tokens_two = after(tokens_two, bands, w_t, weights_half, weights, norms)
        blocks = (tokens, tokens_one, tokens_two, to_partner(tokens_two, "tensor", 4, 1))
        across = to_partner(after(weights_half, tokens_two), "tensor", 4, 2)

        attended = attend(scalars, blocks, w_t, bands)
        saved = (attended[0], *attended[5:])
        contexts = exchange_tensor(attended[1:5])
        across = after(across, attended[1])
        on = to_partner(across, "dp", dp_size, 1)
        normed_low, unit_one, recip_one = norm_in(scalars, contexts, tokens, w_out, norms)
        row_half = tokens.shape[0] // 2
        normed_a = to_partner(normed_low[:row_half], "tensor", 4, 2)
        normed_b = to_partner(normed_low[row_half:], "tensor", 4, 2)

        def core_hop(array):
            return to_partner(array, "tensor", 4, 1)

        across_one = core_hop(across)

        def shards_of(which, pieces):
            return [
                Joined(*[(a, which * rows, rows) for a in group]) for group, rows in pieces
            ]

        here = [((weights,), units), ((weights_one,), units), ((across, across_one), half_units)]
        ups, downs = shards_of(0, here), shards_of(1, here)
        *slopes, partial = feed_first(scalars, normed_low, ups, downs)
        on = after(on, partial, normed_a)
        late = [((on, core_hop(on)), half_units)]
        ups, downs = ups + shards_of(0, late), downs + shards_of(1, late)
        output, slope, summed_grad, branch_grad, norm_grads_two = feed(
            scalars, normed_low, ups[3], downs[3], partial, unit_one, norms, grad_output
        )
        normed_b = after(normed_b, branch_grad)
        branch_two = to_partner(branch_grad, "tensor", 4, 2)
        branch_one = core_hop(branch_grad)
        normed_one = core_hop(normed_low)
        resid_grad, grad_w_out, norm_grads_one, *context_grads = feed_back(
            scalars,
            ([*slopes, slope], summed_grad, branch_grad),
            after(unit_one, normed_b),
            recip_one,
            contexts,
            w_out,
            norms,
            ups,
            downs,
        )
        context_grads = exchange_tensor(context_grads)
        norm_rows = jnp.concatenate([norm_grads_one, norm_grads_two], axis=0)
        least = max(dp_size, 32)
        part = -(-(features + norm_rows.shape[0]) // (8 * least)) * least
        spare = jnp.zeros((8 * part - features - norm_rows.shape[0], features), BF16)
        small_kept, small_sent = halve(
            jnp.concatenate([grad_w_out, norm_rows.astype(BF16), spare], axis=0), "tensor", 1
        )
        small_got = core_hop(small_sent)
        branch_two = after(branch_two, resid_grad)
        normed_twos = [(a, 0, row_half) for a in (normed_a, normed_b)]
        normed_threes = [(core_hop(a), 0, row_half) for a in (normed_a, normed_b)]
        normeds = (normed_low, normed_one, Joined(*normed_twos), Joined(*normed_threes))
        branch_grads = (branch_grad, branch_one, branch_two, core_hop(branch_two))
        small = add(small_kept, after(small_got, branch_two))
        small_kept, small_sent = halve(small, "tensor", 2)
        small_got = to_partner(small_sent, "tensor", 4, 2)
        grad_up, grad_down = feed_weights(scalars, normeds, branch_grads, weights)
        small = add(small_kept, after(small_got, grad_up))

        def with_part(grad, rows):
            pieces = [a.reshape(dp_size, -1, features) for a in (grad, rows)]
            return jnp.concatenate(pieces, axis=1).reshape(-1, features)

        def without_part(array):
            pieces = array.reshape(-1, (units + part) // dp_size, features)
            cut = units // dp_size
            return [
                a.reshape(-1, features) for a in (pieces[:, :cut], pieces[:, cut:])
            ]

        up, down = with_part(grad_up, small[:part]), with_part(grad_down, small[part:])
        up_kept, up_sent = halve(up, "dp", first)
        down_kept, down_sent = halve(down, "dp", second)
        (up_got,), (down_got,) = dp_hop([up_sent], first), dp_hop([down_sent], second)
        context_grads = [after(context_grads[0], up_sent, down_sent), *context_grads[1:]]

        passed = attend_back(scalars, saved, context_grads, bands)
        up_kept, up_sent = halve(add(up_kept, after(up_got, passed[0])), "dp", second)
        down_kept, down_sent = halve(add(down_kept, after(down_got, passed[0])), "dp", first)
        (up_got,), (down_got,) = dp_hop([up_sent], second), dp_hop([down_sent], first)
        passed = [*passed[:6], after(passed[6], up_sent, down_sent)]
        shares = attend_steps(scalars, saved, passed)
        both = jnp.stack(
            [add(up_kept, after(up_got, shares)), add(down_kept, after(down_got, shares))]
        )
        kept, sent = halve(both, "dp", others[0])
        (got,) = dp_hop([sent], others[0])
        shares = after(shares, sent)
        low, high, *token_grads = attend_grads(
            scalars, passed, shares, blocks, w_t, max(dp_size, 16)
        )
        both = add(kept, after(got, low))
        for bit in others[1:]:
            kept, sent = halve(both, "dp", bit)
            (got,) = dp_hop([sent], bit)
            both = add(kept, got)
        low, high = after(low, both), after(high, both)
        both_got = dp_hop([both], others[-1])[0]
        low_kept, low_sent = halve(low, "dp", first)
        high_kept, high_sent = halve(high, "dp", second)
        (low_got,), (high_got,) = dp_hop([low_sent], first), dp_hop([high_sent], second)
        token_got = (core_hop(token_grads[3]), core_hop(token_grads[1]))
        away = add(token_grads[2], after(token_got[0], low_sent, high_sent))
        arrived = to_partner(away, "tensor", 4, 2)
        low_kept, low_sent = halve(add(low_kept, after(low_got, away)), "dp", second)
        high_kept, high_sent = halve(add(high_kept, after(high_got, away)), "dp", first)
        (low_got,), (high_got,) = dp_hop([low_sent], second), dp_hop([high_sent], first)
        both = rejoin(both, after(both_got, low_sent, high_sent), "dp", others[-1])
        for bit in reversed(others[:-1]):
            (got,) = dp_hop([both], bit)
            both = rejoin(both, got, "dp", bit)
        up, down = both[0], both[1]
        (up_got,), (down_got,) = dp_hop([up], second), dp_hop([down], first)
        wide = jnp.stack([add(low_kept, low_got), add(high_kept, high_got)])
        kept_wide = wide
        (wide_got,) = dp_hop([wide], others[0])
        up = rejoin(up, after(up_got, arrived), "dp", second)
        down = rejoin(down, down_got, "dp", first)
        (up, small_up), (down, small_down) = without_part(up), without_part(down)
        (up_got,), (down_got,) = dp_hop([up], first), dp_hop([down], second)
        wide = add(kept_wide, after(wide_got, up, down))
        for bit in others[1:]:
            (wide_got,) = dp_hop([wide], bit)
            wide = add(wide, wide_got)
        low, high = wide[0], wide[1]
        low_got, down_part_got = dp_hop([low, small_down], second)
        high_got, up_part_got = dp_hop([high, small_up], first)
        here = token_grads[0].astype(F32) + token_got[1].astype(F32)
        grad_tokens = resid_grad + here + after(arrived, low, high).astype(F32)
        small = jnp.concatenate(
            [
                rejoin(small_up, up_part_got, "dp", first),
                rejoin(small_down, down_part_got, "dp", second),
            ],
            axis=0,
        )
        small_got = to_partner(small, "tensor", 4, 2)
        low, high = rejoin(low, low_got, "dp", second), rejoin(high, high_got, "dp", first)
        (low_got,), (high_got,) = dp_hop([low], first), dp_hop([high], second)
        grad_up = rejoin(up, after(up_got, low), "dp", first).astype(F32)
        grad_down = rejoin(down, after(down_got, high), "dp", second).astype(F32)
        small = rejoin(small, after(small_got, low, high), "tensor", 2)
        small_got = core_hop(small)
        low_got, high_got = after(low_got, grad_up), after(high_got, grad_down)
        small = rejoin(small, small_got, "tensor", 1)
        grad_w_out = small[:features].astype(F32)
        norm_rows = small[features : features + 16].astype(F32)
        qkv_wide = jnp.concatenate(
            [
                rejoin(low, low_got, "dp", first),
                rejoin(high, high_got, "dp", second),
            ],
            axis=0,
        ).astype(F32)
        return (
            output,
            grad_tokens,
            qkv_wide[:width].T,
            qkv_wide[width : 2 * width].T,
            qkv_wide[2 * width : 3 * width].T,
            qkv_wide[3 * width : 3 * width + heads, :KERNEL],
            grad_w_out,
            norm_rows[0],
            norm_rows[1],
            grad_up,
            grad_down,
            norm_rows[8],
            norm_rows[9],
        )

    rows = P(("dp", "tensor"), None)
    columns = P(None, "tensor")
    in_specs = (
        rows,
        columns,
        columns,
        columns,
        P("tensor", None),
        P(),
        P(),
        P(),
        columns,
        P("tensor", None),
        P(),
        P(),
        P("dp", None),
        rows,
    )
    out_specs = (
        rows,
        rows,
        columns,
        columns,
        columns,
        P("tensor", None),
        P(),
        P(),
        P(),
        columns,
        P("tensor", None),
        P(),
        P(),
    )
    return jax.shard_map(shards, mesh=mesh, in_specs=in_specs, out_specs=out_specs, check_vma=False)
```
